32 devices in a mesh: dp: 16 (over z, y, x), mp: 2 (over core).
Axes of the slice: x: 2, y: 2, z: 4, core: 2. Of those that a mesh axis runs over, the one named last changes fastest.
Arguments:
- text: bfloat16 [768, 40, 768], P('dp'), may hold values from -6 to 6
- cotangent: bfloat16 [768, 40, 768], P('dp'), may hold values from -6 to 6
- lengths: int32 [768], P('dp'), may hold values from 1 to 40
- box_corners: int32 [768, 4], P('dp'), may hold values from 0 to 12, as said below
- box_counts: int32 [16, 16], P('dp'), may hold values from 1 to 6, 48 in all within a row
- region_box: int32 [768], P('dp'), may hold values from 0 to 767, as said below
- patches: bfloat16 [256, 145, 1024], P('dp'), may hold values from -6 to 6
- proj_weight: bfloat16 [1024, 768], replicated, may hold values from -0.1875 to 0.1875
- proj_bias: float32 [768], replicated, may hold values from -1 to 1
- attention_in: bfloat16 [2, 3, 768, 768], P(None, None, None, 'mp'), may hold values from -0.21875 to 0.21875
- attention_bias: float32 [2, 2, 768], P(None, None, 'mp'), may hold values from -1 to 1
- attention_out: bfloat16 [2, 768, 768], P(None, 'mp'), may hold values from -0.875 to 0.875
- output_bias: float32 [3, 768], replicated, may hold values from -1 to 1
- norm_gain: float32 [3, 768], replicated, may hold values from 0.5 to 1.5
- norm_bias: float32 [3, 768], replicated, may hold values from -1 to 1
- up_weight: bfloat16 [768, 3072], P(None, 'mp'), may hold values from -0.21875 to 0.21875
- up_bias: float32 [3072], P('mp'), may hold values from -1 to 1
- down_weight: bfloat16 [3072, 768], P('mp'), may hold values from -0.15625 to 0.15625
Outputs:
- merged_text: bfloat16 [768, 40, 768], P('dp', 'mp')
- text_grad: bfloat16 [768, 40, 768], P('dp', 'mp')
- patch_grad: bfloat16 [256, 145, 1024], P(('dp', 'mp'))
- proj_weight_grad: float32 [1024, 768], P('dp', 'mp')
- proj_bias_grad: float32 [768], P('mp')
- attention_in_grad: float32 [2, 3, 768, 768], P(None, None, 'dp', 'mp')
- attention_bias_grad: float32 [2, 2, 768], P(None, None, 'mp')
- attention_out_grad: float32 [2, 768, 768], P(None, 'mp', 'dp')
- output_bias_grad: float32 [3, 768], replicated
- norm_gain_grad: float32 [3, 768], replicated
- norm_bias_grad: float32 [3, 768], replicated
- up_weight_grad: float32 [768, 3072], P('dp', 'mp')
- up_bias_grad: float32 [3072], P('mp')
- down_weight_grad: float32 [3072, 768], P('mp', 'dp')
The draws below stay inside these ranges and needn't reach their ends.
Inputs may be any that keep to these rules, and one draw needn't show every extreme that they name: `box_counts`: each index of dp holds 16 images whose counts sum to 48. `box_corners`: first column < end column and first row < end row; ends are exclusive. `region_box`: a permutation of the 768 box numbers; box b belongs to an image of index b // 48 of dp; the 48 rows of one index of dp name boxes of exactly 16 indices, 3 boxes of each.
All inputs are finite; a program needn't handle non-finite values.
Results may differ from the reference program's by a relative error of at most 0.025.
Values may be sent and summed in bfloat16 or wider, within the bound.
No kernel may reach another device: no remote copies, remote signals or barrier semaphores. Data moves between devices by JAX's collectives and lax.ppermute only.
A program may use at most 320 MiB of HBM per device.

```python
import math
import jax
import jax.numpy as jnp
import numpy as np
from jax import lax

D = 768
HEADS = 12
HEAD_DIM = 64
FF = 3072
V = 1024
GRID = 12
L = 40
BOXMAX = 6
R_DEV = 48
IMG_DEV = 16
PAIR = 3
P_SIZE = 145
ROWS = 768
IMAGES = 256
N_DP = 16


def draw_lengths(key, part):
    key = jax.random.fold_in(key, 11)
    values = jax.random.randint(key, (ROWS,), 1, L + 1)
    return values.at[0].set(L).astype(jnp.int32)


def draw_box_corners(key, part):
    key = jax.random.fold_in(key, 12)
    keys = jax.random.split(key, 4)
    col_start = jax.random.randint(keys[0], (ROWS,), 0, GRID)
    col_width = jax.random.randint(keys[1], (ROWS,), 1, GRID + 1)
    row_start = jax.random.randint(keys[2], (ROWS,), 0, GRID)
    row_width = jax.random.randint(keys[3], (ROWS,), 1, GRID + 1)
    col_end = jnp.minimum(col_start + col_width, GRID)
    row_end = jnp.minimum(row_start + row_width, GRID)
    corners = jnp.stack([col_start, col_end, row_start, row_end], axis=1)
    corners = corners.at[0].set(jnp.array([0, GRID, 0, GRID]))
    return corners.astype(jnp.int32)


def draw_region_box(key, part):
    key = jax.random.fold_in(key, 13)
    keys = jax.random.split(key, 3)
    groups = R_DEV // PAIR
    scores = jax.random.permutation(keys[0], N_DP).astype(jnp.int32) + 3
    scores = scores.at[N_DP - 1].set(0).at[1].set(1).at[N_DP // 2].set(2)
    offsets = jnp.argsort(scores, stable=True).astype(jnp.int32)[:groups]
    source_order = jax.vmap(lambda k: jax.random.permutation(k, R_DEV))(jax.random.split(keys[1], N_DP))
    target_order = jax.vmap(lambda k: jax.random.permutation(k, R_DEV))(jax.random.split(keys[2], N_DP))
    group = source_order // PAIR
    within = source_order % PAIR
    target = (jnp.arange(N_DP)[:, None] + offsets[group]) % N_DP
    local_slot = group * PAIR + within
    slot = target_order[target, local_slot]
    return (target * R_DEV + slot).reshape(ROWS).astype(jnp.int32)


def block_levels(own_key, dims, cuts, smallest, top_value):
    def one(position, blocks):
        steps = jax.random.uniform(jax.random.fold_in(jax.random.fold_in(own_key, 6), position), (blocks,), jnp.float32, smallest / len(cuts), top_value / len(cuts))
        return jnp.repeat(jnp.exp(steps), dims[position] // blocks).reshape((-1,) + (1,) * (len(dims) - position - 1))

    level = one(*cuts[0])
    for cut in cuts[1:]:
        level = level * one(*cut)
    return level


def split_up(amount, total, reach, slope):
    weights = [(1 << 20) // math.isqrt(rank ** slope) + 1 for rank in range(2, amount + 1)]
    spare, holding = total - reach - (amount - 1), [1] * (amount - 1)
    while spare > 0:
        free = [i for i in range(amount - 1) if holding[i] < reach]
        whole, budget = sum([weights[i] for i in free]), spare
        for i in free:
            extra = min(reach - holding[i], max(1, budget * weights[i] // whole), spare)
            holding[i] = holding[i] + extra
            spare = spare - extra
    return np.array([reach] + holding)


def ragged_sizes(key, number_of, total, most, skew):
    if number_of == 2:
        one = jax.random.randint(key, (), max(1, total - most), min(most, total - 1) + 1)
        return jnp.stack([one, total - one])
    sizes = jnp.asarray(split_up(number_of, total, most, skew), jnp.int32)
    pairs = (number_of - 1) // 2
    donor, taker = sizes[1:1 + 2 * pairs:2], sizes[2:2 + 2 * pairs:2]
    slack = jnp.minimum(donor - 1, most - taker)
    shifted = jax.random.randint(jax.random.fold_in(key, 1), (pairs,), 0, 1 << 20) % (slack + 1)
    sizes = sizes.at[1:1 + 2 * pairs:2].set(donor - shifted).at[2:2 + 2 * pairs:2].set(taker + shifted)
    return sizes[jax.random.permutation(jax.random.fold_in(key, 2), number_of)]


def scatter_about(stream_key, extent, deviation, bound, cuts=(), kind=jnp.bfloat16):
    values = deviation * jax.random.normal(stream_key, extent, jnp.float32)
    if cuts:
        values = values * block_levels(stream_key, extent, cuts, -0.22, 0.18)
    return jnp.clip(values, -bound, bound).astype(kind)


def setup_inputs(seed: int = 0) -> dict:
    arg_keys = jax.random.split(jax.random.key(seed), 19)
    text = scatter_about(arg_keys[0], (ROWS, L, D), 1.0, 6.0, ((0, 16),))
    cotangent = scatter_about(arg_keys[1], (ROWS, L, D), 1.0, 6.0, ((0, 16),))
    lengths = draw_lengths(jax.random.fold_in(arg_keys[18], 71), 0)
    box_corners = draw_box_corners(jax.random.fold_in(arg_keys[18], 71), 0)
    box_counts = jax.vmap(lambda own: ragged_sizes(own, IMG_DEV, R_DEV, BOXMAX, 2))(jax.random.split(arg_keys[4], N_DP)).reshape((N_DP, IMG_DEV)).astype(jnp.int32)
    region_box = draw_region_box(jax.random.fold_in(arg_keys[18], 71), 0)
    patches = scatter_about(arg_keys[6], (IMAGES, P_SIZE, V), 1.0, 6.0, ((0, 16),))
    proj_weight = scatter_about(arg_keys[7], (V, D), V ** -0.5, 0.1875)
    proj_bias = scatter_about(arg_keys[8], (D,), 0.2, 1.0, (), jnp.float32)
    attention_in = scatter_about(arg_keys[9], (2, 3, D, D), D ** -0.5, 0.21875, ((3, 2),))
    attention_bias = scatter_about(arg_keys[10], (2, 2, D), 0.2, 1.0, ((2, 2),), jnp.float32)
    attention_out = scatter_about(arg_keys[11], (2, D, D), (D // 16) ** -0.5, 0.875, ((1, 2),))
    output_bias = scatter_about(arg_keys[12], (3, D), 0.2, 1.0, (), jnp.float32)
    norm_gain = jnp.clip(1.0 + 0.1 * jax.random.normal(arg_keys[13], (3, D), jnp.float32), 0.5, 1.5)
    norm_bias = scatter_about(arg_keys[14], (3, D), 0.2, 1.0, (), jnp.float32)
    up_weight = scatter_about(arg_keys[15], (D, FF), D ** -0.5, 0.21875, ((1, 2),))
    up_bias = scatter_about(arg_keys[16], (FF,), 0.2, 1.0, ((0, 2),), jnp.float32)
    down_weight = scatter_about(arg_keys[17], (FF, D), (FF // 2) ** -0.5, 0.15625, ((0, 2),))
    return dict(text=text, cotangent=cotangent, lengths=lengths, box_corners=box_corners, box_counts=box_counts, region_box=region_box, patches=patches, proj_weight=proj_weight, proj_bias=proj_bias, attention_in=attention_in, attention_bias=attention_bias, attention_out=attention_out, output_bias=output_bias, norm_gain=norm_gain, norm_bias=norm_bias, up_weight=up_weight, up_bias=up_bias, down_weight=down_weight)


EPS = 1e-12
NEG = -1e+30
PRECISE = lax.Precision.HIGHEST

@jax.custom_vjp
def low(v):
    return lax.optimization_barrier(v.astype(jnp.bfloat16)).astype(jnp.float32)

@jax.custom_vjp
def low_back(v):
    return v

def low_keep(v):
    return (low(v), None)

def low_pass(kept, grad):
    return (grad,)

def back_keep(v):
    return (v, None)

def back_low(kept, grad):
    return (low(grad),)
low.defvjp(low_keep, low_pass)
low_back.defvjp(back_keep, back_low)

def rounded(v):
    return low_back(low(v))

def linear(a, w):
    return jnp.matmul(a, w, precision=PRECISE)

def normalize(z, gain, shift):
    center = z - lax.optimization_barrier(jnp.mean(z, axis=-1, keepdims=True))
    spread = lax.optimization_barrier(jnp.mean(center * center, axis=-1, keepdims=True))
    return center * lax.rsqrt(spread + EPS) * gain + shift

def split_heads(t):
    return t.reshape(t.shape[:-1] + (HEADS, HEAD_DIM))

def join_heads(t):
    return t.reshape(t.shape[:-2] + (HEADS * HEAD_DIM,))

def attend(q, k, v, keep):
    scores = low_back(jnp.einsum('bqhe,bkhe->bhqk', q, k, precision=PRECISE)) * HEAD_DIM ** (-0.5)
    scores = jnp.where(keep[:, None, None, :], scores, NEG)
    weights = jax.nn.softmax(scores, axis=-1)
    return jnp.einsum('bhqk,bkhe->bqhe', low(weights), v, precision=PRECISE)

def cross_keep(corners, patch_count):
    index = jnp.arange(patch_count, dtype=jnp.int32) - 1
    grid_row = index // GRID
    grid_col = index % GRID
    inside = (grid_col[None, :] >= corners[:, 0:1]) & (grid_col[None, :] < corners[:, 1:2])
    inside = inside & (grid_row[None, :] >= corners[:, 2:3]) & (grid_row[None, :] < corners[:, 3:4])
    return inside | (index[None, :] < 0)

def layer(params, x, patch_rows, keep_self, keep_cross):
    attention_in, attention_bias, attention_out, output_bias, norm_gain, norm_bias, up_weight, up_bias, down_weight = params
    q = rounded(linear(x, attention_in[0, 0]) + attention_bias[0, 0])
    k = rounded(linear(x, attention_in[0, 1]))
    v = rounded(linear(x, attention_in[0, 2]) + attention_bias[0, 1])
    attended = rounded(join_heads(attend(split_heads(q), split_heads(k), split_heads(v), keep_self)))
    after_self = normalize(x + low_back(linear(attended, attention_out[0]) + output_bias[0]), norm_gain[0], norm_bias[0])
    self_low = low(after_self)
    patch_low = low_back(patch_rows)
    q = rounded(linear(self_low, attention_in[1, 0]) + attention_bias[1, 0])
    k = rounded(linear(patch_low, attention_in[1, 1]))
    v = rounded(linear(patch_low, attention_in[1, 2]) + attention_bias[1, 1])
    crossed = rounded(join_heads(attend(split_heads(q), split_heads(k), split_heads(v), keep_cross)))
    after_cross = normalize(after_self + low_back(linear(crossed, attention_out[1]) + output_bias[1]), norm_gain[1], norm_bias[1])
    hidden = low_back(linear(low(after_cross), up_weight) + up_bias)
    activated = low(jax.nn.gelu(hidden, approximate=False))
    return normalize(after_cross + low_back(linear(activated, down_weight) + output_bias[2]), norm_gain[2], norm_bias[2])

def reference(text, cotangent, lengths, box_corners, box_counts, region_box, patches, proj_weight, proj_bias, attention_in, attention_bias, attention_out, output_bias, norm_gain, norm_bias, up_weight, up_bias, down_weight):
    params = tuple((a.astype(jnp.float32) for a in (attention_in, attention_bias, attention_out, output_bias, norm_gain, norm_bias, up_weight, up_bias, down_weight)))
    ends = jnp.cumsum(box_counts.reshape(-1)).astype(jnp.int32)
    row_image = lax.optimization_barrier(jnp.sum((ends[None, :] <= region_box[:, None]).astype(jnp.int32), axis=1)).astype(jnp.int32)

    def project(raw, weight, shift):
        return low(low_back(linear(raw, weight) + shift))
    projected, project_back = jax.vjp(project, patches.astype(jnp.float32), proj_weight.astype(jnp.float32), proj_bias.astype(jnp.float32))
    blocks = ROWS // R_DEV
    patch_count = patches.shape[1]

    def pack(a):
        return a.reshape((blocks, R_DEV) + a.shape[1:])

    def step(total, block):
        x, upstream, phrase_len, corners, images = block
        keep_self = jnp.arange(L, dtype=jnp.int32)[None, :] < phrase_len[:, None]
        keep_cross = cross_keep(corners, patch_count)
        rows = projected[images]
        out, back = jax.vjp(lambda p, a, b: layer(p, a, b, keep_self, keep_cross), params, x, rows)
        grad_params, grad_x, grad_rows = back(upstream)
        total = jax.tree.map(lambda s, t: s + t, total, grad_params)
        return (total, (out.astype(jnp.bfloat16), grad_x.astype(jnp.bfloat16), grad_rows.astype(jnp.bfloat16)))
    zeros = jax.tree.map(jnp.zeros_like, params)
    totals, outs = lax.scan(step, zeros, (pack(text.astype(jnp.float32)), pack(cotangent.astype(jnp.float32)), pack(lengths), pack(box_corners), pack(row_image)))
    merged, grad_text, row_grads = outs
    image_grads = jax.ops.segment_sum(row_grads.reshape((ROWS,) + row_grads.shape[2:]).astype(jnp.float32), row_image, num_segments=IMAGES)
    grad_patches, grad_weight, grad_bias = project_back(image_grads)
    return (merged.reshape(text.shape), grad_text.reshape(text.shape), grad_patches.astype(jnp.bfloat16), grad_weight, grad_bias, totals[0], totals[1], totals[2], totals[3], totals[4], totals[5], totals[6], totals[7], totals[8])
```

```python
import math
from functools import partial

import jax
import jax.numpy as jnp
from jax import lax
from jax.experimental import pallas as pl
from jax.experimental.pallas import tpu as pltpu
from jax.sharding import PartitionSpec as P

HEAD_DIM = 64
GRID = 12
EPS = 1e-12
NEG = -1e30
SCALE = HEAD_DIM ** (-0.5)

F32 = jnp.float32
BF16 = jnp.bfloat16

GROUP = 4 * HEAD_DIM
BAND = 32
BANDS = 5
LANES = 128
TILE = 256
PAIRED = 2
VMEM_LIMIT = 58 << 20


def dot(left, right):
    return lax.dot_general(left, right, (((1,), (0,)), ((), ())), preferred_element_type=F32)


def dot_nt(left, right):
    return lax.dot_general(left, right, (((1,), (1,)), ((), ())), preferred_element_type=F32)


def dot_tn(left, right):
    return lax.dot_general(left, right, (((0,), (0,)), ((), ())), preferred_element_type=F32)


def rows_spec(block, offset):
    rank = len(block)
    return pl.BlockSpec(block, lambda s, *_: (s + offset,) + (0,) * (rank - 1))


def whole_spec(shape):
    rank = len(shape)
    return pl.BlockSpec(shape, lambda s, *_: (0,) * rank, pipeline_mode=pl.Buffered(1))


ANY = pl.BlockSpec(memory_space=pl.ANY)


def run(body, steps, scalars, ins, outs, scratch, flops, after=()):
    ns, ni, no = len(scalars), len(ins), len(outs)

    def kernel(*refs):
        rest = refs[ns + ni + len(after) :]
        body(refs[:ns], refs[ns : ns + ni], rest[:no], rest[no:])

    moved = sum(math.prod(a.shape) * a.dtype.itemsize for a, _ in ins)
    ins = list(ins) + [(array, ANY) for array in after]
    moved += sum(math.prod(shape) * jnp.dtype(dtype).itemsize for shape, dtype, _ in outs)
    return pl.pallas_call(
        kernel,
        grid_spec=pltpu.PrefetchScalarGridSpec(
            num_scalar_prefetch=ns,
            grid=(steps,),
            in_specs=[spec for _, spec in ins],
            out_specs=[spec for _, _, spec in outs],
            scratch_shapes=scratch,
        ),
        out_shape=[jax.ShapeDtypeStruct(shape, dtype) for shape, dtype, _ in outs],
        compiler_params=pltpu.CompilerParams(
            dimension_semantics=("arbitrary",), vmem_limit_bytes=VMEM_LIMIT
        ),
        cost_estimate=pl.CostEstimate(flops=flops, bytes_accessed=moved, transcendentals=0),
    )(*scalars, *[array for array, _ in ins])


class Loads:
    def __init__(self, steps, sems, pairs):
        self.steps = steps
        self.copies = [
            pltpu.make_async_copy(source, target, sems.at[at])
            for at, (source, target) in enumerate(pairs)
        ]

    def first(self, action):
        if self.steps == 1:
            action()
        else:
            pl.when(pl.program_id(0) == 0)(action)

    def start(self):
        self.first(lambda: [copy.start() for copy in self.copies] and None)

    def wait(self, *which):
        self.first(lambda: [self.copies[at].wait() for at in which] and None)


def side_by_side(own, mate, target, width):
    return [(own, target.at[:, pl.ds(0, width)]), (mate, target.at[:, pl.ds(width, width)])]


def one_above(own, mate, target, height):
    return [(own, target.at[pl.ds(0, height)]), (mate, target.at[pl.ds(height, height)])]


def moments(z):
    center = z - jnp.mean(z, axis=-1, keepdims=True)
    rstd = lax.rsqrt(jnp.mean(center * center, axis=-1, keepdims=True) + EPS)
    return center * rstd, rstd


def norm_grad(unit, rstd, gain, grad):
    inner = grad * gain
    return rstd * (
        inner
        - jnp.mean(inner, axis=-1, keepdims=True)
        - unit * jnp.mean(inner * unit, axis=-1, keepdims=True)
    )


def fold(block):
    return jnp.sum(block.reshape(block.shape[0] // 8, 8, block.shape[1]), axis=0)


def gelu(u):
    z = jnp.abs(u) * (0.5**0.5)
    bell = jnp.exp(u * u * -0.5)
    t = 1.0 / (1.0 + 0.3275911 * z)
    poly = t * (
        0.5 * 0.254829592
        + t
        * (
            0.5 * -0.284496736
            + t * (0.5 * 1.421413741 + t * (0.5 * -1.453152027 + t * (0.5 * 1.061405429)))
        )
    )
    tail = poly * bell
    phi = jnp.where(u >= 0.0, 1.0 - tail, tail)
    return u * phi, phi + u * (bell * (1.0 / math.sqrt(2.0 * math.pi)))


def spread_heads(block, lane_head):
    parts = [jnp.where(lane_head == h, block, 0.0) for h in range(GROUP // HEAD_DIM)]
    return jnp.concatenate(parts, axis=0).astype(BF16)


def gather_heads(block, lane_head, tokens):
    total = jnp.where(lane_head == 0, block[0:tokens], 0.0)
    for h in range(1, GROUP // HEAD_DIM):
        total = jnp.where(lane_head == h, block[h * tokens : (h + 1) * tokens], total)
    return total


def lane_heads():
    return lax.broadcasted_iota(jnp.int32, (1, GROUP), 1) // HEAD_DIM


def attend(items):
    scores = [dot_nt(qm, kb) for qm, kb, vb, keep in items]
    weights = []
    for score, (qm, kb, vb, keep) in zip(scores, items):
        score = jnp.where(keep, score, NEG)
        top = jnp.max(score, axis=1, keepdims=True)
        weight = jnp.exp(score - top)
        weight = weight * (1.0 / jnp.sum(weight, axis=1, keepdims=True))
        weights.append(weight.astype(BF16))
    return [dot(weight, vb) for weight, (qm, kb, vb, keep) in zip(weights, items)]


def attend_grad(items):
    scores = [dot_nt(kb, qm) for qm, kb, vb, dom, keep in items]
    grads = [dot_nt(vb, dom) for qm, kb, vb, dom, keep in items]
    middle = []
    for score, grad, (qm, kb, vb, dom, keep) in zip(scores, grads, items):
        score = jnp.where(keep, score, NEG)
        top = jnp.max(score, axis=0, keepdims=True)
        weight = jnp.exp(score - top)
        weight = weight * (1.0 / jnp.sum(weight, axis=0, keepdims=True))
        inner = jnp.sum(weight * grad, axis=0, keepdims=True)
        grad_score = weight * (grad - inner)
        middle.append(
            (weight.astype(BF16), grad_score.astype(BF16), jnp.transpose(grad_score).astype(BF16))
        )
    results = []
    for (weight, grad_score, turned), (qm, kb, vb, dom, keep) in zip(middle, items):
        results.append((dot(turned, kb), dot(grad_score, qm), dot(weight, dom)))
    return results


def box_keep(corners, slot, shape, axis):
    index = lax.broadcasted_iota(jnp.int32, shape, axis) - 1
    grid_row = (index * 2731) >> 15
    grid_col = index - grid_row * GRID
    inside = (grid_col >= corners[slot * 4]) & (grid_col < corners[slot * 4 + 1])
    inside = inside & (grid_row >= corners[slot * 4 + 2]) & (grid_row < corners[slot * 4 + 3])
    return (inside & (index >= 0)) | (index < 0)


def band_loop(total, body, part=None):
    @pl.loop(0, total // (BAND * BANDS))
    def _(step):
        sums = []
        for band in range(BANDS):
            start = pl.multiple_of(step * (BAND * BANDS) + band * BAND, BAND)
            folded = body(pl.ds(start, BAND))
            if folded is not None:
                sums.append(folded)
        for terms in zip(*sums):
            at = terms[0][0]
            part[at] += sum(value for _, value in terms[1:]) + terms[0][1]


def by_columns(left, weight, finish, transposed=False):
    count = weight.shape[0] if transposed else weight.shape[1]
    for start in range(0, count, GROUP):
        cols = slice(start, start + GROUP)
        value = dot_nt(left, weight[cols, :]) if transposed else dot(left, weight[:, cols])
        finish(cols, value)


def both_halves(own, mate, at):
    return jnp.concatenate([own[at[0], at[1] : at[1] + 1], mate[at[0], at[1] : at[1] + 1]], axis=1)


def row_pairs(source, where, first, count, length, finish):
    for at in range(0, count, 2):
        both = [source[where[first + at + n]].astype(F32) for n in range(2)]
        finish(slice(at * length, (at + 2) * length), jnp.concatenate(both, axis=0))


def split_lanes(target, rows, start, value):
    for lane in range(0, value.shape[1], LANES):
        target[(start + lane) // LANES, rows, :] = value[:, lane : lane + LANES]


def join_lanes(source, rows):
    return jnp.concatenate([source[lane, rows, :] for lane in range(source.shape[0])], axis=1)


def fetch_kernel(count, scalars, ins, outs, scratch):
    (source,) = scalars
    (sems,) = scratch
    copies = [
        pltpu.make_async_copy(table.at[source[at]], out.at[at], sems.at[which * count + at])
        for which, (table, out) in enumerate(zip(ins, outs))
        for at in range(count)
    ]
    for copy in copies:
        copy.start()
    for copy in copies:
        copy.wait()


def project_kernel(images, own_images, patch_pad, patch_count, local, scalars, ins, outs, scratch):
    (core,) = scalars
    patches, proj_weight, proj_bias, ain, ain_mate, bias_own, bias_mate = ins
    proj, keys, values = outs
    taken, raw, w1, w2, sems, weight_sems = scratch
    loads = Loads(
        1,
        weight_sems,
        side_by_side(ain.at[1, 1], ain_mate.at[1, 1], w1, local)
        + side_by_side(ain.at[1, 2], ain_mate.at[1, 2], w2, local),
    )
    parts, span = taken.shape[0], taken.shape[1]
    arrivals = Loads(
        1, sems, [(patches.at[pl.ds(n * span, span)], taken.at[n]) for n in range(parts)]
    )
    arrivals.start()
    loads.start()
    rows = span * images
    width = raw.shape[0] * LANES
    for n in range(parts):
        arrivals.wait(n)
        flat = taken[n].reshape(rows, taken.shape[3])
        for start in range(0, width, GROUP):
            cols = slice(start, start + GROUP)
            split_lanes(
                raw,
                slice(n * rows, (n + 1) * rows),
                start,
                dot(flat, proj_weight[:, cols]) + proj_bias[:, cols],
            )
    loads.wait(0, 1, 2, 3)
    bias = both_halves(bias_own, bias_mate, (1, 1))
    first = core[0] * own_images
    rest = jnp.zeros((patch_pad - patch_count, width), F32)

    @pl.loop(0, images // 2)
    def _(step):
        both = []
        for at in range(2):
            which = lax.rem(step * 2 + at + first, images)
            own = jnp.concatenate(
                [
                    raw[lane, pl.ds(which, patch_count, stride=images), :]
                    for lane in range(raw.shape[0])
                ],
                axis=1,
            )
            both.append(jnp.concatenate([own, rest], axis=0))
        low = jnp.concatenate(both, axis=0).astype(BF16)
        pair = pl.ds(step * 2, 2)
        proj[pair] = low.reshape(2, patch_pad, width)
        for start in range(0, width, GROUP):
            cols = slice(start, start + GROUP)
            keys[pair, :, cols] = (
                dot(low, w1[:, cols]).astype(BF16).reshape(2, patch_pad, GROUP)
            )
            values[pair, :, cols] = (
                (dot(low, w2[:, cols]) + bias[:, cols]).astype(BF16).reshape(2, patch_pad, GROUP)
            )


def self_kernel(steps, rows, local, length, scalars, ins, outs, scratch):
    lens, where = scalars
    x_in, ain, ain_mate, aout, aout_mate, bias_own, bias_mate, out_bias, gain, shift = ins
    x_out, z_one, q_out, k_out, v_out, att_own, att_mate, low_out, cross_q = outs
    wq, wk, wv, wo, wc, qs, ks, vs, acc, low, sems = scratch
    total = rows * length
    loads = Loads(
        steps,
        sems,
        side_by_side(ain.at[0, 0], ain_mate.at[0, 0], wq, local)
        + side_by_side(ain.at[0, 1], ain_mate.at[0, 1], wk, local)
        + side_by_side(ain.at[0, 2], ain_mate.at[0, 2], wv, local)
        + one_above(aout.at[0], aout_mate.at[0], wo, local)
        + side_by_side(ain.at[1, 0], ain_mate.at[1, 0], wc, local),
    )
    loads.start()
    bias_q = both_halves(bias_own, bias_mate, (0, 0))
    bias_v = both_halves(bias_own, bias_mate, (0, 1))
    bias_c = both_halves(bias_own, bias_mate, (1, 0))

    def put(at, both):
        x_out[at] = both.astype(BF16)

    base = pl.program_id(0) * rows
    row_pairs(x_in, where, base, rows, length, put)
    xb = x_out[...]

    def keep_q(cols, value):
        value = (value + bias_q[:, cols]).astype(BF16)
        q_out[:, cols] = value
        qs[:, cols] = value.astype(F32) * SCALE

    def keep_k(cols, value):
        value = value.astype(BF16)
        k_out[:, cols] = value
        ks[:, cols] = value.astype(F32)

    def keep_v(cols, value):
        value = (value + bias_v[:, cols]).astype(BF16)
        v_out[:, cols] = value
        vs[:, cols] = value.astype(F32)

    loads.wait(0, 1)
    by_columns(xb, wq, keep_q)
    loads.wait(2, 3)
    by_columns(xb, wk, keep_k)
    loads.wait(4, 5)
    by_columns(xb, wv, keep_v)
    lane_head = lane_heads()
    key_index = lax.broadcasted_iota(jnp.int32, (1, length), 1)

    @pl.loop(0, rows // PAIRED)
    def _(step):
        items, places = [], []
        for row in range(PAIRED):
            row = step * PAIRED + row
            at = pl.ds(pl.multiple_of(row * length, 8), length)
            keep = key_index < lens[base + row]
            for g in range(qs.shape[1] // GROUP):
                lanes = slice(g * GROUP, (g + 1) * GROUP)
                items.append(
                    (
                        spread_heads(qs[at, lanes], lane_head),
                        ks[at, lanes].astype(BF16),
                        vs[at, lanes].astype(BF16),
                        keep,
                    )
                )
                places.append((at, lanes))
        for (at, lanes), result in zip(places, attend(items)):
            acc[at, lanes] = gather_heads(result, lane_head, length)

    def cast(at):
        value = acc[at].astype(BF16)
        low[at] = value
        att_own[at] = value[:, :local]
        att_mate[at] = value[:, local:]

    def to_acc(cols, value):
        acc[:, cols] = value

    band_loop(total, cast)
    loads.wait(6, 7)
    by_columns(low[...], wo, to_acc)

    def norm(at):
        z = x_out[at].astype(F32) + acc[at] + out_bias[0:1]
        z_one[at] = z
        unit, _ = moments(z)
        h = (unit * gain[0:1] + shift[0:1]).astype(BF16)
        low[at] = h
        low_out[at] = h

    band_loop(total, norm)
    loads.wait(8, 9)

    def to_query(cols, value):
        cross_q[:, cols] = (value + bias_c[:, cols]).astype(BF16)

    by_columns(low[...], wc, to_query)


def cross_kernel(rows, length, scalars, ins, outs, scratch):
    image, corners = scalars
    queries, keys, values = ins
    (att,) = outs
    qs, acc = scratch
    patch_pad = keys.shape[1]
    lane_head = lane_heads()
    base = pl.program_id(0) * rows

    def spread(at):
        qs[at] = queries[at].astype(F32) * SCALE

    band_loop(rows * length, spread)

    @pl.loop(0, rows // PAIRED)
    def _(step):
        items, places = [], []
        for row in range(PAIRED):
            row = step * PAIRED + row
            at = pl.ds(pl.multiple_of(row * length, 8), length)
            which = image[base + row]
            keep = box_keep(corners, base + row, (1, patch_pad), 1)
            for g in range(qs.shape[1] // GROUP):
                lanes = slice(g * GROUP, (g + 1) * GROUP)
                items.append(
                    (
                        spread_heads(qs[at, lanes], lane_head),
                        keys[which, :, lanes],
                        values[which, :, lanes],
                        keep,
                    )
                )
                places.append((at, lanes))
        for (at, lanes), result in zip(places, attend(items)):
            acc[at, lanes] = gather_heads(result, lane_head, length)

    def cast(at):
        att[at] = acc[at].astype(BF16)

    band_loop(rows * length, cast)


def feed_kernel(steps, rows, local, hidden, length, scalars, ins, outs, scratch):
    (where,) = scalars
    grad_in, att, z_one, aout, aout_mate, up, up_mate, down, down_mate = ins[:9]
    out_bias, gains, shift, up_bias, up_bias_mate = ins[9:]
    merged, low_out, df_out, do_out, dz_out, a_own, a_mate = outs[:7]
    g_out, du_out = outs[7:9], outs[9:11]
    da_out, sums, up_sums = outs[11:]
    wo, wu0, wu1, wd0, wd1, acc, kept, unit_two, rstd_two, low, upstream, slope, part, up_part, sems = (
        scratch
    )
    total = rows * length
    loads = Loads(
        steps,
        sems,
        one_above(aout.at[1], aout_mate.at[1], wo, local)
        + [(up, wu0), (down, wd0), (up_mate, wu1), (down_mate, wd1)],
    )
    loads.start()
    part[...] = jnp.zeros_like(part)

    def put(at, both):
        upstream[at] = both.astype(BF16)

    base = pl.program_id(0) * rows
    row_pairs(grad_in, where, base, rows, length, put)

    def to_acc(cols, value):
        acc[:, cols] = value

    a_own[...] = att[:, :local]
    a_mate[...] = att[:, local:]
    loads.wait(0, 1)
    by_columns(att[...], wo, to_acc)

    def norm_two(at):
        unit, _ = moments(z_one[at])
        h_one = unit * gains[0:1] + shift[0:1]
        unit, rstd = moments(h_one + acc[at] + out_bias[1:2])
        h_two = unit * gains[1:2] + shift[1:2]
        unit_two[at] = unit
        rstd_two[at] = rstd
        kept[at] = h_two
        h_low = h_two.astype(BF16)
        low[at] = h_low
        low_out[at] = h_low

    band_loop(total, norm_two)
    acc[...] = jnp.zeros_like(acc)
    loads.wait(2, 3, 4, 5)

    @pl.loop(0, hidden // TILE)
    def _(step):
        cols = pl.ds(pl.multiple_of(step * TILE, TILE), TILE)
        units = [dot(low[...], wu[:, cols]) for wu in (wu0, wu1)]
        for half, (wd, biases) in enumerate(((wd0, up_bias), (wd1, up_bias_mate))):
            bias = biases[:, cols]
            for start in range(0, total, BAND):
                at = slice(start, start + BAND)
                active, sloped = gelu(units[half][at] + bias)
                g_out[half][at, cols] = active.astype(BF16)
                slope[half, at, cols] = sloped
            acc[...] += dot(g_out[half][:, cols], wd[cols, :])

    def norm_three(at):
        unit, rstd = moments(kept[at] + acc[at] + out_bias[2:3])
        gain = gains[2:3]
        unit_three = unit * gain + shift[2:3]
        grad = upstream[at].astype(F32)
        dz = norm_grad(unit, rstd, gain, grad)
        kept[at] = dz
        acc[at] = unit_three
        dz_low = dz.astype(BF16)
        low[at] = dz_low
        df_out[at] = dz_low
        return (
            (0, fold(dz_low.astype(F32))),
            (1, fold(grad * unit)),
            (2, fold(grad)),
        )

    band_loop(total, norm_three, part)

    for row in range(rows):
        merged[where[base + row]] = acc[row * length : (row + 1) * length].astype(BF16)
    acc[...] = jnp.zeros_like(acc)

    @pl.loop(0, hidden // TILE)
    def _(step):
        cols = pl.ds(pl.multiple_of(step * TILE, TILE), TILE)
        grads = [dot_nt(low[...], wd[cols, :]) for wd in (wd0, wd1)]
        for half, wu in enumerate((wu0, wu1)):
            folded = 0.0
            for start in range(0, total, BAND):
                at = slice(start, start + BAND)
                du = (grads[half][at] * slope[half, at, cols]).astype(BF16)
                du_out[half][at, cols] = du
                folded = folded + fold(du.astype(F32))
            up_part[half, :, cols] = folded
            acc[...] += dot_nt(du_out[half][:, cols], wu[:, cols])

    def norm_two_back(at):
        grad = kept[at] + acc[at]
        unit = unit_two[at]
        dz = norm_grad(unit, rstd_two[at], gains[1:2], grad)
        dz_out[at] = dz
        dz_low = dz.astype(BF16)
        low[at] = dz_low
        do_out[at] = dz_low
        return (
            (3, fold(dz_low.astype(F32))),
            (4, fold(grad * unit)),
            (5, fold(grad)),
        )

    band_loop(total, norm_two_back, part)

    def to_grad(cols, value):
        da_out[:, cols] = value.astype(BF16)

    by_columns(low[...], wo, to_grad, transposed=True)
    for at in range(8):
        sums[0, at : at + 1] = jnp.sum(part[at], axis=0, keepdims=True)
    for half in range(2):
        up_sums[0, half : half + 1] = jnp.sum(up_part[half], axis=0, keepdims=True)


def cross_grad_kernel(steps, rows, length, scalars, ins, outs, scratch):
    image, corners = scalars
    queries, grads, keys, values = ins
    own, mate, grad_queries = outs
    qs, gs, acc, dk, dv = scratch
    patch_pad = keys.shape[1]

    def clear():
        @pl.loop(0, dk.shape[0])
        def _(at):
            dk[at] = jnp.zeros(dk.shape[1:], F32)
            dv[at] = jnp.zeros(dv.shape[1:], F32)

    pl.when(pl.program_id(0) == 0)(clear)

    def spread(at):
        qs[at] = queries[at].astype(F32) * SCALE
        gs[at] = grads[at].astype(F32)

    band_loop(rows * length, spread)
    lane_head = lane_heads()
    base = pl.program_id(0) * rows

    @pl.loop(0, rows // PAIRED)
    def _(step):
        items, places = [], []
        for row in range(PAIRED):
            row = step * PAIRED + row
            at = pl.ds(pl.multiple_of(row * length, 8), length)
            which = image[base + row]
            keep = box_keep(corners, base + row, (patch_pad, 1), 0)
            for g in range(qs.shape[1] // GROUP):
                lanes = slice(g * GROUP, (g + 1) * GROUP)
                items.append(
                    (
                        spread_heads(qs[at, lanes], lane_head),
                        keys[which, :, lanes],
                        values[which, :, lanes],
                        spread_heads(gs[at, lanes], lane_head),
                        keep,
                    )
                )
                places.append((at, which, lanes))
        for (at, which, lanes), (grad_q, grad_k, grad_v) in zip(places, attend_grad(items)):
            acc[at, lanes] = gather_heads(grad_q, lane_head, length) * SCALE
            dk[which, :, lanes] += grad_k
            dv[which, :, lanes] += grad_v

    def cast(at):
        grad_queries[at] = acc[at].astype(BF16)

    band_loop(rows * length, cast)

    @pl.when(pl.program_id(0) == steps - 1)
    def _():
        half = own.shape[1]

        @pl.loop(0, half)
        def _(at):
            own[0, at] = dk[at].astype(BF16)
            own[1, at] = dv[at].astype(BF16)
            mate[0, at] = dk[half + at].astype(BF16)
            mate[1, at] = dv[half + at].astype(BF16)


def image_kernel(images, patch_count, local, scalars, ins, outs, scratch):
    (core,) = scalars
    piece, piece_mate, patches, proj_weight, ain, ain_mate = ins
    kv_own, kv_mate, patch_grad, weight_grad, sums = outs
    narrow, wide, taken, w1, w2, part, sems, weight_sems = scratch
    parts, span = taken.shape[0], taken.shape[1]
    loads = Loads(
        1,
        weight_sems,
        side_by_side(ain.at[1, 1], ain_mate.at[1, 1], w1, local)
        + side_by_side(ain.at[1, 2], ain_mate.at[1, 2], w2, local),
    )
    arrivals = Loads(
        1, sems, [(patches.at[pl.ds(n * span, span)], taken.at[n]) for n in range(parts)]
    )
    loads.start()
    arrivals.start()
    part[...] = jnp.zeros_like(part)
    own_images, patch_pad = piece.shape[1], piece.shape[2]
    width = w1.shape[0]

    slab = 80

    @pl.loop(0, wide.shape[1] // slab)
    def _(step):
        at = pl.ds(pl.multiple_of(step * slab, slab), slab)
        for lane in range(wide.shape[0]):
            wide[lane, at] = jnp.zeros((slab, LANES), F32)

    loads.wait(0, 1, 2, 3)
    first = core[0] * own_images

    @pl.loop(0, own_images // 2)
    def _(step):
        pair = pl.ds(step * 2, 2)
        halves = []
        for half in (slice(0, local), slice(local, width)):
            swapped = slice(width - half.stop, width - half.start)
            both = piece[:, pair, :, half].astype(F32) + piece_mate[:, pair, :, swapped].astype(F32)
            both = both.astype(BF16)
            halves.append([both[at].reshape(2 * patch_pad, local) for at in range(2)])
        (dk_own, dv_own), (dk_mate, dv_mate) = halves
        rows = pl.ds(pl.multiple_of(step * 2 * patch_pad, 2 * patch_pad), 2 * patch_pad)
        kv_own[rows, :local] = dk_own
        kv_own[rows, local:] = dv_own
        kv_mate[rows, :local] = dk_mate
        kv_mate[rows, local:] = dv_mate
        dk = jnp.concatenate([dk_own, dk_mate], axis=1)
        dv = jnp.concatenate([dv_own, dv_mate], axis=1)
        part[1] += fold(dv.astype(F32))
        for start in range(0, width, GROUP):
            cols = slice(start, start + GROUP)
            grad = dot_nt(dk, w1[cols, :]) + dot_nt(dv, w2[cols, :])
            grad = grad.astype(BF16).astype(F32)
            part[0, :, cols] += fold(grad)
            for at in range(2):
                one = grad[at * patch_pad : at * patch_pad + patch_count]
                which = step * 2 + at
                spot = pl.ds(which, patch_count, stride=own_images)
                split_lanes(narrow, spot, start, one)
                split_lanes(wide, pl.ds(which + first, patch_count, stride=images), start, one)

    for n in range(parts):
        arrivals.wait(n)
        few = slice(n * span * own_images, (n + 1) * span * own_images)
        some = join_lanes(narrow, few).astype(BF16)
        for start in range(0, proj_weight.shape[0], GROUP):
            cols = slice(start, start + GROUP)
            back = dot_nt(some, proj_weight[cols, :]).astype(BF16)
            patch_grad[n * span : (n + 1) * span, :, cols] = back.reshape(span, own_images, GROUP)
        flat = taken[n].reshape(span * images, taken.shape[3])
        grad = join_lanes(wide, slice(n * span * images, (n + 1) * span * images)).astype(BF16)
        product = dot_tn(flat, grad)
        if n == 0:
            weight_grad[...] = product
        else:
            weight_grad[...] += product
    for at in range(2):
        sums[at : at + 1] = jnp.sum(part[at], axis=0, keepdims=True)


def self_grad_kernel(steps, rows, local, length, scalars, ins, outs, scratch):
    lens, where = scalars
    dq2, z_one, dz_two, q_in, k_in, v_in, ain, ain_mate, aout, aout_mate, gain = ins
    text_grad, do_out, dq2_own, dq2_mate, qkv_own, qkv_mate, sums = outs
    wc, wo, wq, wk, wv, acc, kept, low, low_k, low_v, qs, ks, vs, part, sems = scratch
    total = rows * length
    loads = Loads(
        steps,
        sems,
        side_by_side(ain.at[1, 0], ain_mate.at[1, 0], wc, local)
        + one_above(aout.at[0], aout_mate.at[0], wo, local)
        + side_by_side(ain.at[0, 0], ain_mate.at[0, 0], wq, local)
        + side_by_side(ain.at[0, 1], ain_mate.at[0, 1], wk, local)
        + side_by_side(ain.at[0, 2], ain_mate.at[0, 2], wv, local),
    )
    loads.start()
    part[...] = jnp.zeros_like(part)

    def to_acc(cols, value):
        acc[:, cols] = value

    loads.wait(0, 1)
    by_columns(dq2[...], wc, to_acc, transposed=True)

    def norm_back(at):
        unit, rstd = moments(z_one[at])
        grad = dz_two[at] + acc[at]
        dz = norm_grad(unit, rstd, gain[0:1], grad)
        kept[at] = dz
        dz_low = dz.astype(BF16)
        low[at] = dz_low
        do_out[at] = dz_low
        qs[at] = q_in[at].astype(F32) * SCALE
        ks[at] = k_in[at].astype(F32)
        vs[at] = v_in[at].astype(F32)
        query = dq2[at]
        dq2_own[at] = query[:, :local]
        dq2_mate[at] = query[:, local:]
        return (
            (0, fold(dz_low.astype(F32))),
            (1, fold(grad * unit)),
            (2, fold(grad)),
            (5, fold(query.astype(F32))),
        )

    band_loop(total, norm_back, part)
    loads.wait(2, 3)
    by_columns(low[...], wo, to_acc, transposed=True)
    lane_head = lane_heads()
    key_index = lax.broadcasted_iota(jnp.int32, (length, 1), 0)
    base = pl.program_id(0) * rows

    @pl.loop(0, rows // PAIRED)
    def _(step):
        items, places = [], []
        for row in range(PAIRED):
            row = step * PAIRED + row
            at = pl.ds(pl.multiple_of(row * length, 8), length)
            keep = key_index < lens[base + row]
            for g in range(qs.shape[1] // GROUP):
                lanes = slice(g * GROUP, (g + 1) * GROUP)
                items.append(
                    (
                        spread_heads(qs[at, lanes], lane_head),
                        ks[at, lanes].astype(BF16),
                        vs[at, lanes].astype(BF16),
                        spread_heads(acc[at, lanes], lane_head),
                        keep,
                    )
                )
                places.append((at, lanes))
        for (at, lanes), (grad_q, grad_k, grad_v) in zip(places, attend_grad(items)):
            qs[at, lanes] = gather_heads(grad_q, lane_head, length) * SCALE
            ks[at, lanes] = grad_k
            vs[at, lanes] = grad_v

    def cast(at):
        sums = []
        for slot, (source, target) in enumerate(((qs, low), (ks, low_k), (vs, low_v))):
            value = source[at].astype(BF16)
            target[at] = value
            qkv_own[at, slot * local : (slot + 1) * local] = value[:, :local]
            qkv_mate[at, slot * local : (slot + 1) * local] = value[:, local:]
            if slot != 1:
                sums.append((3 + slot // 2, fold(value.astype(F32))))
        return sums

    band_loop(total, cast, part)
    loads.wait(4, 5, 6, 7, 8, 9)
    for start in range(0, kept.shape[1], GROUP):
        cols = slice(start, start + GROUP)
        acc[:, cols] = (
            kept[:, cols]
            + dot_nt(low[...], wq[cols, :])
            + dot_nt(low_k[...], wk[cols, :])
            + dot_nt(low_v[...], wv[cols, :])
        )

    for row in range(rows):
        text_grad[where[base + row]] = acc[row * length : (row + 1) * length].astype(BF16)
    for at in range(8):
        sums[0, at : at + 1] = jnp.sum(part[at], axis=0, keepdims=True)


def pack_kernel(local, hidden, scalars, ins, outs, scratch):
    (core,) = scalars
    feed, up, self_, image = ins
    feed_sum = jnp.sum(feed[...], axis=0)
    self_sum = jnp.sum(self_[...], axis=0)
    up_sum = jnp.sum(up[...], axis=0)
    common = [(0, 0), (1, 3), (1, 0), (0, 1), (1, 4), (1, 1), (0, 2), (1, 5), (1, 2)]
    even = core[0] == 0
    for out, mine in zip(outs, (True, False)):
        out[...] = jnp.zeros_like(out)
        at = 0
        for which, row in common:
            source = feed_sum if which else self_sum
            for half in range(2):
                out[at : at + 1] = source[row : row + 1, half * local : (half + 1) * local]
                at += 1
        lanes = slice(0, local) if mine else slice(local, 2 * local)
        for row in (3, 4, 5):
            out[at : at + 1] = self_sum[row : row + 1, lanes]
            at += 1
        out[at : at + 1] = image[1:2, lanes]
        at += 1
        half = 0 if mine else 1
        for start in range(0, hidden, local):
            out[at : at + 1] = up_sum[half : half + 1, start : start + local]
            at += 1
        low, high = image[0:1, :local], image[0:1, local:]
        out[at : at + 1] = jnp.where(even == mine, low, high)


def halve_kernel(rows, length, scalars, ins, outs, scratch):
    core, where = scalars
    (tall,) = scratch

    def put(at, both):
        split_lanes(tall, at, 0, both)

    row_pairs(ins[0], where, 0, rows, length, put)
    half = length // 2
    for out, first in zip(outs, (core[0] * half, (1 - core[0]) * half)):
        for token in range(half):
            out[token] = join_lanes(
                tall, pl.ds(first + token, rows, stride=length)
            ).astype(BF16)


def place_kernel(scalars, ins, outs, scratch):
    own, mate, place = ins
    (out,) = outs
    count, slots = out.shape[1], own.shape[1]
    index = lax.broadcasted_iota(jnp.int32, (count, slots), 1)
    from_own = jnp.where(place[...] == index, 1.0, 0.0).astype(BF16)
    from_mate = jnp.where(place[...] == index + slots, 1.0, 0.0).astype(BF16)
    for token in range(out.shape[0]):
        out[token] = (dot(from_own, own[token]) + dot(from_mate, mate[token])).astype(BF16)


def body(
    text,
    cotangent,
    lengths,
    box_corners,
    box_counts,
    region_box,
    patches,
    proj_weight,
    proj_bias,
    attention_in,
    attention_bias,
    attention_out,
    output_bias,
    norm_gain,
    norm_bias,
    up_weight,
    up_bias,
    down_weight,
):
    rows, length, width = text.shape
    images, patch_count, vision = patches.shape
    local = attention_in.shape[-1]
    hidden = up_weight.shape[-1]
    devices = lax.axis_size("dp")
    me, core = lax.axis_index("dp"), lax.axis_index("mp")
    pair = -(-rows // devices)
    each, odd = pair // 2, pair % 2
    deep = each + odd
    slots = devices * each + devices // 2 * odd
    patch_pad = -(-patch_count // 16) * 16
    own_images = images // 2
    step_rows = 12 if slots % 12 == 0 else 8
    steps = slots // step_rows
    tokens = step_rows * length
    all_tokens = slots * length
    full = slots * 2 == rows
    core_scalar = core.astype(jnp.int32).reshape(1)

    def mate(value):
        return lax.ppermute(value, "mp", [(0, 1), (1, 0)])

    def tie(*values):
        return lax.optimization_barrier(values)

    def exchange(value):
        return lax.all_to_all(value, "dp", split_axis=0, concat_axis=0, tiled=True)

    ain_mate = mate(attention_in)
    bias_mate = mate(attention_bias)
    aout_mate = mate(attention_out)
    up_bias_own = up_bias.reshape(1, hidden)
    up_bias_mate = mate(up_bias_own)
    up_mate = mate(up_weight)
    down_mate = mate(down_weight)

    number = jnp.arange(rows, dtype=jnp.int32)
    target = region_box // rows
    earlier = (target[:, None] == target[None, :]) & (number[None, :] < number[:, None])
    nth = jnp.sum(earlier.astype(jnp.int32), axis=1)
    even_part = nth < 2 * each
    row_core = jnp.where(even_part, nth // max(each, 1), (target ^ me) & 1)
    depth = jnp.where(even_part, nth % max(each, 1), each)
    spot = jnp.arange(devices * deep, dtype=jnp.int32)
    hit = (spot[:, None] == (target * deep + depth)[None, :]) & (row_core == core)[None, :]
    source = jnp.sum(jnp.where(hit, number[None, :], 0), axis=1)
    slot = jnp.where(even_part, target * each + depth, devices * each + (target >> 1))
    place = jnp.where(row_core == core, slot, slot + slots)[:, None]
    order = jnp.arange(slots, dtype=jnp.int32)
    late = order - devices * each
    where = jnp.where(
        late < 0,
        order // max(each, 1) * deep + order % max(each, 1),
        (2 * late + ((me & 1) ^ core)) * deep + each,
    )
    meta = jnp.concatenate(
        [(region_box % rows)[:, None], lengths[:, None], box_corners], axis=1
    )
    meta_out = jnp.sum(jnp.where(hit[:, :, None], meta[None], 0), axis=1)
    if not full:
        empty = jnp.array([0, 1, 0, 1, 0, 1], jnp.int32)
        meta_out = jnp.where(jnp.any(hit, axis=1)[:, None], meta_out, empty[None])
    arrived = exchange(meta_out)[where]
    ends = jnp.cumsum(box_counts[0])
    image = jnp.sum((ends[None, :] <= arrived[:, 0:1]).astype(jnp.int32), axis=1)
    image = (image + own_images * core) % images
    lens = arrived[:, 1]
    corners = arrived[:, 2:].reshape(-1)

    block_shape = (devices * deep, length, width)
    if full:
        x_out, upstream_out = run(
            partial(fetch_kernel, devices * deep),
            1,
            [source],
            [(text, ANY), (cotangent, ANY)],
            [(block_shape, BF16, whole_spec(block_shape))] * 2,
            [pltpu.SemaphoreType.DMA((2 * devices * deep,))],
            0,
        )
    else:
        valid = jnp.any(hit, axis=1)[:, None, None]
        x_out = jnp.where(valid, text[source], 0)
        upstream_out = jnp.where(valid, cotangent[source], 0)
    x_in = exchange(x_out)

    patches, aout_mate, image, corners, lens = tie(patches, aout_mate, image, corners, lens)
    by_patch = jnp.transpose(patches, (1, 0, 2))
    parts = next(n for n in (5, 4, 3, 2, 1) if patch_count % n == 0)
    weight_scratch = pltpu.VMEM((width, width), BF16)

    def slabs(count):
        return pltpu.VMEM((width // LANES, count, LANES), F32)

    patch_scratch = pltpu.VMEM((parts, patch_count // parts, images, vision), BF16)
    image_shape = (images, patch_pad, width)
    proj, keys, values = run(
        partial(project_kernel, images, own_images, patch_pad, patch_count, local),
        1,
        [core_scalar],
        [
            (by_patch, ANY),
            (proj_weight, whole_spec(proj_weight.shape)),
            (proj_bias.reshape(1, width), whole_spec((1, width))),
            (attention_in, ANY),
            (ain_mate, ANY),
            (attention_bias, whole_spec(attention_bias.shape)),
            (bias_mate, whole_spec(bias_mate.shape)),
        ],
        [(image_shape, BF16, whole_spec(image_shape))] * 3,
        [
            patch_scratch,
            slabs(patch_count * images),
            weight_scratch,
            weight_scratch,
            pltpu.SemaphoreType.DMA((parts,)),
            pltpu.SemaphoreType.DMA((4,)),
        ],
        2 * images * patch_pad * width * (vision + 2 * width),
    )

    upstream_out, proj, keys, values = tie(upstream_out, proj, keys, values)
    upstream_in = exchange(upstream_out)

    def token_in(value):
        return (value, rows_spec((tokens, value.shape[1]), 0))

    def token_out(cols, dtype):
        return ((all_tokens, cols), dtype, rows_spec((tokens, cols), 0))

    block_out = (block_shape, BF16, whole_spec(block_shape))

    def f32_tokens(cols):
        return pltpu.VMEM((tokens, cols), F32)

    def low_tokens(cols):
        return pltpu.VMEM((tokens, cols), BF16)

    def whole(value):
        return (value, whole_spec(value.shape))

    attention_flops = 4 * 4 * all_tokens * width * 64

    x, z_one, q_self, k_self, v_self, att_own, att_mate, self_low, queries = run(
        partial(self_kernel, steps, step_rows, local, length),
        steps,
        [lens, where],
        [
            whole(x_in),
            (attention_in, ANY),
            (ain_mate, ANY),
            (attention_out, ANY),
            (aout_mate, ANY),
            whole(attention_bias),
            whole(bias_mate),
            whole(output_bias),
            whole(norm_gain),
            whole(norm_bias),
        ],
        [token_out(width, BF16), token_out(width, F32)]
        + [token_out(width, BF16)] * 3
        + [token_out(local, BF16)] * 2
        + [token_out(width, BF16)] * 2,
        [weight_scratch] * 5
        + [f32_tokens(width)] * 4
        + [low_tokens(width), pltpu.SemaphoreType.DMA((10,))],
        2 * all_tokens * width * width * 5 + attention_flops,
    )

    (attended,) = run(
        partial(cross_kernel, step_rows, length),
        steps,
        [image, corners],
        [token_in(queries), whole(keys), whole(values)],
        [token_out(width, BF16)],
        [f32_tokens(width)] * 2,
        attention_flops * 4,
    )

    result = run(
        partial(feed_kernel, steps, step_rows, local, hidden, length),
        steps,
        [where],
        [
            whole(upstream_in),
            token_in(attended),
            token_in(z_one),
            (attention_out, ANY),
            (aout_mate, ANY),
            (up_weight, ANY),
            (up_mate, ANY),
            (down_weight, ANY),
            (down_mate, ANY),
            whole(output_bias),
            whole(norm_gain),
            whole(norm_bias),
            whole(up_bias_own),
            whole(up_bias_mate),
        ],
        [block_out]
        + [token_out(width, BF16)] * 3
        + [token_out(width, F32)]
        + [token_out(local, BF16)] * 2
        + [token_out(hidden, BF16)] * 4
        + [
            token_out(width, BF16),
            ((steps, 8, width), F32, rows_spec((1, 8, width), 0)),
            ((steps, 2, hidden), F32, rows_spec((1, 2, hidden), 0)),
        ],
        [weight_scratch]
        + [pltpu.VMEM((width, hidden), BF16)] * 2
        + [pltpu.VMEM((hidden, width), BF16)] * 2
        + [f32_tokens(width)] * 3
        + [f32_tokens(1), low_tokens(width), low_tokens(width)]
        + [pltpu.VMEM((2, tokens, hidden), F32)]
        + [pltpu.VMEM((8, 8, width), F32), pltpu.VMEM((2, 8, hidden), F32)]
        + [pltpu.SemaphoreType.DMA((6,))],
        2 * all_tokens * width * (2 * width + 8 * hidden),
    )
    merged_out, cross_low, grad_ffn, grad_cross, dz_two, a_own, a_mate = result[:7]
    g_own, g_mate, du_own, du_mate, grad_att, feed_sums, up_sums = result[7:]

    bits = devices.bit_length() - 1

    def partner_bits(value, mask):
        return lax.ppermute(value, "dp", [(d, d ^ mask) for d in range(devices)])

    def opened(value):
        return value.reshape((2,) * bits + (value.shape[0] // devices, value.shape[1]))

    def swap(value, axis, bit):
        mine = (me >> bit) & 1
        away = lax.dynamic_index_in_dim(value, 1 - mine, axis, keepdims=False)
        stay = lax.dynamic_index_in_dim(value, mine, axis, keepdims=False)
        return stay, partner_bits(away, 1 << bit)

    def first_swaps(by_x, by_y):
        return swap(opened(by_x), bits - 1, 0) + swap(opened(by_y), bits - 2, 1)

    def second_swaps(stay_x, got_x, stay_y, got_y):
        return swap(add(stay_x, got_x), bits - 2, 1) + swap(add(stay_y, got_y), bits - 2, 0)

    def add(stay, got):
        return (stay.astype(F32) + got.astype(F32)).astype(BF16)

    def last_parts(stay_x, got_x, stay_y, got_y):
        parts = [add(stay_x, got_x), add(stay_y, got_y)]
        return jnp.concatenate(
            [part.reshape((devices // 4,) + part.shape[-2:]) for part in parts], axis=2
        )

    def last_sum(both, first_width):
        groups = [[low + 4 * n for n in range(devices // 4)] for low in range(4)]
        both = lax.all_to_all(
            both, "dp", split_axis=0, concat_axis=0, axis_index_groups=groups, tiled=True
        )
        total = jnp.sum(both.astype(F32), axis=0)
        return total[:, :first_width], total[:, first_width:]

    def low_tn(left, right):
        return dot_tn(left, right).astype(BF16)

    merged_in = exchange(merged_out)
    up_away, down_away = low_tn(cross_low, du_mate), low_tn(grad_ffn, g_mate)
    grad_att, queries, up_away, down_away = tie(grad_att, queries, up_away, down_away)
    up_got, down_got = mate(up_away), mate(down_away)

    half_shape = (2, own_images, patch_pad, width)
    image_acc = pltpu.VMEM(image_shape, F32)
    piece, piece_out, grad_queries = run(
        partial(cross_grad_kernel, steps, step_rows, length),
        steps,
        [image, corners],
        [token_in(queries), token_in(grad_att), whole(keys), whole(values)],
        [(half_shape, BF16, whole_spec(half_shape))] * 2 + [token_out(width, BF16)],
        [f32_tokens(width)] * 3 + [image_acc] * 2,
        attention_flops * 12,
    )
    piece_mate = mate(piece_out)

    up_part = (dot_tn(cross_low, du_own) + up_got.astype(F32)).astype(BF16)
    down_part = (dot_tn(grad_ffn, g_own) + down_got.astype(F32)).astype(BF16)
    grad_queries, up_part, down_part = tie(grad_queries, up_part, down_part)
    feed_stage = first_swaps(up_part, down_part)

    result = run(
        partial(self_grad_kernel, steps, step_rows, local, length),
        steps,
        [lens, where],
        [
            token_in(grad_queries),
            token_in(z_one),
            token_in(dz_two),
            token_in(q_self),
            token_in(k_self),
            token_in(v_self),
            (attention_in, ANY),
            (ain_mate, ANY),
            (attention_out, ANY),
            (aout_mate, ANY),
            whole(norm_gain),
        ],
        [block_out]
        + [token_out(width, BF16)]
        + [token_out(local, BF16)] * 2
        + [token_out(3 * local, BF16)] * 2
        + [((steps, 8, width), F32, rows_spec((1, 8, width), 0))],
        [weight_scratch] * 5
        + [f32_tokens(width)] * 2
        + [low_tokens(width)] * 3
        + [f32_tokens(width)] * 3
        + [pltpu.VMEM((8, 8, width), F32), pltpu.SemaphoreType.DMA((10,))],
        2 * all_tokens * width * width * 5 + attention_flops * 2,
    )
    text_out, grad_self, dq_own, dq_mate, qkv_own, qkv_mate, self_sums = result
    text_in = exchange(text_out)

    self_away = jnp.concatenate(
        [
            low_tn(x, qkv_mate),
            low_tn(grad_self, att_mate),
            low_tn(grad_cross, a_mate),
            low_tn(self_low, dq_mate),
        ],
        axis=1,
    )
    self_got = mate(self_away)
    feed_stage = tie(self_away, *feed_stage)[1:]
    feed_stage = second_swaps(*feed_stage)
    self_own = jnp.concatenate(
        [
            dot_tn(x, qkv_own),
            dot_tn(grad_self, att_own),
            dot_tn(grad_cross, a_own),
            dot_tn(self_low, dq_own),
        ],
        axis=1,
    )
    self_part = (self_own + self_got.astype(F32)).astype(BF16)
    half_width = self_part.shape[1] // 2
    self_stage = first_swaps(self_part[:, :half_width], self_part[:, half_width:])
    feed_parts = last_parts(*feed_stage)
    piece, piece_mate, self_part, feed_parts = tie(piece, piece_mate, self_part, feed_parts)

    flat_images = own_images * patch_pad
    patch_grad_shape = (patch_count, own_images, vision)
    kv_own, kv_mate, patch_grad, proj_weight_sum, image_sums = run(
        partial(image_kernel, images, patch_count, local),
        1,
        [core_scalar],
        [
            whole(piece),
            whole(piece_mate),
            (by_patch, ANY),
            whole(proj_weight),
            (attention_in, ANY),
            (ain_mate, ANY),
        ],
        [
            ((flat_images, width), BF16, whole_spec((flat_images, width))),
            ((flat_images, width), BF16, whole_spec((flat_images, width))),
            (patch_grad_shape, BF16, whole_spec(patch_grad_shape)),
            ((vision, width), F32, whole_spec((vision, width))),
            ((8, width), F32, whole_spec((8, width))),
        ],
        [
            slabs(patch_count * own_images),
            slabs(patch_count * images),
            patch_scratch,
            weight_scratch,
            weight_scratch,
            pltpu.VMEM((2, 8, width), F32),
            pltpu.SemaphoreType.DMA((parts,)),
            pltpu.SemaphoreType.DMA((4,)),
        ],
        2 * flat_images * width * (2 * width + 2 * vision),
    )

    up_grad, down_grad = last_sum(feed_parts, hidden)
    self_stage = second_swaps(*self_stage)
    kv_low = proj[:own_images].reshape(flat_images, width)
    kv_away = low_tn(kv_low, kv_mate)
    kv_got = mate(kv_away)
    proj_away = lax.dynamic_slice_in_dim(proj_weight_sum, (1 - core) * local, local, 1)
    proj_got = mate(proj_away.astype(BF16))
    kv_part = (dot_tn(kv_low, kv_own) + kv_got.astype(F32)).astype(BF16)
    proj_own = lax.dynamic_slice_in_dim(proj_weight_sum, core * local, local, 1)
    proj_part = (proj_own + proj_got.astype(F32)).astype(BF16)
    proj_part = proj_part.reshape(width, vision * local // width)
    image_stage = first_swaps(kv_part, proj_part)
    self_one, self_two = last_sum(last_parts(*self_stage), half_width)
    image_stage = second_swaps(*image_stage)
    kv_grad, proj_grad = last_sum(last_parts(*image_stage), width)
    proj_grad = proj_grad.reshape(vision // devices, local)

    lines = 23 + hidden // local
    packed_shape = (-(-lines // 8) * 8, local)
    small, small_out = run(
        partial(pack_kernel, local, hidden),
        1,
        [core_scalar],
        [whole(feed_sums), whole(up_sums), whole(self_sums), whole(image_sums)],
        [(packed_shape, F32, whole_spec(packed_shape))] * 2,
        [],
        0,
        [up_grad, kv_part, proj_part],
    )
    small = small + mate(small_out)
    for bit in range(bits):
        small = small + partner_bits(small, 1 << bit)
    common = small[:18].reshape(3, 3, width)
    bias_grad = small[18:22].reshape(2, 2, local)
    up_bias_grad = small[22 : 22 + hidden // local].reshape(hidden)
    proj_bias_grad = small[22 + hidden // local]

    ready = [self_one[:, at * local : (at + 1) * local] for at in range(3)]
    out_self, out_cross, query_cross = [
        self_two[:, at * local : (at + 1) * local] for at in range(3)
    ]
    in_grad = jnp.stack(
        ready + [query_cross, kv_grad[:, :local], kv_grad[:, local:]]
    ).reshape(2, 3, width // devices, local)
    out_grad = jnp.stack([out_self.T, out_cross.T])

    def tokens_out(value, after, after_place):
        shape = (length // 2, slots, width)
        own, away = run(
            partial(halve_kernel, slots, length),
            1,
            [core_scalar, where],
            [whole(value)],
            [(shape, BF16, whole_spec(shape))] * 2,
            [slabs(all_tokens)],
            0,
            after,
        )
        shape = (length // 2, rows, width)
        (out,) = run(
            place_kernel,
            1,
            [],
            [whole(own), whole(mate(away)), whole(place)],
            [(shape, BF16, whole_spec(shape))],
            [],
            0,
            after_place,
        )
        return jnp.transpose(out, (1, 0, 2))

    return (
        tokens_out(merged_in, [self_part], [kv_part]),
        tokens_out(text_in, [kv_away], [kv_part, proj_part]),
        jnp.transpose(patch_grad, (1, 0, 2)),
        proj_grad,
        proj_bias_grad,
        in_grad,
        bias_grad,
        out_grad,
        common[0],
        common[1],
        common[2],
        up_grad,
        up_bias_grad,
        down_grad.T,
    )


def solution(mesh):
    placed = (
        P("dp", None, None),
        P("dp", None, None),
        P("dp"),
        P("dp", None),
        P("dp", None),
        P("dp"),
        P("dp", None, None),
        P(),
        P(),
        P(None, None, None, "mp"),
        P(None, None, "mp"),
        P(None, "mp", None),
        P(),
        P(),
        P(),
        P(None, "mp"),
        P("mp"),
        P("mp", None),
    )
    return jax.shard_map(
        body,
        mesh=mesh,
        in_specs=placed,
        out_specs=(
            P("dp", "mp", None),
            P("dp", "mp", None),
            P(("dp", "mp"), None, None),
            P("dp", "mp"),
            P("mp"),
            P(None, None, "dp", "mp"),
            P(None, None, "mp"),
            P(None, "mp", "dp"),
            P(),
            P(),
            P(),
            P("dp", "mp"),
            P("mp"),
            P("mp", "dp"),
        ),
        check_vma=False,
    )
```

```python
import math
from functools import partial

import jax
import jax.numpy as jnp
from jax import lax
from jax.experimental import pallas as pl
from jax.experimental.pallas import tpu as pltpu
from jax.sharding import PartitionSpec as P

HEAD_DIM = 64
GRID = 12
EPS = 1e-12
NEG = -1e30
SCALE = HEAD_DIM ** (-0.5)

F32 = jnp.float32
BF16 = jnp.bfloat16

GROUP = 4 * HEAD_DIM
BAND = 32
BANDS = 5
LANES = 128
TILE = 256
PAIRED = 4
VMEM_LIMIT = 58 << 20


def dot(left, right):
    return lax.dot_general(left, right, (((1,), (0,)), ((), ())), preferred_element_type=F32)


def dot_nt(left, right):
    return lax.dot_general(left, right, (((1,), (1,)), ((), ())), preferred_element_type=F32)


def dot_tn(left, right):
    return lax.dot_general(left, right, (((0,), (0,)), ((), ())), preferred_element_type=F32)


def rows_spec(block, offset):
    rank = len(block)
    return pl.BlockSpec(block, lambda s, *_: (s + offset,) + (0,) * (rank - 1))


def whole_spec(shape):
    rank = len(shape)
    return pl.BlockSpec(shape, lambda s, *_: (0,) * rank, pipeline_mode=pl.Buffered(1))


ANY = pl.BlockSpec(memory_space=pl.ANY)


def run(body, steps, scalars, ins, outs, scratch, flops, after=()):
    ns, ni, no = len(scalars), len(ins), len(outs)

    def kernel(*refs):
        rest = refs[ns + ni + len(after) :]
        body(refs[:ns], refs[ns : ns + ni], rest[:no], rest[no:])

    moved = sum(math.prod(a.shape) * a.dtype.itemsize for a, _ in ins)
    ins = list(ins) + [(array, ANY) for array in after]
    moved += sum(math.prod(shape) * jnp.dtype(dtype).itemsize for shape, dtype, _ in outs)
    return pl.pallas_call(
        kernel,
        grid_spec=pltpu.PrefetchScalarGridSpec(
            num_scalar_prefetch=ns,
            grid=(steps,),
            in_specs=[spec for _, spec in ins],
            out_specs=[spec for _, _, spec in outs],
            scratch_shapes=scratch,
        ),
        out_shape=[jax.ShapeDtypeStruct(shape, dtype) for shape, dtype, _ in outs],
        compiler_params=pltpu.CompilerParams(
            dimension_semantics=("arbitrary",), vmem_limit_bytes=VMEM_LIMIT
        ),
        cost_estimate=pl.CostEstimate(flops=flops, bytes_accessed=moved, transcendentals=0),
    )(*scalars, *[array for array, _ in ins])


class Loads:
    def __init__(self, steps, sems, pairs):
        self.steps = steps
        self.copies = [
            pltpu.make_async_copy(source, target, sems.at[at])
            for at, (source, target) in enumerate(pairs)
        ]

    def first(self, action):
        if self.steps == 1:
            action()
        else:
            pl.when(pl.program_id(0) == 0)(action)

    def start(self):
        self.first(lambda: [copy.start() for copy in self.copies] and None)

    def wait(self, *which):
        self.first(lambda: [self.copies[at].wait() for at in which] and None)


def side_by_side(own, mate, target, width):
    return [(own, target.at[:, pl.ds(0, width)]), (mate, target.at[:, pl.ds(width, width)])]


def one_above(own, mate, target, height):
    return [(own, target.at[pl.ds(0, height)]), (mate, target.at[pl.ds(height, height)])]


def moments(z):
    center = z - jnp.mean(z, axis=-1, keepdims=True)
    rstd = lax.rsqrt(jnp.mean(center * center, axis=-1, keepdims=True) + EPS)
    return center * rstd, rstd


def norm_grad(unit, rstd, gain, grad):
    inner = grad * gain
    return rstd * (
        inner
        - jnp.mean(inner, axis=-1, keepdims=True)
        - unit * jnp.mean(inner * unit, axis=-1, keepdims=True)
    )


def fold(block):
    return jnp.sum(block.reshape(block.shape[0] // 8, 8, block.shape[1]), axis=0)


def gelu(u):
    bell = jnp.exp2(u * u * (-0.5 / math.log(2.0)))
    t = 1.0 / (1.0 + (0.3275911 * 0.5**0.5) * jnp.abs(u))
    poly = t * (
        0.5 * 0.254829592
        + t
        * (
            0.5 * -0.284496736
            + t * (0.5 * 1.421413741 + t * (0.5 * -1.453152027 + t * (0.5 * 1.061405429)))
        )
    )
    tail = poly * bell
    phi = jnp.where(u >= 0.0, 1.0 - tail, tail)
    return u * phi, phi + u * (bell * (1.0 / math.sqrt(2.0 * math.pi)))


def spread_heads(block, lane_head):
    parts = [jnp.where(lane_head == h, block, 0.0) for h in range(GROUP // HEAD_DIM)]
    return jnp.concatenate(parts, axis=0).astype(BF16)


def gather_heads(block, lane_head, tokens):
    total = jnp.where(lane_head == 0, block[0:tokens], 0.0)
    for h in range(1, GROUP // HEAD_DIM):
        total = jnp.where(lane_head == h, block[h * tokens : (h + 1) * tokens], total)
    return total


def lane_heads():
    return lax.broadcasted_iota(jnp.int32, (1, GROUP), 1) // HEAD_DIM


def attend(items):
    scores = [dot_nt(qm, kb) for qm, kb, vb, keep in items]
    weights = []
    for score, (qm, kb, vb, keep) in zip(scores, items):
        score = jnp.where(keep, score, NEG)
        top = jnp.max(score, axis=1, keepdims=True)
        weight = jnp.exp(score - top)
        weight = weight * (1.0 / jnp.sum(weight, axis=1, keepdims=True))
        weights.append(weight.astype(BF16))
    return [dot(weight, vb) for weight, (qm, kb, vb, keep) in zip(weights, items)]


def attend_grad(items):
    scores = [dot_nt(kb, qm) for qm, kb, vb, dom, keep in items]
    grads = [dot_nt(vb, dom) for qm, kb, vb, dom, keep in items]
    middle = []
    for score, grad, (qm, kb, vb, dom, keep) in zip(scores, grads, items):
        score = jnp.where(keep, score, NEG)
        top = jnp.max(score, axis=0, keepdims=True)
        weight = jnp.exp(score - top)
        weight = weight * (1.0 / jnp.sum(weight, axis=0, keepdims=True))
        inner = jnp.sum(weight * grad, axis=0, keepdims=True)
        grad_score = weight * (grad - inner)
        middle.append(
            (weight.astype(BF16), grad_score.astype(BF16), jnp.transpose(grad_score).astype(BF16))
        )
    results = []
    for (weight, grad_score, turned), (qm, kb, vb, dom, keep) in zip(middle, items):
        results.append((dot(turned, kb), dot(grad_score, qm), dot(weight, dom)))
    return results


def box_keep(corners, slot, shape, axis):
    index = lax.broadcasted_iota(jnp.int32, shape, axis) - 1
    grid_row = (index * 2731) >> 15
    grid_col = index - grid_row * GRID
    inside = (grid_col >= corners[slot * 4]) & (grid_col < corners[slot * 4 + 1])
    inside = inside & (grid_row >= corners[slot * 4 + 2]) & (grid_row < corners[slot * 4 + 3])
    return (inside & (index >= 0)) | (index < 0)


def band_loop(total, body, part=None):
    @pl.loop(0, total // (BAND * BANDS))
    def _(step):
        sums = []
        for band in range(BANDS):
            start = pl.multiple_of(step * (BAND * BANDS) + band * BAND, BAND)
            folded = body(pl.ds(start, BAND))
            if folded is not None:
                sums.append(folded)
        for terms in zip(*sums):
            at = terms[0][0]
            part[at] += sum(value for _, value in terms[1:]) + terms[0][1]


def by_columns(left, weight, finish, transposed=False):
    count = weight.shape[0] if transposed else weight.shape[1]
    for start in range(0, count, GROUP):
        cols = slice(start, start + GROUP)
        value = dot_nt(left, weight[cols, :]) if transposed else dot(left, weight[:, cols])
        finish(cols, value)


def both_halves(own, mate, at):
    return jnp.concatenate([own[at[0], at[1] : at[1] + 1], mate[at[0], at[1] : at[1] + 1]], axis=1)


def row_pairs(source, where, first, count, length, finish):
    for at in range(0, count, 2):
        both = [source[where[first + at + n]].astype(F32) for n in range(2)]
        finish(slice(at * length, (at + 2) * length), jnp.concatenate(both, axis=0))


def split_lanes(target, rows, start, value):
    for lane in range(0, value.shape[1], LANES):
        target[(start + lane) // LANES, rows, :] = value[:, lane : lane + LANES]


def join_lanes(source, rows):
    return jnp.concatenate([source[lane, rows, :] for lane in range(source.shape[0])], axis=1)


def fetch_kernel(count, scalars, ins, outs, scratch):
    (source,) = scalars
    (sems,) = scratch
    copies = [
        pltpu.make_async_copy(table.at[source[at]], out.at[at], sems.at[which * count + at])
        for which, (table, out) in enumerate(zip(ins, outs))
        for at in range(count)
    ]
    for copy in copies:
        copy.start()
    for copy in copies:
        copy.wait()


def project_kernel(images, own_images, patch_pad, patch_count, local, scalars, ins, outs, scratch):
    (core,) = scalars
    patches, proj_weight, proj_bias, ain, ain_mate, bias_own, bias_mate = ins
    proj, keys, values = outs
    taken, raw, w1, w2, sems, weight_sems = scratch
    loads = Loads(
        1,
        weight_sems,
        side_by_side(ain.at[1, 1], ain_mate.at[1, 1], w1, local)
        + side_by_side(ain.at[1, 2], ain_mate.at[1, 2], w2, local),
    )
    parts, span = taken.shape[0], taken.shape[1]
    arrivals = Loads(
        1, sems, [(patches.at[pl.ds(n * span, span)], taken.at[n]) for n in range(parts)]
    )
    arrivals.start()
    loads.start()
    rows = span * images
    width = raw.shape[0] * LANES
    for n in range(parts):
        arrivals.wait(n)
        flat = taken[n].reshape(rows, taken.shape[3])
        for start in range(0, width, GROUP):
            cols = slice(start, start + GROUP)
            split_lanes(
                raw,
                slice(n * rows, (n + 1) * rows),
                start,
                dot(flat, proj_weight[:, cols]) + proj_bias[:, cols],
            )
    loads.wait(0, 1, 2, 3)
    bias = both_halves(bias_own, bias_mate, (1, 1))
    first = core[0] * own_images
    rest = jnp.zeros((patch_pad - patch_count, width), F32)

    @pl.loop(0, images // 2)
    def _(step):
        both = []
        for at in range(2):
            which = lax.rem(step * 2 + at + first, images)
            own = jnp.concatenate(
                [
                    raw[lane, pl.ds(which, patch_count, stride=images), :]
                    for lane in range(raw.shape[0])
                ],
                axis=1,
            )
            both.append(jnp.concatenate([own, rest], axis=0))
        low = jnp.concatenate(both, axis=0).astype(BF16)
        pair = pl.ds(step * 2, 2)

        @pl.when(step < own_images // 2)
        def _():
            proj[pair] = low.reshape(2, patch_pad, width)

        for start in range(0, width, GROUP):
            cols = slice(start, start + GROUP)
            keys[pair, :, cols] = (
                dot(low, w1[:, cols]).astype(BF16).reshape(2, patch_pad, GROUP)
            )
            values[pair, :, cols] = (
                (dot(low, w2[:, cols]) + bias[:, cols]).astype(BF16).reshape(2, patch_pad, GROUP)
            )


def self_kernel(steps, rows, local, length, scalars, ins, outs, scratch):
    lens, where = scalars
    x_in, ain, ain_mate, aout, aout_mate, bias_own, bias_mate, out_bias, gain, shift = ins
    x_out, unit_one, q_out, k_out, v_out, att_own, att_mate, low_out, cross_q, rstd_one = outs
    wq, wk, wv, wo, wc, qs, ks, vs, acc, low, sems = scratch
    total = rows * length
    loads = Loads(
        steps,
        sems,
        side_by_side(ain.at[0, 0], ain_mate.at[0, 0], wq, local)
        + side_by_side(ain.at[0, 1], ain_mate.at[0, 1], wk, local)
        + side_by_side(ain.at[0, 2], ain_mate.at[0, 2], wv, local)
        + one_above(aout.at[0], aout_mate.at[0], wo, local)
        + side_by_side(ain.at[1, 0], ain_mate.at[1, 0], wc, local),
    )
    loads.start()
    bias_q = both_halves(bias_own, bias_mate, (0, 0))
    bias_v = both_halves(bias_own, bias_mate, (0, 1))
    bias_c = both_halves(bias_own, bias_mate, (1, 0))

    def put(at, both):
        x_out[at] = both.astype(BF16)

    base = pl.program_id(0) * rows
    row_pairs(x_in, where, base, rows, length, put)
    xb = x_out[...]

    def keep_q(cols, value):
        value = (value + bias_q[:, cols]).astype(BF16)
        q_out[:, cols] = value
        qs[:, cols] = value.astype(F32) * SCALE

    def keep_k(cols, value):
        value = value.astype(BF16)
        k_out[:, cols] = value
        ks[:, cols] = value.astype(F32)

    def keep_v(cols, value):
        value = (value + bias_v[:, cols]).astype(BF16)
        v_out[:, cols] = value
        vs[:, cols] = value.astype(F32)

    loads.wait(0, 1)
    by_columns(xb, wq, keep_q)
    loads.wait(2, 3)
    by_columns(xb, wk, keep_k)
    loads.wait(4, 5)
    by_columns(xb, wv, keep_v)
    lane_head = lane_heads()
    key_index = lax.broadcasted_iota(jnp.int32, (1, length), 1)

    @pl.loop(0, rows // PAIRED)
    def _(step):
        items, places = [], []
        for row in range(PAIRED):
            row = step * PAIRED + row
            at = pl.ds(pl.multiple_of(row * length, 8), length)
            keep = key_index < lens[base + row]
            for g in range(qs.shape[1] // GROUP):
                lanes = slice(g * GROUP, (g + 1) * GROUP)
                items.append(
                    (
                        spread_heads(qs[at, lanes], lane_head),
                        ks[at, lanes].astype(BF16),
                        vs[at, lanes].astype(BF16),
                        keep,
                    )
                )
                places.append((at, lanes))
        for (at, lanes), result in zip(places, attend(items)):
            acc[at, lanes] = gather_heads(result, lane_head, length)

    def cast(at):
        value = acc[at].astype(BF16)
        low[at] = value
        att_own[at] = value[:, :local]
        att_mate[at] = value[:, local:]

    def to_acc(cols, value):
        acc[:, cols] = value

    band_loop(total, cast)
    loads.wait(6, 7)
    by_columns(low[...], wo, to_acc)

    def norm(at):
        z = x_out[at].astype(F32) + acc[at] + out_bias[0:1]
        unit, rstd = moments(z)
        unit_one[at] = unit
        rstd_one[at] = rstd
        h = (unit * gain[0:1] + shift[0:1]).astype(BF16)
        low[at] = h
        low_out[at] = h

    band_loop(total, norm)
    loads.wait(8, 9)

    def to_query(cols, value):
        cross_q[:, cols] = (value + bias_c[:, cols]).astype(BF16)

    by_columns(low[...], wc, to_query)


def cross_kernel(rows, length, scalars, ins, outs, scratch):
    image, corners = scalars
    queries, keys, values = ins
    (att,) = outs
    qs, acc = scratch
    patch_pad = keys.shape[1]
    lane_head = lane_heads()
    base = pl.program_id(0) * rows

    def spread(at):
        qs[at] = queries[at].astype(F32) * SCALE

    band_loop(rows * length, spread)

    @pl.loop(0, rows // PAIRED)
    def _(step):
        items, places = [], []
        for row in range(PAIRED):
            row = step * PAIRED + row
            at = pl.ds(pl.multiple_of(row * length, 8), length)
            which = image[base + row]
            keep = box_keep(corners, base + row, (1, patch_pad), 1)
            for g in range(qs.shape[1] // GROUP):
                lanes = slice(g * GROUP, (g + 1) * GROUP)
                items.append(
                    (
                        spread_heads(qs[at, lanes], lane_head),
                        keys[which, :, lanes],
                        values[which, :, lanes],
                        keep,
                    )
                )
                places.append((at, lanes))
        for (at, lanes), result in zip(places, attend(items)):
            acc[at, lanes] = gather_heads(result, lane_head, length)

    def cast(at):
        att[at] = acc[at].astype(BF16)

    band_loop(rows * length, cast)


def feed_kernel(steps, rows, local, hidden, length, scalars, ins, outs, scratch):
    (where,) = scalars
    grad_in, att, unit_one, aout, aout_mate, up, up_mate, down, down_mate = ins[:9]
    out_bias, gains, shift, up_bias, up_bias_mate = ins[9:]
    merged, low_out, df_out, do_out, dz_out, a_own, a_mate = outs[:7]
    g_out, du_out = outs[7:9], outs[9:11]
    da_out, sums, up_sums = outs[11:]
    wo, wu, wd, acc, kept, unit_two, rstd_two, low, upstream, even, odd, slope = scratch[:12]
    part, up_part, sems = scratch[12:]
    tiles = hidden // TILE
    total = rows * length
    loads = Loads(
        steps,
        sems,
        one_above(aout.at[1], aout_mate.at[1], wo, local)
        + [
            (source.at[:, pl.ds(t * TILE, TILE)], wu.at[t, :, pl.ds(half * TILE, TILE)])
            for t in range(tiles)
            for half, source in enumerate((up, up_mate))
        ]
        + [
            (source.at[pl.ds(t * TILE, TILE)], wd.at[t, pl.ds(half * TILE, TILE)])
            for t in range(tiles)
            for half, source in enumerate((down, down_mate))
        ],
    )
    loads.start()
    part[...] = jnp.zeros_like(part)

    def put(at, both):
        upstream[at] = both.astype(BF16)

    base = pl.program_id(0) * rows
    row_pairs(grad_in, where, base, rows, length, put)

    def to_acc(cols, value):
        acc[:, cols] = value

    a_own[...] = att[:, :local]
    a_mate[...] = att[:, local:]
    loads.wait(0, 1)
    by_columns(att[...], wo, to_acc)

    def norm_two(at):
        h_one = unit_one[at] * gains[0:1] + shift[0:1]
        unit, rstd = moments(h_one + acc[at] + out_bias[1:2])
        h_two = unit * gains[1:2] + shift[1:2]
        unit_two[at] = unit
        rstd_two[at] = rstd
        kept[at] = h_two
        h_low = h_two.astype(BF16)
        low[at] = h_low
        low_out[at] = h_low

    band_loop(total, norm_two)
    acc[...] = jnp.zeros_like(acc)
    loads.wait(*range(2, 2 + 4 * tiles))
    biases = (up_bias, up_bias_mate)

    def activate(units, t):
        cols = pl.ds(pl.multiple_of(t * TILE, TILE), TILE)
        for half in range(2):
            lanes = slice(half * TILE, (half + 1) * TILE)
            bias = biases[half][:, cols]
            for start in range(0, total, BAND):
                at = slice(start, start + BAND)
                active, sloped = gelu(units[at, lanes] + bias)
                g_out[half][at, cols] = active.astype(BF16)
                slope[t, at, lanes] = sloped

    def add_down(t):
        cols = pl.ds(pl.multiple_of(t * TILE, TILE), TILE)
        both = jnp.concatenate([g_out[0][:, cols], g_out[1][:, cols]], axis=1)
        acc[...] += dot(both, wd[t])

    even[...] = dot(low[...], wu[0])

    @pl.loop(0, tiles // 2)
    def _(step):
        first = 2 * step
        odd[...] = dot(low[...], wu[first + 1])
        activate(even, first)
        add_down(first)
        even[...] = dot(low[...], wu[jnp.minimum(first + 2, tiles - 1)])
        activate(odd, first + 1)
        add_down(first + 1)

    def norm_three(at):
        unit, rstd = moments(kept[at] + acc[at] + out_bias[2:3])
        gain = gains[2:3]
        unit_three = unit * gain + shift[2:3]
        grad = upstream[at].astype(F32)
        dz = norm_grad(unit, rstd, gain, grad)
        kept[at] = dz
        acc[at] = unit_three
        dz_low = dz.astype(BF16)
        low[at] = dz_low
        df_out[at] = dz_low
        return (
            (0, fold(dz_low.astype(F32))),
            (1, fold(grad * unit)),
            (2, fold(grad)),
        )

    band_loop(total, norm_three, part)

    for row in range(rows):
        merged[where[base + row]] = acc[row * length : (row + 1) * length].astype(BF16)
    acc[...] = jnp.zeros_like(acc)

    @pl.loop(0, tiles)
    def _(t):
        cols = pl.ds(pl.multiple_of(t * TILE, TILE), TILE)
        grads = dot_nt(low[...], wd[t])
        for half in range(2):
            lanes = slice(half * TILE, (half + 1) * TILE)
            folded = 0.0
            for start in range(0, total, BAND):
                at = slice(start, start + BAND)
                du = (grads[at, lanes] * slope[t, at, lanes]).astype(BF16)
                du_out[half][at, cols] = du
                folded = folded + fold(du.astype(F32))
            up_part[half, :, cols] = folded
        both = jnp.concatenate([du_out[0][:, cols], du_out[1][:, cols]], axis=1)
        acc[...] += dot_nt(both, wu[t])

    def norm_two_back(at):
        grad = kept[at] + acc[at]
        unit = unit_two[at]
        dz = norm_grad(unit, rstd_two[at], gains[1:2], grad)
        dz_out[at] = dz
        dz_low = dz.astype(BF16)
        low[at] = dz_low
        do_out[at] = dz_low
        return (
            (3, fold(dz_low.astype(F32))),
            (4, fold(grad * unit)),
            (5, fold(grad)),
        )

    band_loop(total, norm_two_back, part)

    def to_grad(cols, value):
        da_out[:, cols] = value.astype(BF16)

    by_columns(low[...], wo, to_grad, transposed=True)
    for at in range(8):
        sums[0, at : at + 1] = jnp.sum(part[at], axis=0, keepdims=True)
    for half in range(2):
        up_sums[0, half : half + 1] = jnp.sum(up_part[half], axis=0, keepdims=True)


def cross_grad_kernel(steps, rows, length, scalars, ins, outs, scratch):
    image, corners = scalars
    queries, grads, keys, values = ins
    own, mate, grad_queries = outs
    qs, gs, acc, dk, dv = scratch
    patch_pad = keys.shape[1]

    def clear():
        @pl.loop(0, dk.shape[0])
        def _(at):
            dk[at] = jnp.zeros(dk.shape[1:], F32)
            dv[at] = jnp.zeros(dv.shape[1:], F32)

    pl.when(pl.program_id(0) == 0)(clear)

    def spread(at):
        qs[at] = queries[at].astype(F32) * SCALE
        gs[at] = grads[at].astype(F32)

    band_loop(rows * length, spread)
    lane_head = lane_heads()
    base = pl.program_id(0) * rows

    @pl.loop(0, rows // PAIRED)
    def _(step):
        items, places = [], []
        for row in range(PAIRED):
            row = step * PAIRED + row
            at = pl.ds(pl.multiple_of(row * length, 8), length)
            which = image[base + row]
            keep = box_keep(corners, base + row, (patch_pad, 1), 0)
            for g in range(qs.shape[1] // GROUP):
                lanes = slice(g * GROUP, (g + 1) * GROUP)
                items.append(
                    (
                        spread_heads(qs[at, lanes], lane_head),
                        keys[which, :, lanes],
                        values[which, :, lanes],
                        spread_heads(gs[at, lanes], lane_head),
                        keep,
                    )
                )
                places.append((at, which, lanes))
        for (at, which, lanes), (grad_q, grad_k, grad_v) in zip(places, attend_grad(items)):
            acc[at, lanes] = gather_heads(grad_q, lane_head, length) * SCALE
            dk[which, :, lanes] += grad_k
            dv[which, :, lanes] += grad_v

    def cast(at):
        grad_queries[at] = acc[at].astype(BF16)

    band_loop(rows * length, cast)

    @pl.when(pl.program_id(0) == steps - 1)
    def _():
        half = own.shape[1]

        @pl.loop(0, half)
        def _(at):
            own[0, at] = dk[at].astype(BF16)
            own[1, at] = dv[at].astype(BF16)
            mate[0, at] = dk[half + at].astype(BF16)
            mate[1, at] = dv[half + at].astype(BF16)


def image_kernel(images, patch_count, local, scalars, ins, outs, scratch):
    (core,) = scalars
    piece, piece_mate, patches, proj_weight, ain, ain_mate = ins
    kv_own, kv_mate, patch_grad, weight_grad, sums = outs
    narrow, wide, taken, w1, w2, part, sems, weight_sems = scratch
    parts, span = taken.shape[0], taken.shape[1]
    loads = Loads(
        1,
        weight_sems,
        side_by_side(ain.at[1, 1], ain_mate.at[1, 1], w1, local)
        + side_by_side(ain.at[1, 2], ain_mate.at[1, 2], w2, local),
    )
    arrivals = Loads(
        1, sems, [(patches.at[pl.ds(n * span, span)], taken.at[n]) for n in range(parts)]
    )
    loads.start()
    arrivals.start()
    part[...] = jnp.zeros_like(part)
    own_images, patch_pad = piece.shape[1], piece.shape[2]
    width = w1.shape[0]

    slab = 80

    @pl.loop(0, wide.shape[1] // slab)
    def _(step):
        at = pl.ds(pl.multiple_of(step * slab, slab), slab)
        for lane in range(wide.shape[0]):
            wide[lane, at] = jnp.zeros((slab, LANES), F32)

    loads.wait(0, 1, 2, 3)
    first = core[0] * own_images

    @pl.loop(0, own_images // 2)
    def _(step):
        pair = pl.ds(step * 2, 2)
        halves = []
        for half in (slice(0, local), slice(local, width)):
            swapped = slice(width - half.stop, width - half.start)
            both = piece[:, pair, :, half].astype(F32) + piece_mate[:, pair, :, swapped].astype(F32)
            both = both.astype(BF16)
            halves.append([both[at].reshape(2 * patch_pad, local) for at in range(2)])
        (dk_own, dv_own), (dk_mate, dv_mate) = halves
        rows = pl.ds(pl.multiple_of(step * 2 * patch_pad, 2 * patch_pad), 2 * patch_pad)
        kv_own[rows, :local] = dk_own
        kv_own[rows, local:] = dv_own
        kv_mate[rows, :local] = dk_mate
        kv_mate[rows, local:] = dv_mate
        dk = jnp.concatenate([dk_own, dk_mate], axis=1)
        dv = jnp.concatenate([dv_own, dv_mate], axis=1)
        part[1] += fold(dv.astype(F32))
        for start in range(0, width, GROUP):
            cols = slice(start, start + GROUP)
            grad = dot_nt(dk, w1[cols, :]) + dot_nt(dv, w2[cols, :])
            grad = grad.astype(BF16).astype(F32)
            part[0, :, cols] += fold(grad)
            for at in range(2):
                one = grad[at * patch_pad : at * patch_pad + patch_count]
                which = step * 2 + at
                spot = pl.ds(which, patch_count, stride=own_images)
                split_lanes(narrow, spot, start, one)
                split_lanes(wide, pl.ds(which + first, patch_count, stride=images), start, one)

    for n in range(parts):
        arrivals.wait(n)
        few = slice(n * span * own_images, (n + 1) * span * own_images)
        some = join_lanes(narrow, few).astype(BF16)
        for start in range(0, proj_weight.shape[0], GROUP):
            cols = slice(start, start + GROUP)
            back = dot_nt(some, proj_weight[cols, :]).astype(BF16)
            patch_grad[n * span : (n + 1) * span, :, cols] = back.reshape(span, own_images, GROUP)
        flat = taken[n].reshape(span * images, taken.shape[3])
        grad = join_lanes(wide, slice(n * span * images, (n + 1) * span * images)).astype(BF16)
        product = dot_tn(flat, grad)
        if n == 0:
            weight_grad[...] = product
        else:
            weight_grad[...] += product
    for at in range(2):
        sums[at : at + 1] = jnp.sum(part[at], axis=0, keepdims=True)


def self_grad_kernel(steps, rows, local, length, scalars, ins, outs, scratch):
    lens, where = scalars
    dq2, unit_one, rstd_one, dz_two, q_in, k_in, v_in, ain, ain_mate, aout, aout_mate, gain = ins
    text_grad, do_out, dq2_own, dq2_mate, qkv_own, qkv_mate, sums = outs
    wc, wo, wq, wk, wv, acc, kept, low, low_k, low_v, qs, ks, vs, part, sems = scratch
    total = rows * length
    loads = Loads(
        steps,
        sems,
        side_by_side(ain.at[1, 0], ain_mate.at[1, 0], wc, local)
        + one_above(aout.at[0], aout_mate.at[0], wo, local)
        + side_by_side(ain.at[0, 0], ain_mate.at[0, 0], wq, local)
        + side_by_side(ain.at[0, 1], ain_mate.at[0, 1], wk, local)
        + side_by_side(ain.at[0, 2], ain_mate.at[0, 2], wv, local),
    )
    loads.start()
    part[...] = jnp.zeros_like(part)

    def to_acc(cols, value):
        acc[:, cols] = value

    loads.wait(0, 1)
    by_columns(dq2[...], wc, to_acc, transposed=True)

    def norm_back(at):
        unit = unit_one[at]
        grad = dz_two[at] + acc[at]
        dz = norm_grad(unit, rstd_one[at], gain[0:1], grad)
        kept[at] = dz
        dz_low = dz.astype(BF16)
        low[at] = dz_low
        do_out[at] = dz_low
        qs[at] = q_in[at].astype(F32) * SCALE
        ks[at] = k_in[at].astype(F32)
        vs[at] = v_in[at].astype(F32)
        query = dq2[at]
        dq2_own[at] = query[:, :local]
        dq2_mate[at] = query[:, local:]
        return (
            (0, fold(dz_low.astype(F32))),
            (1, fold(grad * unit)),
            (2, fold(grad)),
            (5, fold(query.astype(F32))),
        )

    band_loop(total, norm_back, part)
    loads.wait(2, 3)
    by_columns(low[...], wo, to_acc, transposed=True)
    lane_head = lane_heads()
    key_index = lax.broadcasted_iota(jnp.int32, (length, 1), 0)
    base = pl.program_id(0) * rows

    @pl.loop(0, rows // PAIRED)
    def _(step):
        items, places = [], []
        for row in range(PAIRED):
            row = step * PAIRED + row
            at = pl.ds(pl.multiple_of(row * length, 8), length)
            keep = key_index < lens[base + row]
            for g in range(qs.shape[1] // GROUP):
                lanes = slice(g * GROUP, (g + 1) * GROUP)
                items.append(
                    (
                        spread_heads(qs[at, lanes], lane_head),
                        ks[at, lanes].astype(BF16),
                        vs[at, lanes].astype(BF16),
                        spread_heads(acc[at, lanes], lane_head),
                        keep,
                    )
                )
                places.append((at, lanes))
        for (at, lanes), (grad_q, grad_k, grad_v) in zip(places, attend_grad(items)):
            qs[at, lanes] = gather_heads(grad_q, lane_head, length) * SCALE
            ks[at, lanes] = grad_k
            vs[at, lanes] = grad_v

    def cast(at):
        sums = []
        for slot, (source, target) in enumerate(((qs, low), (ks, low_k), (vs, low_v))):
            value = source[at].astype(BF16)
            target[at] = value
            qkv_own[at, slot * local : (slot + 1) * local] = value[:, :local]
            qkv_mate[at, slot * local : (slot + 1) * local] = value[:, local:]
            if slot != 1:
                sums.append((3 + slot // 2, fold(value.astype(F32))))
        return sums

    band_loop(total, cast, part)
    loads.wait(4, 5, 6, 7, 8, 9)
    for start in range(0, kept.shape[1], GROUP):
        cols = slice(start, start + GROUP)
        acc[:, cols] = (
            kept[:, cols]
            + dot_nt(low[...], wq[cols, :])
            + dot_nt(low_k[...], wk[cols, :])
            + dot_nt(low_v[...], wv[cols, :])
        )

    for row in range(rows):
        text_grad[where[base + row]] = acc[row * length : (row + 1) * length].astype(BF16)
    for at in range(8):
        sums[0, at : at + 1] = jnp.sum(part[at], axis=0, keepdims=True)


def pack_kernel(local, hidden, scalars, ins, outs, scratch):
    (core,) = scalars
    feed, up, self_, image = ins
    feed_sum = jnp.sum(feed[...], axis=0)
    self_sum = jnp.sum(self_[...], axis=0)
    up_sum = jnp.sum(up[...], axis=0)
    common = [(0, 0), (1, 3), (1, 0), (0, 1), (1, 4), (1, 1), (0, 2), (1, 5), (1, 2)]
    even = core[0] == 0
    for out, mine in zip(outs, (True, False)):
        out[...] = jnp.zeros_like(out)
        at = 0
        for which, row in common:
            source = feed_sum if which else self_sum
            for half in range(2):
                out[at : at + 1] = source[row : row + 1, half * local : (half + 1) * local]
                at += 1
        lanes = slice(0, local) if mine else slice(local, 2 * local)
        for row in (3, 4, 5):
            out[at : at + 1] = self_sum[row : row + 1, lanes]
            at += 1
        out[at : at + 1] = image[1:2, lanes]
        at += 1
        half = 0 if mine else 1
        for start in range(0, hidden, local):
            out[at : at + 1] = up_sum[half : half + 1, start : start + local]
            at += 1
        low, high = image[0:1, :local], image[0:1, local:]
        out[at : at + 1] = jnp.where(even == mine, low, high)


def halve_kernel(rows, length, scalars, ins, outs, scratch):
    core, where = scalars
    (tall,) = scratch

    def put(at, both):
        split_lanes(tall, at, 0, both)

    row_pairs(ins[0], where, 0, rows, length, put)
    half = length // 2
    for out, first in zip(outs, (core[0] * half, (1 - core[0]) * half)):
        for token in range(half):
            out[token] = join_lanes(
                tall, pl.ds(first + token, rows, stride=length)
            ).astype(BF16)


def place_kernel(scalars, ins, outs, scratch):
    own, mate, place = ins
    (out,) = outs
    count, slots = out.shape[1], own.shape[1]
    index = lax.broadcasted_iota(jnp.int32, (count, slots), 1)
    from_own = jnp.where(place[...] == index, 1.0, 0.0).astype(BF16)
    from_mate = jnp.where(place[...] == index + slots, 1.0, 0.0).astype(BF16)
    for token in range(out.shape[0]):
        out[token] = (dot(from_own, own[token]) + dot(from_mate, mate[token])).astype(BF16)


def body(
    text,
    cotangent,
    lengths,
    box_corners,
    box_counts,
    region_box,
    patches,
    proj_weight,
    proj_bias,
    attention_in,
    attention_bias,
    attention_out,
    output_bias,
    norm_gain,
    norm_bias,
    up_weight,
    up_bias,
    down_weight,
):
    rows, length, width = text.shape
    images, patch_count, vision = patches.shape
    local = attention_in.shape[-1]
    hidden = up_weight.shape[-1]
    devices = lax.axis_size("dp")
    me, core = lax.axis_index("dp"), lax.axis_index("mp")
    pair = -(-rows // devices)
    each, odd = pair // 2, pair % 2
    deep = each + odd
    slots = devices * each + devices // 2 * odd
    patch_pad = -(-patch_count // 16) * 16
    own_images = images // 2
    step_rows = 12 if slots % 12 == 0 else 8
    steps = slots // step_rows
    tokens = step_rows * length
    all_tokens = slots * length
    full = slots * 2 == rows
    core_scalar = core.astype(jnp.int32).reshape(1)

    def mate(value):
        return lax.ppermute(value, "mp", [(0, 1), (1, 0)])

    def tie(*values):
        return lax.optimization_barrier(values)

    def exchange(value):
        return lax.all_to_all(value, "dp", split_axis=0, concat_axis=0, tiled=True)

    ain_mate = mate(attention_in)
    bias_mate = mate(attention_bias)
    aout_mate = mate(attention_out)
    up_bias_own = up_bias.reshape(1, hidden)
    up_bias_mate = mate(up_bias_own)
    up_mate = mate(up_weight)
    down_mate = mate(down_weight)

    number = jnp.arange(rows, dtype=jnp.int32)
    target = region_box // rows
    earlier = (target[:, None] == target[None, :]) & (number[None, :] < number[:, None])
    nth = jnp.sum(earlier.astype(jnp.int32), axis=1)
    even_part = nth < 2 * each
    row_core = jnp.where(even_part, nth // max(each, 1), (target ^ me) & 1)
    depth = jnp.where(even_part, nth % max(each, 1), each)
    spot = jnp.arange(devices * deep, dtype=jnp.int32)
    hit = (spot[:, None] == (target * deep + depth)[None, :]) & (row_core == core)[None, :]
    source = jnp.sum(jnp.where(hit, number[None, :], 0), axis=1)
    slot = jnp.where(even_part, target * each + depth, devices * each + (target >> 1))
    place = jnp.where(row_core == core, slot, slot + slots)[:, None]
    order = jnp.arange(slots, dtype=jnp.int32)
    late = order - devices * each
    where = jnp.where(
        late < 0,
        order // max(each, 1) * deep + order % max(each, 1),
        (2 * late + ((me & 1) ^ core)) * deep + each,
    )
    meta = jnp.concatenate(
        [(region_box % rows)[:, None], lengths[:, None], box_corners], axis=1
    )
    meta_out = jnp.sum(jnp.where(hit[:, :, None], meta[None], 0), axis=1)
    if not full:
        empty = jnp.array([0, 1, 0, 1, 0, 1], jnp.int32)
        meta_out = jnp.where(jnp.any(hit, axis=1)[:, None], meta_out, empty[None])
    arrived = exchange(meta_out)[where]
    ends = jnp.cumsum(box_counts[0])
    image = jnp.sum((ends[None, :] <= arrived[:, 0:1]).astype(jnp.int32), axis=1)
    image = (image + own_images * core) % images
    lens = arrived[:, 1]
    corners = arrived[:, 2:].reshape(-1)

    block_shape = (devices * deep, length, width)
    if full:
        x_out, upstream_out = run(
            partial(fetch_kernel, devices * deep),
            1,
            [source],
            [(text, ANY), (cotangent, ANY)],
            [(block_shape, BF16, whole_spec(block_shape))] * 2,
            [pltpu.SemaphoreType.DMA((2 * devices * deep,))],
            0,
        )
    else:
        valid = jnp.any(hit, axis=1)[:, None, None]
        x_out = jnp.where(valid, text[source], 0)
        upstream_out = jnp.where(valid, cotangent[source], 0)
    x_in = exchange(x_out)

    patches, aout_mate, image, corners, lens = tie(patches, aout_mate, image, corners, lens)
    by_patch = jnp.transpose(patches, (1, 0, 2))
    parts = next(n for n in (5, 4, 3, 2, 1) if patch_count % n == 0)
    weight_scratch = pltpu.VMEM((width, width), BF16)

    def slabs(count):
        return pltpu.VMEM((width // LANES, count, LANES), F32)

    patch_scratch = pltpu.VMEM((parts, patch_count // parts, images, vision), BF16)
    image_shape = (images, patch_pad, width)
    proj, keys, values = run(
        partial(project_kernel, images, own_images, patch_pad, patch_count, local),
        1,
        [core_scalar],
        [
            (by_patch, ANY),
            (proj_weight, whole_spec(proj_weight.shape)),
            (proj_bias.reshape(1, width), whole_spec((1, width))),
            (attention_in, ANY),
            (ain_mate, ANY),
            (attention_bias, whole_spec(attention_bias.shape)),
            (bias_mate, whole_spec(bias_mate.shape)),
        ],
        [((own_images,) + image_shape[1:], BF16, whole_spec((own_images,) + image_shape[1:]))]
        + [(image_shape, BF16, whole_spec(image_shape))] * 2,
        [
            patch_scratch,
            slabs(patch_count * images),
            weight_scratch,
            weight_scratch,
            pltpu.SemaphoreType.DMA((parts,)),
            pltpu.SemaphoreType.DMA((4,)),
        ],
        2 * images * patch_pad * width * (vision + 2 * width),
    )

    upstream_out, proj, keys, values = tie(upstream_out, proj, keys, values)
    upstream_in = exchange(upstream_out)

    def token_in(value):
        return (value, rows_spec((tokens, value.shape[1]), 0))

    def token_out(cols, dtype):
        return ((all_tokens, cols), dtype, rows_spec((tokens, cols), 0))

    block_out = (block_shape, BF16, whole_spec(block_shape))

    def f32_tokens(cols):
        return pltpu.VMEM((tokens, cols), F32)

    def low_tokens(cols):
        return pltpu.VMEM((tokens, cols), BF16)

    def whole(value):
        return (value, whole_spec(value.shape))

    attention_flops = 4 * 4 * all_tokens * width * 64

    x, unit_one, q_self, k_self, v_self, att_own, att_mate, self_low, queries, rstd_one = run(
        partial(self_kernel, steps, step_rows, local, length),
        steps,
        [lens, where],
        [
            whole(x_in),
            (attention_in, ANY),
            (ain_mate, ANY),
            (attention_out, ANY),
            (aout_mate, ANY),
            whole(attention_bias),
            whole(bias_mate),
            whole(output_bias),
            whole(norm_gain),
            whole(norm_bias),
        ],
        [token_out(width, BF16), token_out(width, F32)]
        + [token_out(width, BF16)] * 3
        + [token_out(local, BF16)] * 2
        + [token_out(width, BF16)] * 2
        + [token_out(1, F32)],
        [weight_scratch] * 5
        + [f32_tokens(width)] * 4
        + [low_tokens(width), pltpu.SemaphoreType.DMA((10,))],
        2 * all_tokens * width * width * 5 + attention_flops,
    )

    (attended,) = run(
        partial(cross_kernel, step_rows, length),
        steps,
        [image, corners],
        [token_in(queries), whole(keys), whole(values)],
        [token_out(width, BF16)],
        [f32_tokens(width)] * 2,
        attention_flops * 4,
    )

    result = run(
        partial(feed_kernel, steps, step_rows, local, hidden, length),
        steps,
        [where],
        [
            whole(upstream_in),
            token_in(attended),
            token_in(unit_one),
            (attention_out, ANY),
            (aout_mate, ANY),
            (up_weight, ANY),
            (up_mate, ANY),
            (down_weight, ANY),
            (down_mate, ANY),
            whole(output_bias),
            whole(norm_gain),
            whole(norm_bias),
            whole(up_bias_own),
            whole(up_bias_mate),
        ],
        [block_out]
        + [token_out(width, BF16)] * 3
        + [token_out(width, F32)]
        + [token_out(local, BF16)] * 2
        + [token_out(hidden, BF16)] * 4
        + [
            token_out(width, BF16),
            ((steps, 8, width), F32, rows_spec((1, 8, width), 0)),
            ((steps, 2, hidden), F32, rows_spec((1, 2, hidden), 0)),
        ],
        [weight_scratch]
        + [
            pltpu.VMEM((hidden // TILE, width, 2 * TILE), BF16),
            pltpu.VMEM((hidden // TILE, 2 * TILE, width), BF16),
        ]
        + [f32_tokens(width)] * 3
        + [f32_tokens(1), low_tokens(width), low_tokens(width)]
        + [f32_tokens(2 * TILE)] * 2
        + [pltpu.VMEM((hidden // TILE, tokens, 2 * TILE), F32)]
        + [pltpu.VMEM((8, 8, width), F32), pltpu.VMEM((2, 8, hidden), F32)]
        + [pltpu.SemaphoreType.DMA((2 + 4 * hidden // TILE,))],
        2 * all_tokens * width * (2 * width + 8 * hidden),
    )
    merged_out, cross_low, grad_ffn, grad_cross, dz_two, a_own, a_mate = result[:7]
    g_own, g_mate, du_own, du_mate, grad_att, feed_sums, up_sums = result[7:]

    bits = devices.bit_length() - 1

    def partner_bits(value, mask):
        return lax.ppermute(value, "dp", [(d, d ^ mask) for d in range(devices)])

    def opened(value):
        return value.reshape((2,) * bits + (value.shape[0] // devices, value.shape[1]))

    def swap(value, axis, bit):
        mine = (me >> bit) & 1
        away = lax.dynamic_index_in_dim(value, 1 - mine, axis, keepdims=False)
        stay = lax.dynamic_index_in_dim(value, mine, axis, keepdims=False)
        return stay, partner_bits(away, 1 << bit)

    def first_swaps(by_x, by_y):
        return swap(opened(by_x), bits - 1, 0) + swap(opened(by_y), bits - 2, 1)

    def second_swaps(stay_x, got_x, stay_y, got_y):
        return swap(add(stay_x, got_x), bits - 2, 1) + swap(add(stay_y, got_y), bits - 2, 0)

    def add(stay, got):
        return (stay.astype(F32) + got.astype(F32)).astype(BF16)

    def last_parts(stay_x, got_x, stay_y, got_y):
        parts = [add(stay_x, got_x), add(stay_y, got_y)]
        return jnp.concatenate(
            [part.reshape((devices // 4,) + part.shape[-2:]) for part in parts], axis=2
        )

    def last_sum(both, first_width):
        groups = [[low + 4 * n for n in range(devices // 4)] for low in range(4)]
        both = lax.all_to_all(
            both, "dp", split_axis=0, concat_axis=0, axis_index_groups=groups, tiled=True
        )
        total = jnp.sum(both.astype(F32), axis=0)
        return total[:, :first_width], total[:, first_width:]

    def low_tn(left, right):
        return dot_tn(left, right).astype(BF16)

    merged_in = exchange(merged_out)
    up_away, down_away = low_tn(cross_low, du_mate), low_tn(grad_ffn, g_mate)
    grad_att, queries, up_away, down_away = tie(grad_att, queries, up_away, down_away)
    up_got, down_got = mate(up_away), mate(down_away)

    half_shape = (2, own_images, patch_pad, width)
    image_acc = pltpu.VMEM(image_shape, F32)
    piece, piece_out, grad_queries = run(
        partial(cross_grad_kernel, steps, step_rows, length),
        steps,
        [image, corners],
        [token_in(queries), token_in(grad_att), whole(keys), whole(values)],
        [(half_shape, BF16, whole_spec(half_shape))] * 2 + [token_out(width, BF16)],
        [f32_tokens(width)] * 3 + [image_acc] * 2,
        attention_flops * 12,
    )
    piece_mate = mate(piece_out)

    up_part = (dot_tn(cross_low, du_own) + up_got.astype(F32)).astype(BF16)
    down_part = (dot_tn(grad_ffn, g_own) + down_got.astype(F32)).astype(BF16)
    grad_queries, up_part, down_part = tie(grad_queries, up_part, down_part)
    feed_stage = first_swaps(up_part, down_part)

    result = run(
        partial(self_grad_kernel, steps, step_rows, local, length),
        steps,
        [lens, where],
        [
            token_in(grad_queries),
            token_in(unit_one),
            token_in(rstd_one),
            token_in(dz_two),
            token_in(q_self),
            token_in(k_self),
            token_in(v_self),
            (attention_in, ANY),
            (ain_mate, ANY),
            (attention_out, ANY),
            (aout_mate, ANY),
            whole(norm_gain),
        ],
        [block_out]
        + [token_out(width, BF16)]
        + [token_out(local, BF16)] * 2
        + [token_out(3 * local, BF16)] * 2
        + [((steps, 8, width), F32, rows_spec((1, 8, width), 0))],
        [weight_scratch] * 5
        + [f32_tokens(width)] * 2
        + [low_tokens(width)] * 3
        + [f32_tokens(width)] * 3
        + [pltpu.VMEM((8, 8, width), F32), pltpu.SemaphoreType.DMA((10,))],
        2 * all_tokens * width * width * 5 + attention_flops * 2,
    )
    text_out, grad_self, dq_own, dq_mate, qkv_own, qkv_mate, self_sums = result
    text_in = exchange(text_out)

    self_away = jnp.concatenate(
        [
            low_tn(x, qkv_mate),
            low_tn(grad_self, att_mate),
            low_tn(grad_cross, a_mate),
            low_tn(self_low, dq_mate),
        ],
        axis=1,
    )
    self_got = mate(self_away)
    feed_stage = tie(self_away, *feed_stage)[1:]
    feed_stage = second_swaps(*feed_stage)
    self_own = jnp.concatenate(
        [
            dot_tn(x, qkv_own),
            dot_tn(grad_self, att_own),
            dot_tn(grad_cross, a_own),
            dot_tn(self_low, dq_own),
        ],
        axis=1,
    )
    self_part = (self_own + self_got.astype(F32)).astype(BF16)
    half_width = self_part.shape[1] // 2
    self_stage = first_swaps(self_part[:, :half_width], self_part[:, half_width:])
    feed_parts = last_parts(*feed_stage)
    piece, piece_mate, self_part, feed_parts = tie(piece, piece_mate, self_part, feed_parts)

    flat_images = own_images * patch_pad
    patch_grad_shape = (patch_count, own_images, vision)
    kv_own, kv_mate, patch_grad, proj_weight_sum, image_sums = run(
        partial(image_kernel, images, patch_count, local),
        1,
        [core_scalar],
        [
            whole(piece),
            whole(piece_mate),
            (by_patch, ANY),
            whole(proj_weight),
            (attention_in, ANY),
            (ain_mate, ANY),
        ],
        [
            ((flat_images, width), BF16, whole_spec((flat_images, width))),
            ((flat_images, width), BF16, whole_spec((flat_images, width))),
            (patch_grad_shape, BF16, whole_spec(patch_grad_shape)),
            ((vision, width), F32, whole_spec((vision, width))),
            ((8, width), F32, whole_spec((8, width))),
        ],
        [
            slabs(patch_count * own_images),
            slabs(patch_count * images),
            patch_scratch,
            weight_scratch,
            weight_scratch,
            pltpu.VMEM((2, 8, width), F32),
            pltpu.SemaphoreType.DMA((parts,)),
            pltpu.SemaphoreType.DMA((4,)),
        ],
        2 * flat_images * width * (2 * width + 2 * vision),
    )

    up_grad, down_grad = last_sum(feed_parts, hidden)
    self_stage = second_swaps(*self_stage)
    kv_low = proj.reshape(flat_images, width)
    kv_away = low_tn(kv_low, kv_mate)
    kv_got = mate(kv_away)
    proj_away = lax.dynamic_slice_in_dim(proj_weight_sum, (1 - core) * local, local, 1)
    proj_got = mate(proj_away.astype(BF16))
    kv_part = (dot_tn(kv_low, kv_own) + kv_got.astype(F32)).astype(BF16)
    proj_own = lax.dynamic_slice_in_dim(proj_weight_sum, core * local, local, 1)
    proj_part = (proj_own + proj_got.astype(F32)).astype(BF16)
    proj_part = proj_part.reshape(width, vision * local // width)
    image_stage = first_swaps(kv_part, proj_part)
    self_one, self_two = last_sum(last_parts(*self_stage), half_width)
    image_stage = second_swaps(*image_stage)
    kv_grad, proj_grad = last_sum(last_parts(*image_stage), width)
    proj_grad = proj_grad.reshape(vision // devices, local)

    lines = 23 + hidden // local
    packed_shape = (-(-lines // 8) * 8, local)
    small, small_out = run(
        partial(pack_kernel, local, hidden),
        1,
        [core_scalar],
        [whole(feed_sums), whole(up_sums), whole(self_sums), whole(image_sums)],
        [(packed_shape, F32, whole_spec(packed_shape))] * 2,
        [],
        0,
        [up_grad, kv_part, proj_part],
    )
    small = small + mate(small_out)
    for bit in range(bits):
        small = small + partner_bits(small, 1 << bit)
    common = small[:18].reshape(3, 3, width)
    bias_grad = small[18:22].reshape(2, 2, local)
    up_bias_grad = small[22 : 22 + hidden // local].reshape(hidden)
    proj_bias_grad = small[22 + hidden // local]

    ready = [self_one[:, at * local : (at + 1) * local] for at in range(3)]
    out_self, out_cross, query_cross = [
        self_two[:, at * local : (at + 1) * local] for at in range(3)
    ]
    in_grad = jnp.stack(
        ready + [query_cross, kv_grad[:, :local], kv_grad[:, local:]]
    ).reshape(2, 3, width // devices, local)
    out_grad = jnp.stack([out_self.T, out_cross.T])

    def tokens_out(value, after, after_place):
        shape = (length // 2, slots, width)
        own, away = run(
            partial(halve_kernel, slots, length),
            1,
            [core_scalar, where],
            [whole(value)],
            [(shape, BF16, whole_spec(shape))] * 2,
            [slabs(all_tokens)],
            0,
            after,
        )
        shape = (length // 2, rows, width)
        (out,) = run(
            place_kernel,
            1,
            [],
            [whole(own), whole(mate(away)), whole(place)],
            [(shape, BF16, whole_spec(shape))],
            [],
            0,
            after_place,
        )
        return jnp.transpose(out, (1, 0, 2))

    return (
        tokens_out(merged_in, [self_part], [kv_part]),
        tokens_out(text_in, [kv_away], [kv_part, proj_part]),
        jnp.transpose(patch_grad, (1, 0, 2)),
        proj_grad,
        proj_bias_grad,
        in_grad,
        bias_grad,
        out_grad,
        common[0],
        common[1],
        common[2],
        up_grad,
        up_bias_grad,
        down_grad.T,
    )


def solution(mesh):
    placed = (
        P("dp", None, None),
        P("dp", None, None),
        P("dp"),
        P("dp", None),
        P("dp", None),
        P("dp"),
        P("dp", None, None),
        P(),
        P(),
        P(None, None, None, "mp"),
        P(None, None, "mp"),
        P(None, "mp", None),
        P(),
        P(),
        P(),
        P(None, "mp"),
        P("mp"),
        P("mp", None),
    )
    return jax.shard_map(
        body,
        mesh=mesh,
        in_specs=placed,
        out_specs=(
            P("dp", "mp", None),
            P("dp", "mp", None),
            P(("dp", "mp"), None, None),
            P("dp", "mp"),
            P("mp"),
            P(None, None, "dp", "mp"),
            P(None, None, "mp"),
            P(None, "mp", "dp"),
            P(),
            P(),
            P(),
            P("dp", "mp"),
            P("mp"),
            P("mp", "dp"),
        ),
        check_vma=False,
    )
```

```python
import math
from functools import partial

import jax
import jax.numpy as jnp
from jax import lax
from jax.experimental import pallas as pl
from jax.experimental.pallas import tpu as pltpu
from jax.sharding import PartitionSpec as P

HEAD_DIM = 64
GRID = 12
EPS = 1e-12
NEG = -1e30
SCALE = HEAD_DIM ** (-0.5)

F32 = jnp.float32
BF16 = jnp.bfloat16

GROUP = 4 * HEAD_DIM
BAND = 32
BANDS = 5
LANES = 128
TILE = 256
PAIRED = 4
VMEM_LIMIT = 58 << 20


def dot(left, right):
    return lax.dot_general(left, right, (((1,), (0,)), ((), ())), preferred_element_type=F32)


def dot_nt(left, right):
    return lax.dot_general(left, right, (((1,), (1,)), ((), ())), preferred_element_type=F32)


def dot_tn(left, right):
    return lax.dot_general(left, right, (((0,), (0,)), ((), ())), preferred_element_type=F32)


def rows_spec(block, offset):
    rank = len(block)
    return pl.BlockSpec(block, lambda s, *_: (s + offset,) + (0,) * (rank - 1))


def whole_spec(shape):
    rank = len(shape)
    return pl.BlockSpec(shape, lambda s, *_: (0,) * rank, pipeline_mode=pl.Buffered(1))


ANY = pl.BlockSpec(memory_space=pl.ANY)


def run(body, steps, scalars, ins, outs, scratch, flops, after=()):
    ns, ni, no = len(scalars), len(ins), len(outs)

    def kernel(*refs):
        rest = refs[ns + ni + len(after) :]
        body(refs[:ns], refs[ns : ns + ni], rest[:no], rest[no:])

    moved = sum(math.prod(a.shape) * a.dtype.itemsize for a, _ in ins)
    ins = list(ins) + [(array, ANY) for array in after]
    moved += sum(math.prod(shape) * jnp.dtype(dtype).itemsize for shape, dtype, _ in outs)
    return pl.pallas_call(
        kernel,
        grid_spec=pltpu.PrefetchScalarGridSpec(
            num_scalar_prefetch=ns,
            grid=(steps,),
            in_specs=[spec for _, spec in ins],
            out_specs=[spec for _, _, spec in outs],
            scratch_shapes=scratch,
        ),
        out_shape=[jax.ShapeDtypeStruct(shape, dtype) for shape, dtype, _ in outs],
        compiler_params=pltpu.CompilerParams(
            dimension_semantics=("arbitrary",), vmem_limit_bytes=VMEM_LIMIT
        ),
        cost_estimate=pl.CostEstimate(
            flops=flops, bytes_accessed=moved, transcendentals=0
        ),
    )(*scalars, *[array for array, _ in ins])


class Loads:
    def __init__(self, steps, sems, pairs):
        self.steps = steps
        self.copies = [
            pltpu.make_async_copy(source, target, sems.at[at])
            for at, (source, target) in enumerate(pairs)
        ]

    def first(self, action):
        if self.steps == 1:
            action()
        else:
            pl.when(pl.program_id(0) == 0)(action)

    def start(self):
        self.first(lambda: [copy.start() for copy in self.copies] and None)

    def wait(self, *which):
        self.first(lambda: [self.copies[at].wait() for at in which] and None)


def side_by_side(own, mate, target, width):
    return [(own, target.at[:, pl.ds(0, width)]), (mate, target.at[:, pl.ds(width, width)])]


def one_above(own, mate, target, height):
    return [(own, target.at[pl.ds(0, height)]), (mate, target.at[pl.ds(height, height)])]


def moments(z):
    center = z - jnp.mean(z, axis=-1, keepdims=True)
    rstd = lax.rsqrt(jnp.mean(center * center, axis=-1, keepdims=True) + EPS)
    return center * rstd, rstd


def norm_grad(unit, rstd, gain, grad):
    inner = grad * gain
    return rstd * (
        inner
        - jnp.mean(inner, axis=-1, keepdims=True)
        - unit * jnp.mean(inner * unit, axis=-1, keepdims=True)
    )


def fold(block):
    return jnp.sum(block.reshape(block.shape[0] // 8, 8, block.shape[1]), axis=0)


def gelu(u):
    bell = jnp.exp2(u * u * (-0.5 / math.log(2.0)))
    t = 1.0 / (1.0 + (0.3275911 * 0.5**0.5) * jnp.abs(u))
    poly = t * (
        0.5 * 0.254829592
        + t
        * (
            0.5 * -0.284496736
            + t * (0.5 * 1.421413741 + t * (0.5 * -1.453152027 + t * (0.5 * 1.061405429)))
        )
    )
    tail = poly * bell
    phi = jnp.where(u >= 0.0, 1.0 - tail, tail)
    return u * phi, phi + u * (bell * (1.0 / math.sqrt(2.0 * math.pi)))


def spread_heads(block, lane_head):
    parts = [jnp.where(lane_head == h, block, 0.0) for h in range(GROUP // HEAD_DIM)]
    return jnp.concatenate(parts, axis=0).astype(BF16)


def gather_heads(block, lane_head, tokens):
    total = jnp.where(lane_head == 0, block[0:tokens], 0.0)
    for h in range(1, GROUP // HEAD_DIM):
        total = jnp.where(lane_head == h, block[h * tokens : (h + 1) * tokens], total)
    return total


def lane_heads():
    return lax.broadcasted_iota(jnp.int32, (1, GROUP), 1) // HEAD_DIM


def attend(items):
    scores = [dot_nt(qm, kb) for qm, kb, vb, keep in items]
    weights = []
    for score, (qm, kb, vb, keep) in zip(scores, items):
        score = jnp.where(keep, score, NEG)
        top = jnp.max(score, axis=1, keepdims=True)
        weight = jnp.exp(score - top)
        weight = weight * (1.0 / jnp.sum(weight, axis=1, keepdims=True))
        weights.append(weight.astype(BF16))
    return [dot(weight, vb) for weight, (qm, kb, vb, keep) in zip(weights, items)]


def attend_grad(items):
    scores = [dot_nt(kb, qm) for qm, kb, vb, dom, keep in items]
    grads = [dot_nt(vb, dom) for qm, kb, vb, dom, keep in items]
    middle = []
    for score, grad, (qm, kb, vb, dom, keep) in zip(scores, grads, items):
        score = jnp.where(keep, score, NEG)
        top = jnp.max(score, axis=0, keepdims=True)
        weight = jnp.exp(score - top)
        weight = weight * (1.0 / jnp.sum(weight, axis=0, keepdims=True))
        inner = jnp.sum(weight * grad, axis=0, keepdims=True)
        grad_score = weight * (grad - inner)
        middle.append(
            (weight.astype(BF16), grad_score.astype(BF16), jnp.transpose(grad_score).astype(BF16))
        )
    results = []
    for (weight, grad_score, turned), (qm, kb, vb, dom, keep) in zip(middle, items):
        results.append((dot(turned, kb), dot(grad_score, qm), dot(weight, dom)))
    return results


def box_keep(corners, slot, shape, axis):
    index = lax.broadcasted_iota(jnp.int32, shape, axis) - 1
    grid_row = (index * 2731) >> 15
    grid_col = index - grid_row * GRID
    inside = (grid_col >= corners[slot * 4]) & (grid_col < corners[slot * 4 + 1])
    inside = inside & (grid_row >= corners[slot * 4 + 2]) & (grid_row < corners[slot * 4 + 3])
    return (inside & (index >= 0)) | (index < 0)


def band_loop(total, body, part=None):
    @pl.loop(0, total // (BAND * BANDS))
    def _(step):
        sums = []
        for band in range(BANDS):
            start = pl.multiple_of(step * (BAND * BANDS) + band * BAND, BAND)
            folded = body(pl.ds(start, BAND))
            if folded is not None:
                sums.append(folded)
        for terms in zip(*sums):
            at = terms[0][0]
            part[at] += sum(value for _, value in terms[1:]) + terms[0][1]


def by_columns(left, weight, finish, transposed=False):
    count = weight.shape[0] if transposed else weight.shape[1]
    for start in range(0, count, GROUP):
        cols = slice(start, start + GROUP)
        value = dot_nt(left, weight[cols, :]) if transposed else dot(left, weight[:, cols])
        finish(cols, value)


def both_halves(own, mate, at):
    return jnp.concatenate([own[at[0], at[1] : at[1] + 1], mate[at[0], at[1] : at[1] + 1]], axis=1)


def row_pairs(source, where, first, count, length, finish):
    for at in range(0, count, 2):
        both = [source[where[first + at + n]].astype(F32) for n in range(2)]
        finish(slice(at * length, (at + 2) * length), jnp.concatenate(both, axis=0))


def split_lanes(target, rows, start, value):
    for lane in range(0, value.shape[1], LANES):
        target[(start + lane) // LANES, rows, :] = value[:, lane : lane + LANES]


def join_lanes(source, rows):
    return jnp.concatenate([source[lane, rows, :] for lane in range(source.shape[0])], axis=1)


def fetch_kernel(count, scalars, ins, outs, scratch):
    (source,) = scalars
    (sems,) = scratch
    copies = [
        pltpu.make_async_copy(table.at[source[at]], out.at[at], sems.at[which * count + at])
        for which, (table, out) in enumerate(zip(ins, outs))
        for at in range(count)
    ]
    for copy in copies:
        copy.start()
    for copy in copies:
        copy.wait()


def project_kernel(images, own_images, patch_pad, patch_count, local, scalars, ins, outs, scratch):
    (core,) = scalars
    patches, proj_weight, proj_bias, ain, ain_mate, bias_own, bias_mate = ins
    proj, keys, values = outs
    taken, raw, w1, w2, sems, weight_sems = scratch
    loads = Loads(
        1,
        weight_sems,
        side_by_side(ain.at[1, 1], ain_mate.at[1, 1], w1, local)
        + side_by_side(ain.at[1, 2], ain_mate.at[1, 2], w2, local),
    )
    parts, span = taken.shape[0], taken.shape[1]
    arrivals = Loads(
        1, sems, [(patches.at[pl.ds(n * span, span)], taken.at[n]) for n in range(parts)]
    )
    arrivals.start()
    loads.start()
    rows = span * images
    width = raw.shape[0] * LANES
    for n in range(parts):
        arrivals.wait(n)
        flat = taken[n].reshape(rows, taken.shape[3])
        for start in range(0, width, GROUP):
            cols = slice(start, start + GROUP)
            split_lanes(
                raw,
                slice(n * rows, (n + 1) * rows),
                start,
                dot(flat, proj_weight[:, cols]) + proj_bias[:, cols],
            )
    loads.wait(0, 1, 2, 3)
    bias = both_halves(bias_own, bias_mate, (1, 1))
    first = core[0] * own_images
    rest = jnp.zeros((patch_pad - patch_count, width), F32)

    group = 4

    @pl.loop(0, images // group)
    def _(step):
        both = []
        for at in range(group):
            which = lax.rem(step * group + at + first, images)
            own = jnp.concatenate(
                [
                    raw[lane, pl.ds(which, patch_count, stride=images), :]
                    for lane in range(raw.shape[0])
                ],
                axis=1,
            )
            both.append(jnp.concatenate([own, rest], axis=0))
        low = jnp.concatenate(both, axis=0).astype(BF16)
        some = pl.ds(step * group, group)

        @pl.when(step < own_images // group)
        def _():
            proj[some] = low.reshape(group, patch_pad, width)

        shape = (group, patch_pad, GROUP)
        for start in range(0, width, GROUP):
            cols = slice(start, start + GROUP)
            keys[some, :, cols] = dot(low, w1[:, cols]).astype(BF16).reshape(shape)
            values[some, :, cols] = (
                (dot(low, w2[:, cols]) + bias[:, cols]).astype(BF16).reshape(shape)
            )


def self_kernel(steps, rows, local, length, scalars, ins, outs, scratch):
    lens, where = scalars
    x_in, ain, ain_mate, aout, aout_mate, bias_own, bias_mate, out_bias, gain, shift = ins
    x_out, unit_one, q_out, k_out, v_out, att_own, att_mate, low_out, cross_q, rstd_one = outs
    wq, wk, wv, wo, wc, qs, ks, vs, acc, low, sems = scratch
    total = rows * length
    loads = Loads(
        steps,
        sems,
        side_by_side(ain.at[0, 0], ain_mate.at[0, 0], wq, local)
        + side_by_side(ain.at[0, 1], ain_mate.at[0, 1], wk, local)
        + side_by_side(ain.at[0, 2], ain_mate.at[0, 2], wv, local)
        + one_above(aout.at[0], aout_mate.at[0], wo, local)
        + side_by_side(ain.at[1, 0], ain_mate.at[1, 0], wc, local),
    )
    loads.start()
    bias_q = both_halves(bias_own, bias_mate, (0, 0))
    bias_v = both_halves(bias_own, bias_mate, (0, 1))
    bias_c = both_halves(bias_own, bias_mate, (1, 0))

    def put(at, both):
        x_out[at] = both.astype(BF16)

    base = pl.program_id(0) * rows
    row_pairs(x_in, where, base, rows, length, put)
    xb = x_out[...]

    def keep_q(cols, value):
        value = (value + bias_q[:, cols]).astype(BF16)
        q_out[:, cols] = value
        qs[:, cols] = value.astype(F32) * SCALE

    def keep_k(cols, value):
        value = value.astype(BF16)
        k_out[:, cols] = value
        ks[:, cols] = value.astype(F32)

    def keep_v(cols, value):
        value = (value + bias_v[:, cols]).astype(BF16)
        v_out[:, cols] = value
        vs[:, cols] = value.astype(F32)

    loads.wait(0, 1)
    by_columns(xb, wq, keep_q)
    loads.wait(2, 3)
    by_columns(xb, wk, keep_k)
    loads.wait(4, 5)
    by_columns(xb, wv, keep_v)
    lane_head = lane_heads()
    key_index = lax.broadcasted_iota(jnp.int32, (1, length), 1)

    @pl.loop(0, rows // PAIRED)
    def _(step):
        items, places = [], []
        for row in range(PAIRED):
            row = step * PAIRED + row
            at = pl.ds(pl.multiple_of(row * length, 8), length)
            keep = key_index < lens[base + row]
            for g in range(qs.shape[1] // GROUP):
                lanes = slice(g * GROUP, (g + 1) * GROUP)
                items.append(
                    (
                        spread_heads(qs[at, lanes], lane_head),
                        ks[at, lanes].astype(BF16),
                        vs[at, lanes].astype(BF16),
                        keep,
                    )
                )
                places.append((at, lanes))
        for (at, lanes), result in zip(places, attend(items)):
            acc[at, lanes] = gather_heads(result, lane_head, length)

    def cast(at):
        value = acc[at].astype(BF16)
        low[at] = value
        att_own[at] = value[:, :local]
        att_mate[at] = value[:, local:]

    def to_acc(cols, value):
        acc[:, cols] = value

    band_loop(total, cast)
    loads.wait(6, 7)
    by_columns(low[...], wo, to_acc)

    def norm(at):
        z = x_out[at].astype(F32) + acc[at] + out_bias[0:1]
        unit, rstd = moments(z)
        unit_one[at] = unit
        rstd_one[at] = rstd
        h = (unit * gain[0:1] + shift[0:1]).astype(BF16)
        low[at] = h
        low_out[at] = h

    band_loop(total, norm)
    loads.wait(8, 9)

    def to_query(cols, value):
        cross_q[:, cols] = (value + bias_c[:, cols]).astype(BF16)

    by_columns(low[...], wc, to_query)


def cross_kernel(rows, length, scalars, ins, outs, scratch):
    image, corners = scalars
    queries, keys, values = ins
    (att,) = outs
    qs, acc = scratch
    patch_pad = keys.shape[1]
    lane_head = lane_heads()
    base = pl.program_id(0) * rows

    def spread(at):
        qs[at] = queries[at].astype(F32) * SCALE

    band_loop(rows * length, spread)

    @pl.loop(0, rows // PAIRED)
    def _(step):
        items, places = [], []
        for row in range(PAIRED):
            row = step * PAIRED + row
            at = pl.ds(pl.multiple_of(row * length, 8), length)
            which = image[base + row]
            keep = box_keep(corners, base + row, (1, patch_pad), 1)
            for g in range(qs.shape[1] // GROUP):
                lanes = slice(g * GROUP, (g + 1) * GROUP)
                items.append(
                    (
                        spread_heads(qs[at, lanes], lane_head),
                        keys[which, :, lanes],
                        values[which, :, lanes],
                        keep,
                    )
                )
                places.append((at, lanes))
        for (at, lanes), result in zip(places, attend(items)):
            acc[at, lanes] = gather_heads(result, lane_head, length)

    def cast(at):
        att[at] = acc[at].astype(BF16)

    band_loop(rows * length, cast)


def feed_kernel(steps, rows, local, hidden, length, scalars, ins, outs, scratch):
    (where,) = scalars
    grad_in, att, unit_one, aout, aout_mate, up, up_mate, down, down_mate = ins[:9]
    out_bias, gains, shift, up_bias, up_bias_mate = ins[9:]
    merged, low_out, df_out, do_out, dz_out, a_own, a_mate = outs[:7]
    g_out, du_out = outs[7:9], outs[9:11]
    da_out, sums, up_sums = outs[11:]
    wo, wu, wd, acc, kept, unit_two, rstd_two, low, upstream, even, odd, slope = scratch[:12]
    part, up_part, sems = scratch[12:]
    tiles = hidden // TILE
    total = rows * length
    loads = Loads(
        steps,
        sems,
        one_above(aout.at[1], aout_mate.at[1], wo, local)
        + [
            (source.at[:, pl.ds(t * TILE, TILE)], wu.at[t, :, pl.ds(half * TILE, TILE)])
            for t in range(tiles)
            for half, source in enumerate((up, up_mate))
        ]
        + [
            (source.at[pl.ds(t * TILE, TILE)], wd.at[t, pl.ds(half * TILE, TILE)])
            for t in range(tiles)
            for half, source in enumerate((down, down_mate))
        ],
    )
    loads.start()
    part[...] = jnp.zeros_like(part)

    def put(at, both):
        upstream[at] = both.astype(BF16)

    base = pl.program_id(0) * rows
    row_pairs(grad_in, where, base, rows, length, put)

    def to_acc(cols, value):
        acc[:, cols] = value

    a_own[...] = att[:, :local]
    a_mate[...] = att[:, local:]
    loads.wait(0, 1)
    by_columns(att[...], wo, to_acc)

    def norm_two(at):
        h_one = unit_one[at] * gains[0:1] + shift[0:1]
        unit, rstd = moments(h_one + acc[at] + out_bias[1:2])
        h_two = unit * gains[1:2] + shift[1:2]
        unit_two[at] = unit
        rstd_two[at] = rstd
        kept[at] = h_two
        h_low = h_two.astype(BF16)
        low[at] = h_low
        low_out[at] = h_low

    band_loop(total, norm_two)
    acc[...] = jnp.zeros_like(acc)
    loads.wait(*range(2, 2 + 4 * tiles))
    biases = (up_bias, up_bias_mate)

    def activate(units, t):
        cols = slice(t * TILE, (t + 1) * TILE)
        for half in range(2):
            lanes = slice(half * TILE, (half + 1) * TILE)
            bias = biases[half][:, cols]
            for start in range(0, total, BAND):
                at = slice(start, start + BAND)
                active, sloped = gelu(units[at, lanes] + bias)
                g_out[half][at, cols] = active.astype(BF16)
                slope[t, at, lanes] = sloped

    def add_down(t):
        cols = slice(t * TILE, (t + 1) * TILE)
        both = jnp.concatenate([g_out[0][:, cols], g_out[1][:, cols]], axis=1)
        acc[...] += dot(both, wd[t])

    units = (even, odd)
    even[...] = dot(low[...], wu[0])
    for t in range(tiles):
        if t + 1 < tiles:
            units[(t + 1) % 2][...] = dot(low[...], wu[t + 1])
        activate(units[t % 2], t)
        add_down(t)

    def norm_three(at):
        unit, rstd = moments(kept[at] + acc[at] + out_bias[2:3])
        gain = gains[2:3]
        unit_three = unit * gain + shift[2:3]
        grad = upstream[at].astype(F32)
        dz = norm_grad(unit, rstd, gain, grad)
        kept[at] = dz
        acc[at] = unit_three
        dz_low = dz.astype(BF16)
        low[at] = dz_low
        df_out[at] = dz_low
        return (
            (0, fold(dz_low.astype(F32))),
            (1, fold(grad * unit)),
            (2, fold(grad)),
        )

    band_loop(total, norm_three, part)

    for row in range(rows):
        merged[where[base + row]] = acc[row * length : (row + 1) * length].astype(BF16)
    acc[...] = jnp.zeros_like(acc)

    for t in range(tiles):
        cols = slice(t * TILE, (t + 1) * TILE)
        grads = dot_nt(low[...], wd[t])
        for half in range(2):
            lanes = slice(half * TILE, (half + 1) * TILE)
            folded = 0.0
            for start in range(0, total, BAND):
                at = slice(start, start + BAND)
                du = (grads[at, lanes] * slope[t, at, lanes]).astype(BF16)
                du_out[half][at, cols] = du
                folded = folded + fold(du.astype(F32))
            up_part[half, :, cols] = folded
        both = jnp.concatenate([du_out[0][:, cols], du_out[1][:, cols]], axis=1)
        acc[...] += dot_nt(both, wu[t])

    def norm_two_back(at):
        grad = kept[at] + acc[at]
        unit = unit_two[at]
        dz = norm_grad(unit, rstd_two[at], gains[1:2], grad)
        dz_out[at] = dz
        dz_low = dz.astype(BF16)
        low[at] = dz_low
        do_out[at] = dz_low
        return (
            (3, fold(dz_low.astype(F32))),
            (4, fold(grad * unit)),
            (5, fold(grad)),
        )

    band_loop(total, norm_two_back, part)

    def to_grad(cols, value):
        da_out[:, cols] = value.astype(BF16)

    by_columns(low[...], wo, to_grad, transposed=True)
    for at in range(8):
        sums[0, at : at + 1] = jnp.sum(part[at], axis=0, keepdims=True)
    for half in range(2):
        up_sums[0, half : half + 1] = jnp.sum(up_part[half], axis=0, keepdims=True)


def cross_grad_kernel(steps, rows, length, scalars, ins, outs, scratch):
    image, corners = scalars
    queries, grads, keys, values = ins
    own, mate, grad_queries = outs
    qs, gs, acc, dk, dv = scratch
    patch_pad = keys.shape[1]

    def clear():
        @pl.loop(0, dk.shape[0])
        def _(at):
            dk[at] = jnp.zeros(dk.shape[1:], F32)
            dv[at] = jnp.zeros(dv.shape[1:], F32)

    pl.when(pl.program_id(0) == 0)(clear)

    def spread(at):
        qs[at] = queries[at].astype(F32) * SCALE
        gs[at] = grads[at].astype(F32)

    band_loop(rows * length, spread)
    lane_head = lane_heads()
    base = pl.program_id(0) * rows

    @pl.loop(0, rows // PAIRED)
    def _(step):
        items, places = [], []
        for row in range(PAIRED):
            row = step * PAIRED + row
            at = pl.ds(pl.multiple_of(row * length, 8), length)
            which = image[base + row]
            keep = box_keep(corners, base + row, (patch_pad, 1), 0)
            for g in range(qs.shape[1] // GROUP):
                lanes = slice(g * GROUP, (g + 1) * GROUP)
                items.append(
                    (
                        spread_heads(qs[at, lanes], lane_head),
                        keys[which, :, lanes],
                        values[which, :, lanes],
                        spread_heads(gs[at, lanes], lane_head),
                        keep,
                    )
                )
                places.append((at, which, lanes))
        for (at, which, lanes), (grad_q, grad_k, grad_v) in zip(places, attend_grad(items)):
            acc[at, lanes] = gather_heads(grad_q, lane_head, length) * SCALE
            dk[which, :, lanes] += grad_k
            dv[which, :, lanes] += grad_v

    def cast(at):
        grad_queries[at] = acc[at].astype(BF16)

    band_loop(rows * length, cast)

    @pl.when(pl.program_id(0) == steps - 1)
    def _():
        half = own.shape[1]

        @pl.loop(0, half)
        def _(at):
            own[0, at] = dk[at].astype(BF16)
            own[1, at] = dv[at].astype(BF16)
            mate[0, at] = dk[half + at].astype(BF16)
            mate[1, at] = dv[half + at].astype(BF16)


def image_kernel(images, patch_count, local, scalars, ins, outs, scratch):
    (core,) = scalars
    piece, piece_mate, patches, proj_weight, ain, ain_mate = ins
    kv_own, kv_mate, patch_grad, weight_grad, sums = outs
    narrow, wide, taken, w1, w2, part, sems, weight_sems = scratch
    parts, span = taken.shape[0], taken.shape[1]
    loads = Loads(
        1,
        weight_sems,
        side_by_side(ain.at[1, 1], ain_mate.at[1, 1], w1, local)
        + side_by_side(ain.at[1, 2], ain_mate.at[1, 2], w2, local),
    )
    arrivals = Loads(
        1, sems, [(patches.at[pl.ds(n * span, span)], taken.at[n]) for n in range(parts)]
    )
    loads.start()
    arrivals.start()
    part[...] = jnp.zeros_like(part)
    own_images, patch_pad = piece.shape[1], piece.shape[2]
    width = w1.shape[0]

    slab = 80

    @pl.loop(0, wide.shape[1] // slab)
    def _(step):
        at = pl.ds(pl.multiple_of(step * slab, slab), slab)
        for lane in range(wide.shape[0]):
            wide[lane, at] = jnp.zeros((slab, LANES), F32)

    loads.wait(0, 1, 2, 3)
    first = core[0] * own_images

    @pl.loop(0, own_images // 2)
    def _(step):
        pair = pl.ds(step * 2, 2)
        halves = []
        for half in (slice(0, local), slice(local, width)):
            swapped = slice(width - half.stop, width - half.start)
            both = piece[:, pair, :, half].astype(F32) + piece_mate[:, pair, :, swapped].astype(F32)
            both = both.astype(BF16)
            halves.append([both[at].reshape(2 * patch_pad, local) for at in range(2)])
        (dk_own, dv_own), (dk_mate, dv_mate) = halves
        rows = pl.ds(pl.multiple_of(step * 2 * patch_pad, 2 * patch_pad), 2 * patch_pad)
        kv_own[rows, :local] = dk_own
        kv_own[rows, local:] = dv_own
        kv_mate[rows, :local] = dk_mate
        kv_mate[rows, local:] = dv_mate
        dk = jnp.concatenate([dk_own, dk_mate], axis=1)
        dv = jnp.concatenate([dv_own, dv_mate], axis=1)
        part[1] += fold(dv.astype(F32))
        for start in range(0, width, GROUP):
            cols = slice(start, start + GROUP)
            grad = dot_nt(dk, w1[cols, :]) + dot_nt(dv, w2[cols, :])
            grad = grad.astype(BF16).astype(F32)
            part[0, :, cols] += fold(grad)
            for at in range(2):
                one = grad[at * patch_pad : at * patch_pad + patch_count]
                which = step * 2 + at
                spot = pl.ds(which, patch_count, stride=own_images)
                split_lanes(narrow, spot, start, one)
                split_lanes(wide, pl.ds(which + first, patch_count, stride=images), start, one)

    for n in range(parts):
        arrivals.wait(n)
        few = slice(n * span * own_images, (n + 1) * span * own_images)
        some = join_lanes(narrow, few).astype(BF16)
        for start in range(0, proj_weight.shape[0], GROUP):
            cols = slice(start, start + GROUP)
            back = dot_nt(some, proj_weight[cols, :]).astype(BF16)
            patch_grad[n * span : (n + 1) * span, :, cols] = back.reshape(span, own_images, GROUP)
        flat = taken[n].reshape(span * images, taken.shape[3])
        grad = join_lanes(wide, slice(n * span * images, (n + 1) * span * images)).astype(BF16)
        product = dot_tn(flat, grad)
        if n == 0:
            weight_grad[...] = product
        else:
            weight_grad[...] += product
    for at in range(2):
        sums[at : at + 1] = jnp.sum(part[at], axis=0, keepdims=True)


def self_grad_kernel(steps, rows, local, length, scalars, ins, outs, scratch):
    lens, where = scalars
    dq2, unit_one, rstd_one, dz_two, q_in, k_in, v_in, ain, ain_mate, aout, aout_mate, gain = ins
    text_grad, do_out, dq2_own, dq2_mate, qkv_own, qkv_mate, sums = outs
    wc, wo, wq, wk, wv, acc, kept, low, low_k, low_v, qs, ks, vs, part, sems = scratch
    total = rows * length
    loads = Loads(
        steps,
        sems,
        side_by_side(ain.at[1, 0], ain_mate.at[1, 0], wc, local)
        + one_above(aout.at[0], aout_mate.at[0], wo, local)
        + side_by_side(ain.at[0, 0], ain_mate.at[0, 0], wq, local)
        + side_by_side(ain.at[0, 1], ain_mate.at[0, 1], wk, local)
        + side_by_side(ain.at[0, 2], ain_mate.at[0, 2], wv, local),
    )
    loads.start()
    part[...] = jnp.zeros_like(part)

    def to_acc(cols, value):
        acc[:, cols] = value

    loads.wait(0, 1)
    by_columns(dq2[...], wc, to_acc, transposed=True)

    def norm_back(at):
        unit = unit_one[at]
        grad = dz_two[at] + acc[at]
        dz = norm_grad(unit, rstd_one[at], gain[0:1], grad)
        kept[at] = dz
        dz_low = dz.astype(BF16)
        low[at] = dz_low
        do_out[at] = dz_low
        qs[at] = q_in[at].astype(F32) * SCALE
        ks[at] = k_in[at].astype(F32)
        vs[at] = v_in[at].astype(F32)
        query = dq2[at]
        dq2_own[at] = query[:, :local]
        dq2_mate[at] = query[:, local:]
        return (
            (0, fold(dz_low.astype(F32))),
            (1, fold(grad * unit)),
            (2, fold(grad)),
            (5, fold(query.astype(F32))),
        )

    band_loop(total, norm_back, part)
    loads.wait(2, 3)
    by_columns(low[...], wo, to_acc, transposed=True)
    lane_head = lane_heads()
    key_index = lax.broadcasted_iota(jnp.int32, (length, 1), 0)
    base = pl.program_id(0) * rows

    @pl.loop(0, rows // PAIRED)
    def _(step):
        items, places = [], []
        for row in range(PAIRED):
            row = step * PAIRED + row
            at = pl.ds(pl.multiple_of(row * length, 8), length)
            keep = key_index < lens[base + row]
            for g in range(qs.shape[1] // GROUP):
                lanes = slice(g * GROUP, (g + 1) * GROUP)
                items.append(
                    (
                        spread_heads(qs[at, lanes], lane_head),
                        ks[at, lanes].astype(BF16),
                        vs[at, lanes].astype(BF16),
                        spread_heads(acc[at, lanes], lane_head),
                        keep,
                    )
                )
                places.append((at, lanes))
        for (at, lanes), (grad_q, grad_k, grad_v) in zip(places, attend_grad(items)):
            qs[at, lanes] = gather_heads(grad_q, lane_head, length) * SCALE
            ks[at, lanes] = grad_k
            vs[at, lanes] = grad_v

    def cast(at):
        sums = []
        for slot, (source, target) in enumerate(((qs, low), (ks, low_k), (vs, low_v))):
            value = source[at].astype(BF16)
            target[at] = value
            qkv_own[at, slot * local : (slot + 1) * local] = value[:, :local]
            qkv_mate[at, slot * local : (slot + 1) * local] = value[:, local:]
            if slot != 1:
                sums.append((3 + slot // 2, fold(value.astype(F32))))
        return sums

    band_loop(total, cast, part)
    loads.wait(4, 5, 6, 7, 8, 9)
    for start in range(0, kept.shape[1], GROUP):
        cols = slice(start, start + GROUP)
        acc[:, cols] = (
            kept[:, cols]
            + dot_nt(low[...], wq[cols, :])
            + dot_nt(low_k[...], wk[cols, :])
            + dot_nt(low_v[...], wv[cols, :])
        )

    for row in range(rows):
        text_grad[where[base + row]] = acc[row * length : (row + 1) * length].astype(BF16)
    for at in range(8):
        sums[0, at : at + 1] = jnp.sum(part[at], axis=0, keepdims=True)


def join_kernel(scalars, ins, outs, scratch):
    stay_x, got_x, stay_y, got_y = ins
    (out,) = outs
    for start, stay, got in ((0, stay_x, got_x), (stay_x.shape[1], stay_y, got_y)):
        for at in range(0, out.shape[0], 96):
            rows = slice(at, at + 96)
            out[rows, start : start + stay.shape[1]] = add_low(stay[rows], got[rows])


def add_low(left, right):
    return (left.astype(F32) + right.astype(F32)).astype(BF16)


def pack_kernel(local, hidden, scalars, ins, outs, scratch):
    (core,) = scalars
    feed, up, self_, image = ins
    feed_sum = jnp.sum(feed[...], axis=0)
    self_sum = jnp.sum(self_[...], axis=0)
    up_sum = jnp.sum(up[...], axis=0)
    common = [(0, 0), (1, 3), (1, 0), (0, 1), (1, 4), (1, 1), (0, 2), (1, 5), (1, 2)]
    even = core[0] == 0
    for out, mine in zip(outs, (True, False)):
        out[...] = jnp.zeros_like(out)
        at = 0
        for which, row in common:
            source = feed_sum if which else self_sum
            for half in range(2):
                out[at : at + 1] = source[row : row + 1, half * local : (half + 1) * local]
                at += 1
        lanes = slice(0, local) if mine else slice(local, 2 * local)
        for row in (3, 4, 5):
            out[at : at + 1] = self_sum[row : row + 1, lanes]
            at += 1
        out[at : at + 1] = image[1:2, lanes]
        at += 1
        half = 0 if mine else 1
        for start in range(0, hidden, local):
            out[at : at + 1] = up_sum[half : half + 1, start : start + local]
            at += 1
        low, high = image[0:1, :local], image[0:1, local:]
        out[at : at + 1] = jnp.where(even == mine, low, high)


def halve_kernel(rows, length, scalars, ins, outs, scratch):
    core, where = scalars
    (tall,) = scratch

    def put(at, both):
        split_lanes(tall, at, 0, both)

    row_pairs(ins[0], where, 0, rows, length, put)
    half = length // 2
    for out, first in zip(outs, (core[0] * half, (1 - core[0]) * half)):
        for token in range(half):
            out[token] = join_lanes(
                tall, pl.ds(first + token, rows, stride=length)
            ).astype(BF16)


def place_kernel(scalars, ins, outs, scratch):
    own, mate, place = ins
    (out,) = outs
    count, slots = out.shape[1], own.shape[1]
    index = lax.broadcasted_iota(jnp.int32, (count, slots), 1)
    from_own = jnp.where(place[...] == index, 1.0, 0.0).astype(BF16)
    from_mate = jnp.where(place[...] == index + slots, 1.0, 0.0).astype(BF16)
    for token in range(out.shape[0]):
        out[token] = (dot(from_own, own[token]) + dot(from_mate, mate[token])).astype(BF16)


def body(
    text,
    cotangent,
    lengths,
    box_corners,
    box_counts,
    region_box,
    patches,
    proj_weight,
    proj_bias,
    attention_in,
    attention_bias,
    attention_out,
    output_bias,
    norm_gain,
    norm_bias,
    up_weight,
    up_bias,
    down_weight,
):
    rows, length, width = text.shape
    images, patch_count, vision = patches.shape
    local = attention_in.shape[-1]
    hidden = up_weight.shape[-1]
    devices = lax.axis_size("dp")
    me, core = lax.axis_index("dp"), lax.axis_index("mp")
    pair = -(-rows // devices)
    each, odd = pair // 2, pair % 2
    deep = each + odd
    slots = devices * each + devices // 2 * odd
    patch_pad = -(-patch_count // 16) * 16
    own_images = images // 2
    step_rows = 12 if slots % 12 == 0 else 8
    steps = slots // step_rows
    tokens = step_rows * length
    all_tokens = slots * length
    full = slots * 2 == rows
    core_scalar = core.astype(jnp.int32).reshape(1)

    def mate(value):
        return lax.ppermute(value, "mp", [(0, 1), (1, 0)])

    def tie(*values):
        return lax.optimization_barrier(values)

    def exchange(value):
        return lax.all_to_all(value, "dp", split_axis=0, concat_axis=0, tiled=True)

    ain_mate = mate(attention_in)
    bias_mate = mate(attention_bias)
    aout_mate = mate(attention_out)
    up_bias_own = up_bias.reshape(1, hidden)
    up_bias_mate = mate(up_bias_own)
    up_mate = mate(up_weight)
    down_mate = mate(down_weight)

    number = jnp.arange(rows, dtype=jnp.int32)
    target = region_box // rows
    earlier = (target[:, None] == target[None, :]) & (number[None, :] < number[:, None])
    nth = jnp.sum(earlier.astype(jnp.int32), axis=1)
    even_part = nth < 2 * each
    row_core = jnp.where(even_part, nth // max(each, 1), (target ^ me) & 1)
    depth = jnp.where(even_part, nth % max(each, 1), each)
    spot = jnp.arange(devices * deep, dtype=jnp.int32)
    hit = (spot[:, None] == (target * deep + depth)[None, :]) & (row_core == core)[None, :]
    source = jnp.sum(jnp.where(hit, number[None, :], 0), axis=1)
    slot = jnp.where(even_part, target * each + depth, devices * each + (target >> 1))
    place = jnp.where(row_core == core, slot, slot + slots)[:, None]
    order = jnp.arange(slots, dtype=jnp.int32)
    late = order - devices * each
    where = jnp.where(
        late < 0,
        order // max(each, 1) * deep + order % max(each, 1),
        (2 * late + ((me & 1) ^ core)) * deep + each,
    )
    meta = jnp.concatenate(
        [(region_box % rows)[:, None], lengths[:, None], box_corners], axis=1
    )
    meta_out = jnp.sum(jnp.where(hit[:, :, None], meta[None], 0), axis=1)
    if not full:
        empty = jnp.array([0, 1, 0, 1, 0, 1], jnp.int32)
        meta_out = jnp.where(jnp.any(hit, axis=1)[:, None], meta_out, empty[None])
    arrived = exchange(meta_out)[where]
    ends = jnp.cumsum(box_counts[0])
    image = jnp.sum((ends[None, :] <= arrived[:, 0:1]).astype(jnp.int32), axis=1)
    image = (image + own_images * core) % images
    lens = arrived[:, 1]
    corners = arrived[:, 2:].reshape(-1)

    block_shape = (devices * deep, length, width)
    if full:
        x_out, upstream_out = run(
            partial(fetch_kernel, devices * deep),
            1,
            [source],
            [(text, ANY), (cotangent, ANY)],
            [(block_shape, BF16, whole_spec(block_shape))] * 2,
            [pltpu.SemaphoreType.DMA((2 * devices * deep,))],
            0,
        )
    else:
        valid = jnp.any(hit, axis=1)[:, None, None]
        x_out = jnp.where(valid, text[source], 0)
        upstream_out = jnp.where(valid, cotangent[source], 0)
    x_in = exchange(x_out)

    patches, aout_mate, image, corners, lens = tie(patches, aout_mate, image, corners, lens)
    by_patch = jnp.transpose(patches, (1, 0, 2))
    parts = next(n for n in (5, 4, 3, 2, 1) if patch_count % n == 0)
    weight_scratch = pltpu.VMEM((width, width), BF16)

    def slabs(count):
        return pltpu.VMEM((width // LANES, count, LANES), F32)

    patch_scratch = pltpu.VMEM((parts, patch_count // parts, images, vision), BF16)
    image_shape = (images, patch_pad, width)
    proj, keys, values = run(
        partial(project_kernel, images, own_images, patch_pad, patch_count, local),
        1,
        [core_scalar],
        [
            (by_patch, ANY),
            (proj_weight, whole_spec(proj_weight.shape)),
            (proj_bias.reshape(1, width), whole_spec((1, width))),
            (attention_in, ANY),
            (ain_mate, ANY),
            (attention_bias, whole_spec(attention_bias.shape)),
            (bias_mate, whole_spec(bias_mate.shape)),
        ],
        [((own_images,) + image_shape[1:], BF16, whole_spec((own_images,) + image_shape[1:]))]
        + [(image_shape, BF16, whole_spec(image_shape))] * 2,
        [
            patch_scratch,
            slabs(patch_count * images),
            weight_scratch,
            weight_scratch,
            pltpu.SemaphoreType.DMA((parts,)),
            pltpu.SemaphoreType.DMA((4,)),
        ],
        2 * images * patch_pad * width * (vision + 2 * width),
    )

    upstream_out, proj, keys, values = tie(upstream_out, proj, keys, values)
    upstream_in = exchange(upstream_out)

    def token_in(value):
        return (value, rows_spec((tokens, value.shape[1]), 0))

    def token_out(cols, dtype):
        return ((all_tokens, cols), dtype, rows_spec((tokens, cols), 0))

    block_out = (block_shape, BF16, whole_spec(block_shape))

    def f32_tokens(cols):
        return pltpu.VMEM((tokens, cols), F32)

    def low_tokens(cols):
        return pltpu.VMEM((tokens, cols), BF16)

    def whole(value):
        return (value, whole_spec(value.shape))

    attention_flops = 4 * 4 * all_tokens * width * 64

    x, unit_one, q_self, k_self, v_self, att_own, att_mate, self_low, queries, rstd_one = run(
        partial(self_kernel, steps, step_rows, local, length),
        steps,
        [lens, where],
        [
            whole(x_in),
            (attention_in, ANY),
            (ain_mate, ANY),
            (attention_out, ANY),
            (aout_mate, ANY),
            whole(attention_bias),
            whole(bias_mate),
            whole(output_bias),
            whole(norm_gain),
            whole(norm_bias),
        ],
        [token_out(width, BF16), token_out(width, F32)]
        + [token_out(width, BF16)] * 3
        + [token_out(local, BF16)] * 2
        + [token_out(width, BF16)] * 2
        + [token_out(1, F32)],
        [weight_scratch] * 5
        + [f32_tokens(width)] * 4
        + [low_tokens(width), pltpu.SemaphoreType.DMA((10,))],
        2 * all_tokens * width * width * 5 + attention_flops,
    )

    (attended,) = run(
        partial(cross_kernel, step_rows, length),
        steps,
        [image, corners],
        [token_in(queries), whole(keys), whole(values)],
        [token_out(width, BF16)],
        [f32_tokens(width)] * 2,
        attention_flops * 4,
    )

    result = run(
        partial(feed_kernel, steps, step_rows, local, hidden, length),
        steps,
        [where],
        [
            whole(upstream_in),
            token_in(attended),
            token_in(unit_one),
            (attention_out, ANY),
            (aout_mate, ANY),
            (up_weight, ANY),
            (up_mate, ANY),
            (down_weight, ANY),
            (down_mate, ANY),
            whole(output_bias),
            whole(norm_gain),
            whole(norm_bias),
            whole(up_bias_own),
            whole(up_bias_mate),
        ],
        [block_out]
        + [token_out(width, BF16)] * 3
        + [token_out(width, F32)]
        + [token_out(local, BF16)] * 2
        + [token_out(hidden, BF16)] * 4
        + [
            token_out(width, BF16),
            ((steps, 8, width), F32, rows_spec((1, 8, width), 0)),
            ((steps, 2, hidden), F32, rows_spec((1, 2, hidden), 0)),
        ],
        [weight_scratch]
        + [
            pltpu.VMEM((hidden // TILE, width, 2 * TILE), BF16),
            pltpu.VMEM((hidden // TILE, 2 * TILE, width), BF16),
        ]
        + [f32_tokens(width)] * 3
        + [f32_tokens(1), low_tokens(width), low_tokens(width)]
        + [f32_tokens(2 * TILE)] * 2
        + [pltpu.VMEM((hidden // TILE, tokens, 2 * TILE), F32)]
        + [pltpu.VMEM((8, 8, width), F32), pltpu.VMEM((2, 8, hidden), F32)]
        + [pltpu.SemaphoreType.DMA((2 + 4 * hidden // TILE,))],
        2 * all_tokens * width * (2 * width + 8 * hidden),
    )
    merged_out, cross_low, grad_ffn, grad_cross, dz_two, a_own, a_mate = result[:7]
    g_own, g_mate, du_own, du_mate, grad_att, feed_sums, up_sums = result[7:]

    bits = devices.bit_length() - 1

    def partner_bits(value, mask):
        return lax.ppermute(value, "dp", [(d, d ^ mask) for d in range(devices)])

    def opened(value):
        return value.reshape((2,) * bits + (value.shape[0] // devices, value.shape[1]))

    def swap(value, axis, bit):
        mine = (me >> bit) & 1
        away = lax.dynamic_index_in_dim(value, 1 - mine, axis, keepdims=False)
        stay = lax.dynamic_index_in_dim(value, mine, axis, keepdims=False)
        return stay, partner_bits(away, 1 << bit)

    def first_swaps(by_x, by_y):
        return swap(opened(by_x), bits - 1, 0) + swap(opened(by_y), bits - 2, 1)

    def second_swaps(stay_x, got_x, stay_y, got_y):
        return swap(add(stay_x, got_x), bits - 2, 1) + swap(add(stay_y, got_y), bits - 2, 0)

    def add(stay, got):
        return add_low(stay, got)

    def last_parts(values, after):
        count = values[0].size // values[0].shape[-1]
        shape = (count, values[0].shape[-1] + values[2].shape[-1])
        values = [value.reshape(count, value.shape[-1]) for value in values]
        (joined,) = run(
            join_kernel,
            1,
            [],
            [whole(value) for value in values],
            [(shape, BF16, whole_spec(shape))],
            [],
            0,
            after,
        )
        return joined.reshape(devices // 4, count // (devices // 4), shape[1])

    def last_sum(both, first_width):
        groups = [[low + 4 * n for n in range(devices // 4)] for low in range(4)]
        both = lax.all_to_all(
            both, "dp", split_axis=0, concat_axis=0, axis_index_groups=groups, tiled=True
        )
        total = jnp.sum(both.astype(F32), axis=0)
        return total[:, :first_width], total[:, first_width:]

    def low_tn(left, right):
        return dot_tn(left, right).astype(BF16)

    merged_in = exchange(merged_out)
    up_away, down_away = low_tn(cross_low, du_mate), low_tn(grad_ffn, g_mate)
    grad_att, queries, up_away, down_away = tie(grad_att, queries, up_away, down_away)
    up_got, down_got = mate(up_away), mate(down_away)

    half_shape = (2, own_images, patch_pad, width)
    image_acc = pltpu.VMEM(image_shape, F32)
    piece, piece_out, grad_queries = run(
        partial(cross_grad_kernel, steps, step_rows, length),
        steps,
        [image, corners],
        [token_in(queries), token_in(grad_att), whole(keys), whole(values)],
        [(half_shape, BF16, whole_spec(half_shape))] * 2 + [token_out(width, BF16)],
        [f32_tokens(width)] * 3 + [image_acc] * 2,
        attention_flops * 12,
    )
    piece_mate = mate(piece_out)

    up_part = (dot_tn(cross_low, du_own) + up_got.astype(F32)).astype(BF16)
    down_part = (dot_tn(grad_ffn, g_own) + down_got.astype(F32)).astype(BF16)
    grad_queries, up_part, down_part = tie(grad_queries, up_part, down_part)
    feed_stage = first_swaps(up_part, down_part)

    result = run(
        partial(self_grad_kernel, steps, step_rows, local, length),
        steps,
        [lens, where],
        [
            token_in(grad_queries),
            token_in(unit_one),
            token_in(rstd_one),
            token_in(dz_two),
            token_in(q_self),
            token_in(k_self),
            token_in(v_self),
            (attention_in, ANY),
            (ain_mate, ANY),
            (attention_out, ANY),
            (aout_mate, ANY),
            whole(norm_gain),
        ],
        [block_out]
        + [token_out(width, BF16)]
        + [token_out(local, BF16)] * 2
        + [token_out(3 * local, BF16)] * 2
        + [((steps, 8, width), F32, rows_spec((1, 8, width), 0))],
        [weight_scratch] * 5
        + [f32_tokens(width)] * 2
        + [low_tokens(width)] * 3
        + [f32_tokens(width)] * 3
        + [pltpu.VMEM((8, 8, width), F32), pltpu.SemaphoreType.DMA((10,))],
        2 * all_tokens * width * width * 5 + attention_flops * 2,
    )
    text_out, grad_self, dq_own, dq_mate, qkv_own, qkv_mate, self_sums = result
    text_in = exchange(text_out)

    self_away = jnp.concatenate(
        [
            low_tn(x, qkv_mate),
            low_tn(grad_self, att_mate),
            low_tn(grad_cross, a_mate),
            low_tn(self_low, dq_mate),
        ],
        axis=1,
    )
    self_got = mate(self_away)
    feed_stage = tie(self_away, *feed_stage)[1:]
    feed_stage = second_swaps(*feed_stage)
    self_own = jnp.concatenate(
        [
            dot_tn(x, qkv_own),
            dot_tn(grad_self, att_own),
            dot_tn(grad_cross, a_own),
            dot_tn(self_low, dq_own),
        ],
        axis=1,
    )
    self_part = (self_own + self_got.astype(F32)).astype(BF16)
    half_width = self_part.shape[1] // 2
    self_stage = first_swaps(self_part[:, :half_width], self_part[:, half_width:])

    flat_images = own_images * patch_pad
    patch_grad_shape = (patch_count, own_images, vision)
    kv_own, kv_mate, patch_grad, proj_weight_sum, image_sums = run(
        partial(image_kernel, images, patch_count, local),
        1,
        [core_scalar],
        [
            whole(piece),
            whole(piece_mate),
            (by_patch, ANY),
            whole(proj_weight),
            (attention_in, ANY),
            (ain_mate, ANY),
        ],
        [
            ((flat_images, width), BF16, whole_spec((flat_images, width))),
            ((flat_images, width), BF16, whole_spec((flat_images, width))),
            (patch_grad_shape, BF16, whole_spec(patch_grad_shape)),
            ((vision, width), F32, whole_spec((vision, width))),
            ((8, width), F32, whole_spec((8, width))),
        ],
        [
            slabs(patch_count * own_images),
            slabs(patch_count * images),
            patch_scratch,
            weight_scratch,
            weight_scratch,
            pltpu.VMEM((2, 8, width), F32),
            pltpu.SemaphoreType.DMA((parts,)),
            pltpu.SemaphoreType.DMA((4,)),
        ],
        2 * flat_images * width * (2 * width + 2 * vision),
    )

    up_grad, down_grad = last_sum(last_parts(feed_stage, [kv_own]), hidden)
    self_stage = second_swaps(*self_stage)
    kv_low = proj.reshape(flat_images, width)
    kv_away = low_tn(kv_low, kv_mate)
    kv_got = mate(kv_away)
    proj_away = lax.dynamic_slice_in_dim(proj_weight_sum, (1 - core) * local, local, 1)
    proj_got = mate(proj_away.astype(BF16))
    kv_part = (dot_tn(kv_low, kv_own) + kv_got.astype(F32)).astype(BF16)
    proj_own = lax.dynamic_slice_in_dim(proj_weight_sum, core * local, local, 1)
    proj_part = (proj_own + proj_got.astype(F32)).astype(BF16)
    proj_part = proj_part.reshape(width, vision * local // width)
    image_stage = first_swaps(kv_part, proj_part)
    self_one, self_two = last_sum(last_parts(self_stage, []), half_width)
    image_stage = second_swaps(*image_stage)
    kv_grad, proj_grad = last_sum(last_parts(image_stage, []), width)
    proj_grad = proj_grad.reshape(vision // devices, local)

    lines = 23 + hidden // local
    packed_shape = (-(-lines // 8) * 8, local)
    small, small_out = run(
        partial(pack_kernel, local, hidden),
        1,
        [core_scalar],
        [whole(feed_sums), whole(up_sums), whole(self_sums), whole(image_sums)],
        [(packed_shape, F32, whole_spec(packed_shape))] * 2,
        [],
        0,
        [up_grad, kv_part, proj_part],
    )
    small = small + mate(small_out)
    for bit in range(bits):
        small = small + partner_bits(small, 1 << bit)
    common = small[:18].reshape(3, 3, width)
    bias_grad = small[18:22].reshape(2, 2, local)
    up_bias_grad = small[22 : 22 + hidden // local].reshape(hidden)
    proj_bias_grad = small[22 + hidden // local]

    ready = [self_one[:, at * local : (at + 1) * local] for at in range(3)]
    out_self, out_cross, query_cross = [
        self_two[:, at * local : (at + 1) * local] for at in range(3)
    ]
    in_grad = jnp.stack(
        ready + [query_cross, kv_grad[:, :local], kv_grad[:, local:]]
    ).reshape(2, 3, width // devices, local)
    out_grad = jnp.stack([out_self.T, out_cross.T])

    def tokens_out(value, after, after_place):
        shape = (length // 2, slots, width)
        own, away = run(
            partial(halve_kernel, slots, length),
            1,
            [core_scalar, where],
            [whole(value)],
            [(shape, BF16, whole_spec(shape))] * 2,
            [slabs(all_tokens)],
            0,
            after,
        )
        shape = (length // 2, rows, width)
        (out,) = run(
            place_kernel,
            1,
            [],
            [whole(own), whole(mate(away)), whole(place)],
            [(shape, BF16, whole_spec(shape))],
            [],
            0,
            after_place,
        )
        return jnp.transpose(out, (1, 0, 2))

    return (
        tokens_out(merged_in, [self_part], [kv_part]),
        tokens_out(text_in, [kv_own], [kv_part, proj_part]),
        jnp.transpose(patch_grad, (1, 0, 2)),
        proj_grad,
        proj_bias_grad,
        in_grad,
        bias_grad,
        out_grad,
        common[0],
        common[1],
        common[2],
        up_grad,
        up_bias_grad,
        down_grad.T,
    )


def solution(mesh):
    placed = (
        P("dp", None, None),
        P("dp", None, None),
        P("dp"),
        P("dp", None),
        P("dp", None),
        P("dp"),
        P("dp", None, None),
        P(),
        P(),
        P(None, None, None, "mp"),
        P(None, None, "mp"),
        P(None, "mp", None),
        P(),
        P(),
        P(),
        P(None, "mp"),
        P("mp"),
        P("mp", None),
    )
    return jax.shard_map(
        body,
        mesh=mesh,
        in_specs=placed,
        out_specs=(
            P("dp", "mp", None),
            P("dp", "mp", None),
            P(("dp", "mp"), None, None),
            P("dp", "mp"),
            P("mp"),
            P(None, None, "dp", "mp"),
            P(None, None, "mp"),
            P(None, "mp", "dp"),
            P(),
            P(),
            P(),
            P("dp", "mp"),
            P("mp"),
            P("mp", "dp"),
        ),
        check_vma=False,
    )
```

```python
import math
from functools import partial

import jax
import jax.numpy as jnp
from jax import lax
from jax.experimental import pallas as pl
from jax.experimental.pallas import tpu as pltpu
from jax.sharding import PartitionSpec as P

HEAD_DIM = 64
GRID = 12
EPS = 1e-12
NEG = -1e30
SCALE = HEAD_DIM ** (-0.5)

F32 = jnp.float32
BF16 = jnp.bfloat16

GROUP = 4 * HEAD_DIM
BAND = 32
BANDS = 5
LANES = 128
TILE = 256
PAIRED = 4
VMEM_LIMIT = 58 << 20


def dot(left, right):
    return lax.dot_general(left, right, (((1,), (0,)), ((), ())), preferred_element_type=F32)


def dot_nt(left, right):
    return lax.dot_general(left, right, (((1,), (1,)), ((), ())), preferred_element_type=F32)


def dot_tn(left, right):
    return lax.dot_general(left, right, (((0,), (0,)), ((), ())), preferred_element_type=F32)


def rows_spec(block, offset):
    rank = len(block)
    return pl.BlockSpec(block, lambda s, *_: (s + offset,) + (0,) * (rank - 1))


def whole_spec(shape):
    rank = len(shape)
    return pl.BlockSpec(shape, lambda s, *_: (0,) * rank, pipeline_mode=pl.Buffered(1))


ANY = pl.BlockSpec(memory_space=pl.ANY)


def run(body, steps, scalars, ins, outs, scratch, flops, after=(), light=False):
    ns, ni, no = len(scalars), len(ins), len(outs)

    def kernel(*refs):
        rest = refs[ns + ni + len(after) :]
        body(refs[:ns], refs[ns : ns + ni], rest[:no], rest[no:])

    moved = sum(math.prod(a.shape) * a.dtype.itemsize for a, _ in ins)
    ins = list(ins) + [(array, ANY) for array in after]
    moved += sum(math.prod(shape) * jnp.dtype(dtype).itemsize for shape, dtype, _ in outs)
    return pl.pallas_call(
        kernel,
        grid_spec=pltpu.PrefetchScalarGridSpec(
            num_scalar_prefetch=ns,
            grid=(steps,),
            in_specs=[spec for _, spec in ins],
            out_specs=[spec for _, _, spec in outs],
            scratch_shapes=scratch,
        ),
        out_shape=[jax.ShapeDtypeStruct(shape, dtype) for shape, dtype, _ in outs],
        compiler_params=pltpu.CompilerParams(
            dimension_semantics=("arbitrary",), vmem_limit_bytes=VMEM_LIMIT
        ),
        cost_estimate=pl.CostEstimate(
            flops=0 if light else flops,
            bytes_accessed=0 if light else moved,
            transcendentals=0,
        ),
    )(*scalars, *[array for array, _ in ins])


class Loads:
    def __init__(self, steps, sems, pairs):
        self.steps = steps
        self.copies = [
            pltpu.make_async_copy(source, target, sems.at[at])
            for at, (source, target) in enumerate(pairs)
        ]

    def first(self, action):
        if self.steps == 1:
            action()
        else:
            pl.when(pl.program_id(0) == 0)(action)

    def start(self):
        self.first(lambda: [copy.start() for copy in self.copies] and None)

    def wait(self, *which):
        self.first(lambda: [self.copies[at].wait() for at in which] and None)


def side_by_side(own, mate, target, width):
    return [(own, target.at[:, pl.ds(0, width)]), (mate, target.at[:, pl.ds(width, width)])]


def one_above(own, mate, target, height):
    return [(own, target.at[pl.ds(0, height)]), (mate, target.at[pl.ds(height, height)])]


def moments(z):
    center = z - jnp.mean(z, axis=-1, keepdims=True)
    rstd = lax.rsqrt(jnp.mean(center * center, axis=-1, keepdims=True) + EPS)
    return center * rstd, rstd


def norm_grad(unit, rstd, gain, grad):
    inner = grad * gain
    return rstd * (
        inner
        - jnp.mean(inner, axis=-1, keepdims=True)
        - unit * jnp.mean(inner * unit, axis=-1, keepdims=True)
    )


def fold(block):
    return jnp.sum(block.reshape(block.shape[0] // 8, 8, block.shape[1]), axis=0)


def gelu(u):
    bell = jnp.exp2(u * u * (-0.5 / math.log(2.0)))
    t = 1.0 / (1.0 + (0.3275911 * 0.5**0.5) * jnp.abs(u))
    poly = t * (
        0.5 * 0.254829592
        + t
        * (
            0.5 * -0.284496736
            + t * (0.5 * 1.421413741 + t * (0.5 * -1.453152027 + t * (0.5 * 1.061405429)))
        )
    )
    tail = poly * bell
    phi = jnp.where(u >= 0.0, 1.0 - tail, tail)
    return u * phi, phi + u * (bell * (1.0 / math.sqrt(2.0 * math.pi)))


def spread_heads(block, lane_head):
    parts = [jnp.where(lane_head == h, block, 0.0) for h in range(GROUP // HEAD_DIM)]
    return jnp.concatenate(parts, axis=0).astype(BF16)


def gather_heads(block, lane_head, tokens):
    total = jnp.where(lane_head == 0, block[0:tokens], 0.0)
    for h in range(1, GROUP // HEAD_DIM):
        total = jnp.where(lane_head == h, block[h * tokens : (h + 1) * tokens], total)
    return total


def lane_heads():
    return lax.broadcasted_iota(jnp.int32, (1, GROUP), 1) // HEAD_DIM


def attend(items):
    scores = [dot_nt(qm, kb) for qm, kb, vb, keep in items]
    weights = []
    for score, (qm, kb, vb, keep) in zip(scores, items):
        score = jnp.where(keep, score, NEG)
        top = jnp.max(score, axis=1, keepdims=True)
        weight = jnp.exp(score - top)
        weight = weight * (1.0 / jnp.sum(weight, axis=1, keepdims=True))
        weights.append(weight.astype(BF16))
    return [dot(weight, vb) for weight, (qm, kb, vb, keep) in zip(weights, items)]


def attend_grad(items):
    scores = [dot_nt(kb, qm) for qm, kb, vb, dom, keep in items]
    grads = [dot_nt(vb, dom) for qm, kb, vb, dom, keep in items]
    middle = []
    for score, grad, (qm, kb, vb, dom, keep) in zip(scores, grads, items):
        score = jnp.where(keep, score, NEG)
        top = jnp.max(score, axis=0, keepdims=True)
        weight = jnp.exp(score - top)
        weight = weight * (1.0 / jnp.sum(weight, axis=0, keepdims=True))
        inner = jnp.sum(weight * grad, axis=0, keepdims=True)
        grad_score = weight * (grad - inner)
        middle.append(
            (weight.astype(BF16), grad_score.astype(BF16), jnp.transpose(grad_score).astype(BF16))
        )
    results = []
    for (weight, grad_score, turned), (qm, kb, vb, dom, keep) in zip(middle, items):
        results.append((dot(turned, kb), dot(grad_score, qm), dot(weight, dom)))
    return results


def box_keep(corners, slot, shape, axis):
    index = lax.broadcasted_iota(jnp.int32, shape, axis) - 1
    grid_row = (index * 2731) >> 15
    grid_col = index - grid_row * GRID
    inside = (grid_col >= corners[slot * 4]) & (grid_col < corners[slot * 4 + 1])
    inside = inside & (grid_row >= corners[slot * 4 + 2]) & (grid_row < corners[slot * 4 + 3])
    return (inside & (index >= 0)) | (index < 0)


def band_loop(total, body, part=None):
    @pl.loop(0, total // (BAND * BANDS))
    def _(step):
        sums = []
        for band in range(BANDS):
            start = pl.multiple_of(step * (BAND * BANDS) + band * BAND, BAND)
            folded = body(pl.ds(start, BAND))
            if folded is not None:
                sums.append(folded)
        for terms in zip(*sums):
            at = terms[0][0]
            part[at] += sum(value for _, value in terms[1:]) + terms[0][1]


def by_columns(left, weight, finish, transposed=False):
    count = weight.shape[0] if transposed else weight.shape[1]
    for start in range(0, count, GROUP):
        cols = slice(start, start + GROUP)
        value = dot_nt(left, weight[cols, :]) if transposed else dot(left, weight[:, cols])
        finish(cols, value)


def both_halves(own, mate, at):
    return jnp.concatenate([own[at[0], at[1] : at[1] + 1], mate[at[0], at[1] : at[1] + 1]], axis=1)


def row_pairs(source, where, first, count, length, finish):
    for at in range(0, count, 2):
        both = [source[where[first + at + n]].astype(F32) for n in range(2)]
        finish(slice(at * length, (at + 2) * length), jnp.concatenate(both, axis=0))


def split_lanes(target, rows, start, value):
    for lane in range(0, value.shape[1], LANES):
        target[(start + lane) // LANES, rows, :] = value[:, lane : lane + LANES]


def join_lanes(source, rows):
    return jnp.concatenate([source[lane, rows, :] for lane in range(source.shape[0])], axis=1)


def fetch_kernel(count, scalars, ins, outs, scratch):
    (source,) = scalars
    (sems,) = scratch
    copies = [
        pltpu.make_async_copy(table.at[source[at]], out.at[at], sems.at[which * count + at])
        for which, (table, out) in enumerate(zip(ins, outs))
        for at in range(count)
    ]
    for copy in copies:
        copy.start()
    for copy in copies:
        copy.wait()


def project_kernel(images, own_images, patch_pad, patch_count, local, scalars, ins, outs, scratch):
    (core,) = scalars
    patches, proj_weight, proj_bias, ain, ain_mate, bias_own, bias_mate = ins
    proj, keys, values = outs
    taken, raw, w1, w2, sems, weight_sems = scratch
    loads = Loads(
        1,
        weight_sems,
        side_by_side(ain.at[1, 1], ain_mate.at[1, 1], w1, local)
        + side_by_side(ain.at[1, 2], ain_mate.at[1, 2], w2, local),
    )
    parts, span = taken.shape[0], taken.shape[1]
    arrivals = Loads(
        1, sems, [(patches.at[pl.ds(n * span, span)], taken.at[n]) for n in range(parts)]
    )
    arrivals.start()
    loads.start()
    rows = span * images
    width = raw.shape[0] * LANES
    for n in range(parts):
        arrivals.wait(n)
        flat = taken[n].reshape(rows, taken.shape[3])
        for start in range(0, width, GROUP):
            cols = slice(start, start + GROUP)
            split_lanes(
                raw,
                slice(n * rows, (n + 1) * rows),
                start,
                dot(flat, proj_weight[:, cols]) + proj_bias[:, cols],
            )
    loads.wait(0, 1, 2, 3)
    bias = both_halves(bias_own, bias_mate, (1, 1))
    first = core[0] * own_images
    rest = jnp.zeros((patch_pad - patch_count, width), F32)

    group = 4

    @pl.loop(0, images // group)
    def _(step):
        both = []
        for at in range(group):
            which = lax.rem(step * group + at + first, images)
            own = jnp.concatenate(
                [
                    raw[lane, pl.ds(which, patch_count, stride=images), :]
                    for lane in range(raw.shape[0])
                ],
                axis=1,
            )
            both.append(jnp.concatenate([own, rest], axis=0))
        low = jnp.concatenate(both, axis=0).astype(BF16)
        some = pl.ds(step * group, group)

        @pl.when(step < own_images // group)
        def _():
            proj[some] = low.reshape(group, patch_pad, width)

        shape = (group, patch_pad, GROUP)
        for start in range(0, width, GROUP):
            cols = slice(start, start + GROUP)
            keys[some, :, cols] = dot(low, w1[:, cols]).astype(BF16).reshape(shape)
            values[some, :, cols] = (
                (dot(low, w2[:, cols]) + bias[:, cols]).astype(BF16).reshape(shape)
            )


def self_kernel(steps, rows, local, length, scalars, ins, outs, scratch):
    lens, where = scalars
    x_in, ain, ain_mate, aout, aout_mate, bias_own, bias_mate, out_bias, gain, shift = ins
    x_out, unit_one, q_out, k_out, v_out, att_own, att_mate, low_out, cross_q, rstd_one = outs
    wq, wk, wv, wo, wc, qs, ks, vs, acc, low, sems = scratch
    total = rows * length
    loads = Loads(
        steps,
        sems,
        side_by_side(ain.at[0, 0], ain_mate.at[0, 0], wq, local)
        + side_by_side(ain.at[0, 1], ain_mate.at[0, 1], wk, local)
        + side_by_side(ain.at[0, 2], ain_mate.at[0, 2], wv, local)
        + one_above(aout.at[0], aout_mate.at[0], wo, local)
        + side_by_side(ain.at[1, 0], ain_mate.at[1, 0], wc, local),
    )
    loads.start()
    bias_q = both_halves(bias_own, bias_mate, (0, 0))
    bias_v = both_halves(bias_own, bias_mate, (0, 1))
    bias_c = both_halves(bias_own, bias_mate, (1, 0))

    def put(at, both):
        x_out[at] = both.astype(BF16)

    base = pl.program_id(0) * rows
    row_pairs(x_in, where, base, rows, length, put)
    xb = x_out[...]

    def keep_q(cols, value):
        value = (value + bias_q[:, cols]).astype(BF16)
        q_out[:, cols] = value
        qs[:, cols] = value.astype(F32) * SCALE

    def keep_k(cols, value):
        value = value.astype(BF16)
        k_out[:, cols] = value
        ks[:, cols] = value.astype(F32)

    def keep_v(cols, value):
        value = (value + bias_v[:, cols]).astype(BF16)
        v_out[:, cols] = value
        vs[:, cols] = value.astype(F32)

    loads.wait(0, 1)
    by_columns(xb, wq, keep_q)
    loads.wait(2, 3)
    by_columns(xb, wk, keep_k)
    loads.wait(4, 5)
    by_columns(xb, wv, keep_v)
    lane_head = lane_heads()
    key_index = lax.broadcasted_iota(jnp.int32, (1, length), 1)

    @pl.loop(0, rows // PAIRED)
    def _(step):
        items, places = [], []
        for row in range(PAIRED):
            row = step * PAIRED + row
            at = pl.ds(pl.multiple_of(row * length, 8), length)
            keep = key_index < lens[base + row]
            for g in range(qs.shape[1] // GROUP):
                lanes = slice(g * GROUP, (g + 1) * GROUP)
                items.append(
                    (
                        spread_heads(qs[at, lanes], lane_head),
                        ks[at, lanes].astype(BF16),
                        vs[at, lanes].astype(BF16),
                        keep,
                    )
                )
                places.append((at, lanes))
        for (at, lanes), result in zip(places, attend(items)):
            acc[at, lanes] = gather_heads(result, lane_head, length)

    def cast(at):
        value = acc[at].astype(BF16)
        low[at] = value
        att_own[at] = value[:, :local]
        att_mate[at] = value[:, local:]

    def to_acc(cols, value):
        acc[:, cols] = value

    band_loop(total, cast)
    loads.wait(6, 7)
    by_columns(low[...], wo, to_acc)

    def norm(at):
        z = x_out[at].astype(F32) + acc[at] + out_bias[0:1]
        unit, rstd = moments(z)
        unit_one[at] = unit
        rstd_one[at] = rstd
        h = (unit * gain[0:1] + shift[0:1]).astype(BF16)
        low[at] = h
        low_out[at] = h

    band_loop(total, norm)
    loads.wait(8, 9)

    def to_query(cols, value):
        cross_q[:, cols] = (value + bias_c[:, cols]).astype(BF16)

    by_columns(low[...], wc, to_query)


def cross_kernel(rows, length, scalars, ins, outs, scratch):
    image, corners = scalars
    queries, keys, values = ins
    (att,) = outs
    qs, acc = scratch
    patch_pad = keys.shape[1]
    lane_head = lane_heads()
    base = pl.program_id(0) * rows

    def spread(at):
        qs[at] = queries[at].astype(F32) * SCALE

    band_loop(rows * length, spread)

    @pl.loop(0, rows // PAIRED)
    def _(step):
        items, places = [], []
        for row in range(PAIRED):
            row = step * PAIRED + row
            at = pl.ds(pl.multiple_of(row * length, 8), length)
            which = image[base + row]
            keep = box_keep(corners, base + row, (1, patch_pad), 1)
            for g in range(qs.shape[1] // GROUP):
                lanes = slice(g * GROUP, (g + 1) * GROUP)
                items.append(
                    (
                        spread_heads(qs[at, lanes], lane_head),
                        keys[which, :, lanes],
                        values[which, :, lanes],
                        keep,
                    )
                )
                places.append((at, lanes))
        for (at, lanes), result in zip(places, attend(items)):
            acc[at, lanes] = gather_heads(result, lane_head, length)

    def cast(at):
        att[at] = acc[at].astype(BF16)

    band_loop(rows * length, cast)


def feed_kernel(steps, rows, local, hidden, length, scalars, ins, outs, scratch):
    (where,) = scalars
    grad_in, att, unit_one, aout, aout_mate, up, up_mate, down, down_mate = ins[:9]
    out_bias, gains, shift, up_bias, up_bias_mate = ins[9:]
    merged, low_out, df_out, do_out, dz_out, a_own, a_mate = outs[:7]
    g_out, du_out = outs[7:9], outs[9:11]
    da_out, sums, up_sums = outs[11:]
    wo, wu, wd, acc, kept, unit_two, rstd_two, low, upstream, even, odd, slope = scratch[:12]
    part, up_part, sems = scratch[12:]
    tiles = hidden // TILE
    total = rows * length
    loads = Loads(
        steps,
        sems,
        one_above(aout.at[1], aout_mate.at[1], wo, local)
        + [
            (source.at[:, pl.ds(t * TILE, TILE)], wu.at[t, :, pl.ds(half * TILE, TILE)])
            for t in range(tiles)
            for half, source in enumerate((up, up_mate))
        ]
        + [
            (source.at[pl.ds(t * TILE, TILE)], wd.at[t, pl.ds(half * TILE, TILE)])
            for t in range(tiles)
            for half, source in enumerate((down, down_mate))
        ],
    )
    loads.start()
    part[...] = jnp.zeros_like(part)

    def put(at, both):
        upstream[at] = both.astype(BF16)

    base = pl.program_id(0) * rows
    row_pairs(grad_in, where, base, rows, length, put)

    def to_acc(cols, value):
        acc[:, cols] = value

    a_own[...] = att[:, :local]
    a_mate[...] = att[:, local:]
    loads.wait(0, 1)
    by_columns(att[...], wo, to_acc)

    def norm_two(at):
        h_one = unit_one[at] * gains[0:1] + shift[0:1]
        unit, rstd = moments(h_one + acc[at] + out_bias[1:2])
        h_two = unit * gains[1:2] + shift[1:2]
        unit_two[at] = unit
        rstd_two[at] = rstd
        kept[at] = h_two
        h_low = h_two.astype(BF16)
        low[at] = h_low
        low_out[at] = h_low

    band_loop(total, norm_two)
    acc[...] = jnp.zeros_like(acc)
    loads.wait(*range(2, 2 + 4 * tiles))
    biases = (up_bias, up_bias_mate)

    def activate(units, t):
        cols = slice(t * TILE, (t + 1) * TILE)
        for half in range(2):
            lanes = slice(half * TILE, (half + 1) * TILE)
            bias = biases[half][:, cols]
            for start in range(0, total, BAND):
                at = slice(start, start + BAND)
                active, sloped = gelu(units[at, lanes] + bias)
                g_out[half][at, cols] = active.astype(BF16)
                slope[t, at, lanes] = sloped

    def add_down(t):
        cols = slice(t * TILE, (t + 1) * TILE)
        both = jnp.concatenate([g_out[0][:, cols], g_out[1][:, cols]], axis=1)
        acc[...] += dot(both, wd[t])

    units = (even, odd)
    even[...] = dot(low[...], wu[0])
    for t in range(tiles):
        if t + 1 < tiles:
            units[(t + 1) % 2][...] = dot(low[...], wu[t + 1])
        activate(units[t % 2], t)
        add_down(t)

    def norm_three(at):
        unit, rstd = moments(kept[at] + acc[at] + out_bias[2:3])
        gain = gains[2:3]
        unit_three = unit * gain + shift[2:3]
        grad = upstream[at].astype(F32)
        dz = norm_grad(unit, rstd, gain, grad)
        kept[at] = dz
        acc[at] = unit_three
        dz_low = dz.astype(BF16)
        low[at] = dz_low
        df_out[at] = dz_low
        return (
            (0, fold(dz_low.astype(F32))),
            (1, fold(grad * unit)),
            (2, fold(grad)),
        )

    band_loop(total, norm_three, part)

    for row in range(rows):
        merged[where[base + row]] = acc[row * length : (row + 1) * length].astype(BF16)
    acc[...] = jnp.zeros_like(acc)

    for t in range(tiles):
        cols = slice(t * TILE, (t + 1) * TILE)
        grads = dot_nt(low[...], wd[t])
        for half in range(2):
            lanes = slice(half * TILE, (half + 1) * TILE)
            folded = 0.0
            for start in range(0, total, BAND):
                at = slice(start, start + BAND)
                du = (grads[at, lanes] * slope[t, at, lanes]).astype(BF16)
                du_out[half][at, cols] = du
                folded = folded + fold(du.astype(F32))
            up_part[half, :, cols] = folded
        both = jnp.concatenate([du_out[0][:, cols], du_out[1][:, cols]], axis=1)
        acc[...] += dot_nt(both, wu[t])

    def norm_two_back(at):
        grad = kept[at] + acc[at]
        unit = unit_two[at]
        dz = norm_grad(unit, rstd_two[at], gains[1:2], grad)
        dz_out[at] = dz
        dz_low = dz.astype(BF16)
        low[at] = dz_low
        do_out[at] = dz_low
        return (
            (3, fold(dz_low.astype(F32))),
            (4, fold(grad * unit)),
            (5, fold(grad)),
        )

    band_loop(total, norm_two_back, part)

    def to_grad(cols, value):
        da_out[:, cols] = value.astype(BF16)

    by_columns(low[...], wo, to_grad, transposed=True)
    for at in range(8):
        sums[0, at : at + 1] = jnp.sum(part[at], axis=0, keepdims=True)
    for half in range(2):
        up_sums[0, half : half + 1] = jnp.sum(up_part[half], axis=0, keepdims=True)


def cross_grad_kernel(steps, rows, length, scalars, ins, outs, scratch):
    image, corners = scalars
    queries, grads, keys, values = ins
    own, mate, grad_queries = outs
    qs, gs, acc, dk, dv = scratch
    patch_pad = keys.shape[1]

    def clear():
        @pl.loop(0, dk.shape[0])
        def _(at):
            dk[at] = jnp.zeros(dk.shape[1:], F32)
            dv[at] = jnp.zeros(dv.shape[1:], F32)

    pl.when(pl.program_id(0) == 0)(clear)

    def spread(at):
        qs[at] = queries[at].astype(F32) * SCALE
        gs[at] = grads[at].astype(F32)

    band_loop(rows * length, spread)
    lane_head = lane_heads()
    base = pl.program_id(0) * rows

    @pl.loop(0, rows // PAIRED)
    def _(step):
        items, places = [], []
        for row in range(PAIRED):
            row = step * PAIRED + row
            at = pl.ds(pl.multiple_of(row * length, 8), length)
            which = image[base + row]
            keep = box_keep(corners, base + row, (patch_pad, 1), 0)
            for g in range(qs.shape[1] // GROUP):
                lanes = slice(g * GROUP, (g + 1) * GROUP)
                items.append(
                    (
                        spread_heads(qs[at, lanes], lane_head),
                        keys[which, :, lanes],
                        values[which, :, lanes],
                        spread_heads(gs[at, lanes], lane_head),
                        keep,
                    )
                )
                places.append((at, which, lanes))
        for (at, which, lanes), (grad_q, grad_k, grad_v) in zip(places, attend_grad(items)):
            acc[at, lanes] = gather_heads(grad_q, lane_head, length) * SCALE
            dk[which, :, lanes] += grad_k
            dv[which, :, lanes] += grad_v

    def cast(at):
        grad_queries[at] = acc[at].astype(BF16)

    band_loop(rows * length, cast)

    @pl.when(pl.program_id(0) == steps - 1)
    def _():
        half = own.shape[1]

        @pl.loop(0, half)
        def _(at):
            own[0, at] = dk[at].astype(BF16)
            own[1, at] = dv[at].astype(BF16)
            mate[0, at] = dk[half + at].astype(BF16)
            mate[1, at] = dv[half + at].astype(BF16)


def image_kernel(images, patch_count, local, scalars, ins, outs, scratch):
    (core,) = scalars
    piece, piece_mate, patches, proj_weight, ain, ain_mate = ins
    kv_own, kv_mate, patch_grad, weight_grad, sums = outs
    narrow, wide, taken, w1, w2, part, sems, weight_sems = scratch
    parts, span = taken.shape[0], taken.shape[1]
    loads = Loads(
        1,
        weight_sems,
        side_by_side(ain.at[1, 1], ain_mate.at[1, 1], w1, local)
        + side_by_side(ain.at[1, 2], ain_mate.at[1, 2], w2, local),
    )
    arrivals = Loads(
        1, sems, [(patches.at[pl.ds(n * span, span)], taken.at[n]) for n in range(parts)]
    )
    loads.start()
    arrivals.start()
    part[...] = jnp.zeros_like(part)
    own_images, patch_pad = piece.shape[1], piece.shape[2]
    width = w1.shape[0]

    slab = 80

    @pl.loop(0, wide.shape[1] // slab)
    def _(step):
        at = pl.ds(pl.multiple_of(step * slab, slab), slab)
        for lane in range(wide.shape[0]):
            wide[lane, at] = jnp.zeros((slab, LANES), F32)

    loads.wait(0, 1, 2, 3)
    first = core[0] * own_images

    @pl.loop(0, own_images // 2)
    def _(step):
        pair = pl.ds(step * 2, 2)
        halves = []
        for half in (slice(0, local), slice(local, width)):
            swapped = slice(width - half.stop, width - half.start)
            both = piece[:, pair, :, half].astype(F32) + piece_mate[:, pair, :, swapped].astype(F32)
            both = both.astype(BF16)
            halves.append([both[at].reshape(2 * patch_pad, local) for at in range(2)])
        (dk_own, dv_own), (dk_mate, dv_mate) = halves
        rows = pl.ds(pl.multiple_of(step * 2 * patch_pad, 2 * patch_pad), 2 * patch_pad)
        kv_own[rows, :local] = dk_own
        kv_own[rows, local:] = dv_own
        kv_mate[rows, :local] = dk_mate
        kv_mate[rows, local:] = dv_mate
        dk = jnp.concatenate([dk_own, dk_mate], axis=1)
        dv = jnp.concatenate([dv_own, dv_mate], axis=1)
        part[1] += fold(dv.astype(F32))
        for start in range(0, width, GROUP):
            cols = slice(start, start + GROUP)
            grad = dot_nt(dk, w1[cols, :]) + dot_nt(dv, w2[cols, :])
            grad = grad.astype(BF16).astype(F32)
            part[0, :, cols] += fold(grad)
            for at in range(2):
                one = grad[at * patch_pad : at * patch_pad + patch_count]
                which = step * 2 + at
                spot = pl.ds(which, patch_count, stride=own_images)
                split_lanes(narrow, spot, start, one)
                split_lanes(wide, pl.ds(which + first, patch_count, stride=images), start, one)

    for n in range(parts):
        arrivals.wait(n)
        few = slice(n * span * own_images, (n + 1) * span * own_images)
        some = join_lanes(narrow, few).astype(BF16)
        for start in range(0, proj_weight.shape[0], GROUP):
            cols = slice(start, start + GROUP)
            back = dot_nt(some, proj_weight[cols, :]).astype(BF16)
            patch_grad[n * span : (n + 1) * span, :, cols] = back.reshape(span, own_images, GROUP)
        flat = taken[n].reshape(span * images, taken.shape[3])
        grad = join_lanes(wide, slice(n * span * images, (n + 1) * span * images)).astype(BF16)
        product = dot_tn(flat, grad)
        if n == 0:
            weight_grad[...] = product
        else:
            weight_grad[...] += product
    for at in range(2):
        sums[at : at + 1] = jnp.sum(part[at], axis=0, keepdims=True)


def self_grad_kernel(steps, rows, local, length, scalars, ins, outs, scratch):
    lens, where = scalars
    dq2, unit_one, rstd_one, dz_two, q_in, k_in, v_in, ain, ain_mate, aout, aout_mate, gain = ins
    text_grad, do_out, dq2_own, dq2_mate, qkv_own, qkv_mate, sums = outs
    wc, wo, wq, wk, wv, acc, kept, low, low_k, low_v, qs, ks, vs, part, sems = scratch
    total = rows * length
    loads = Loads(
        steps,
        sems,
        side_by_side(ain.at[1, 0], ain_mate.at[1, 0], wc, local)
        + one_above(aout.at[0], aout_mate.at[0], wo, local)
        + side_by_side(ain.at[0, 0], ain_mate.at[0, 0], wq, local)
        + side_by_side(ain.at[0, 1], ain_mate.at[0, 1], wk, local)
        + side_by_side(ain.at[0, 2], ain_mate.at[0, 2], wv, local),
    )
    loads.start()
    part[...] = jnp.zeros_like(part)

    def to_acc(cols, value):
        acc[:, cols] = value

    loads.wait(0, 1)
    by_columns(dq2[...], wc, to_acc, transposed=True)

    def norm_back(at):
        unit = unit_one[at]
        grad = dz_two[at] + acc[at]
        dz = norm_grad(unit, rstd_one[at], gain[0:1], grad)
        kept[at] = dz
        dz_low = dz.astype(BF16)
        low[at] = dz_low
        do_out[at] = dz_low
        qs[at] = q_in[at].astype(F32) * SCALE
        ks[at] = k_in[at].astype(F32)
        vs[at] = v_in[at].astype(F32)
        query = dq2[at]
        dq2_own[at] = query[:, :local]
        dq2_mate[at] = query[:, local:]
        return (
            (0, fold(dz_low.astype(F32))),
            (1, fold(grad * unit)),
            (2, fold(grad)),
            (5, fold(query.astype(F32))),
        )

    band_loop(total, norm_back, part)
    loads.wait(2, 3)
    by_columns(low[...], wo, to_acc, transposed=True)
    lane_head = lane_heads()
    key_index = lax.broadcasted_iota(jnp.int32, (length, 1), 0)
    base = pl.program_id(0) * rows

    @pl.loop(0, rows // PAIRED)
    def _(step):
        items, places = [], []
        for row in range(PAIRED):
            row = step * PAIRED + row
            at = pl.ds(pl.multiple_of(row * length, 8), length)
            keep = key_index < lens[base + row]
            for g in range(qs.shape[1] // GROUP):
                lanes = slice(g * GROUP, (g + 1) * GROUP)
                items.append(
                    (
                        spread_heads(qs[at, lanes], lane_head),
                        ks[at, lanes].astype(BF16),
                        vs[at, lanes].astype(BF16),
                        spread_heads(acc[at, lanes], lane_head),
                        keep,
                    )
                )
                places.append((at, lanes))
        for (at, lanes), (grad_q, grad_k, grad_v) in zip(places, attend_grad(items)):
            qs[at, lanes] = gather_heads(grad_q, lane_head, length) * SCALE
            ks[at, lanes] = grad_k
            vs[at, lanes] = grad_v

    def cast(at):
        sums = []
        for slot, (source, target) in enumerate(((qs, low), (ks, low_k), (vs, low_v))):
            value = source[at].astype(BF16)
            target[at] = value
            qkv_own[at, slot * local : (slot + 1) * local] = value[:, :local]
            qkv_mate[at, slot * local : (slot + 1) * local] = value[:, local:]
            if slot != 1:
                sums.append((3 + slot // 2, fold(value.astype(F32))))
        return sums

    band_loop(total, cast, part)
    loads.wait(4, 5, 6, 7, 8, 9)
    for start in range(0, kept.shape[1], GROUP):
        cols = slice(start, start + GROUP)
        acc[:, cols] = (
            kept[:, cols]
            + dot_nt(low[...], wq[cols, :])
            + dot_nt(low_k[...], wk[cols, :])
            + dot_nt(low_v[...], wv[cols, :])
        )

    for row in range(rows):
        text_grad[where[base + row]] = acc[row * length : (row + 1) * length].astype(BF16)
    for at in range(8):
        sums[0, at : at + 1] = jnp.sum(part[at], axis=0, keepdims=True)


def join_kernel(scalars, ins, outs, scratch):
    (out,) = outs
    start = 0
    for stay, got in zip(ins[::2], ins[1::2]):
        for at in range(0, out.shape[0], 96):
            rows = slice(at, at + 96)
            out[rows, start : start + stay.shape[1]] = add_low(stay[rows], got[rows])
        start += stay.shape[1]


def add_low(left, right):
    return (left.astype(F32) + right.astype(F32)).astype(BF16)


def pack_kernel(local, hidden, scalars, ins, outs, scratch):
    (core,) = scalars
    feed, up, self_, image = ins
    feed_sum = jnp.sum(feed[...], axis=0)
    self_sum = jnp.sum(self_[...], axis=0)
    up_sum = jnp.sum(up[...], axis=0)
    common = [(0, 0), (1, 3), (1, 0), (0, 1), (1, 4), (1, 1), (0, 2), (1, 5), (1, 2)]
    even = core[0] == 0
    for out, mine in zip(outs, (True, False)):
        out[...] = jnp.zeros_like(out)
        at = 0
        for which, row in common:
            source = feed_sum if which else self_sum
            for half in range(2):
                out[at : at + 1] = source[row : row + 1, half * local : (half + 1) * local]
                at += 1
        lanes = slice(0, local) if mine else slice(local, 2 * local)
        for row in (3, 4, 5):
            out[at : at + 1] = self_sum[row : row + 1, lanes]
            at += 1
        out[at : at + 1] = image[1:2, lanes]
        at += 1
        half = 0 if mine else 1
        for start in range(0, hidden, local):
            out[at : at + 1] = up_sum[half : half + 1, start : start + local]
            at += 1
        low, high = image[0:1, :local], image[0:1, local:]
        out[at : at + 1] = jnp.where(even == mine, low, high)


def halve_kernel(rows, length, scalars, ins, outs, scratch):
    core, where = scalars
    (tall,) = scratch

    def put(at, both):
        split_lanes(tall, at, 0, both)

    row_pairs(ins[0], where, 0, rows, length, put)
    half = length // 2
    for out, first in zip(outs, (core[0] * half, (1 - core[0]) * half)):
        for token in range(half):
            out[token] = join_lanes(
                tall, pl.ds(first + token, rows, stride=length)
            ).astype(BF16)


def place_kernel(scalars, ins, outs, scratch):
    own, mate, place = ins
    (out,) = outs
    count, slots = out.shape[1], own.shape[1]
    index = lax.broadcasted_iota(jnp.int32, (count, slots), 1)
    from_own = jnp.where(place[...] == index, 1.0, 0.0).astype(BF16)
    from_mate = jnp.where(place[...] == index + slots, 1.0, 0.0).astype(BF16)
    for token in range(out.shape[0]):
        out[token] = (dot(from_own, own[token]) + dot(from_mate, mate[token])).astype(BF16)


def body(
    text,
    cotangent,
    lengths,
    box_corners,
    box_counts,
    region_box,
    patches,
    proj_weight,
    proj_bias,
    attention_in,
    attention_bias,
    attention_out,
    output_bias,
    norm_gain,
    norm_bias,
    up_weight,
    up_bias,
    down_weight,
):
    rows, length, width = text.shape
    images, patch_count, vision = patches.shape
    local = attention_in.shape[-1]
    hidden = up_weight.shape[-1]
    devices = lax.axis_size("dp")
    me, core = lax.axis_index("dp"), lax.axis_index("mp")
    pair = -(-rows // devices)
    each, odd = pair // 2, pair % 2
    deep = each + odd
    slots = devices * each + devices // 2 * odd
    patch_pad = -(-patch_count // 16) * 16
    own_images = images // 2
    step_rows = 12 if slots % 12 == 0 else 8
    steps = slots // step_rows
    tokens = step_rows * length
    all_tokens = slots * length
    full = slots * 2 == rows
    core_scalar = core.astype(jnp.int32).reshape(1)

    def mate(value):
        return lax.ppermute(value, "mp", [(0, 1), (1, 0)])

    def tie(*values):
        return lax.optimization_barrier(values)

    def exchange(value):
        return lax.all_to_all(value, "dp", split_axis=0, concat_axis=0, tiled=True)

    ain_mate = mate(attention_in)
    bias_mate = mate(attention_bias)
    aout_mate = mate(attention_out)
    up_bias_own = up_bias.reshape(1, hidden)
    up_bias_mate = mate(up_bias_own)
    up_mate = mate(up_weight)
    down_mate = mate(down_weight)

    number = jnp.arange(rows, dtype=jnp.int32)
    target = region_box // rows
    earlier = (target[:, None] == target[None, :]) & (number[None, :] < number[:, None])
    nth = jnp.sum(earlier.astype(jnp.int32), axis=1)
    even_part = nth < 2 * each
    row_core = jnp.where(even_part, nth // max(each, 1), (target ^ me) & 1)
    depth = jnp.where(even_part, nth % max(each, 1), each)
    spot = jnp.arange(devices * deep, dtype=jnp.int32)
    hit = (spot[:, None] == (target * deep + depth)[None, :]) & (row_core == core)[None, :]
    source = jnp.sum(jnp.where(hit, number[None, :], 0), axis=1)
    slot = jnp.where(even_part, target * each + depth, devices * each + (target >> 1))
    place = jnp.where(row_core == core, slot, slot + slots)[:, None]
    order = jnp.arange(slots, dtype=jnp.int32)
    late = order - devices * each
    where = jnp.where(
        late < 0,
        order // max(each, 1) * deep + order % max(each, 1),
        (2 * late + ((me & 1) ^ core)) * deep + each,
    )
    meta = jnp.concatenate(
        [(region_box % rows)[:, None], lengths[:, None], box_corners], axis=1
    )
    meta_out = jnp.sum(jnp.where(hit[:, :, None], meta[None], 0), axis=1)
    if not full:
        empty = jnp.array([0, 1, 0, 1, 0, 1], jnp.int32)
        meta_out = jnp.where(jnp.any(hit, axis=1)[:, None], meta_out, empty[None])
    arrived = exchange(meta_out)[where]
    ends = jnp.cumsum(box_counts[0])
    image = jnp.sum((ends[None, :] <= arrived[:, 0:1]).astype(jnp.int32), axis=1)
    image = (image + own_images * core) % images
    lens = arrived[:, 1]
    corners = arrived[:, 2:].reshape(-1)

    block_shape = (devices * deep, length, width)
    if full:
        x_out, upstream_out = run(
            partial(fetch_kernel, devices * deep),
            1,
            [source],
            [(text, ANY), (cotangent, ANY)],
            [(block_shape, BF16, whole_spec(block_shape))] * 2,
            [pltpu.SemaphoreType.DMA((2 * devices * deep,))],
            0,
        )
    else:
        valid = jnp.any(hit, axis=1)[:, None, None]
        x_out = jnp.where(valid, text[source], 0)
        upstream_out = jnp.where(valid, cotangent[source], 0)
    x_in = exchange(x_out)

    patches, aout_mate, image, corners, lens = tie(patches, aout_mate, image, corners, lens)
    by_patch = jnp.transpose(patches, (1, 0, 2))
    parts = next(n for n in (5, 4, 3, 2, 1) if patch_count % n == 0)
    weight_scratch = pltpu.VMEM((width, width), BF16)

    def slabs(count):
        return pltpu.VMEM((width // LANES, count, LANES), F32)

    patch_scratch = pltpu.VMEM((parts, patch_count // parts, images, vision), BF16)
    image_shape = (images, patch_pad, width)
    proj, keys, values = run(
        partial(project_kernel, images, own_images, patch_pad, patch_count, local),
        1,
        [core_scalar],
        [
            (by_patch, ANY),
            (proj_weight, whole_spec(proj_weight.shape)),
            (proj_bias.reshape(1, width), whole_spec((1, width))),
            (attention_in, ANY),
            (ain_mate, ANY),
            (attention_bias, whole_spec(attention_bias.shape)),
            (bias_mate, whole_spec(bias_mate.shape)),
        ],
        [((own_images,) + image_shape[1:], BF16, whole_spec((own_images,) + image_shape[1:]))]
        + [(image_shape, BF16, whole_spec(image_shape))] * 2,
        [
            patch_scratch,
            slabs(patch_count * images),
            weight_scratch,
            weight_scratch,
            pltpu.SemaphoreType.DMA((parts,)),
            pltpu.SemaphoreType.DMA((4,)),
        ],
        2 * images * patch_pad * width * (vision + 2 * width),
    )

    upstream_out, proj, keys, values = tie(upstream_out, proj, keys, values)
    upstream_in = exchange(upstream_out)

    def token_in(value):
        return (value, rows_spec((tokens, value.shape[1]), 0))

    def token_out(cols, dtype):
        return ((all_tokens, cols), dtype, rows_spec((tokens, cols), 0))

    block_out = (block_shape, BF16, whole_spec(block_shape))

    def f32_tokens(cols):
        return pltpu.VMEM((tokens, cols), F32)

    def low_tokens(cols):
        return pltpu.VMEM((tokens, cols), BF16)

    def whole(value):
        return (value, whole_spec(value.shape))

    attention_flops = 4 * 4 * all_tokens * width * 64

    x, unit_one, q_self, k_self, v_self, att_own, att_mate, self_low, queries, rstd_one = run(
        partial(self_kernel, steps, step_rows, local, length),
        steps,
        [lens, where],
        [
            whole(x_in),
            (attention_in, ANY),
            (ain_mate, ANY),
            (attention_out, ANY),
            (aout_mate, ANY),
            whole(attention_bias),
            whole(bias_mate),
            whole(output_bias),
            whole(norm_gain),
            whole(norm_bias),
        ],
        [token_out(width, BF16), token_out(width, F32)]
        + [token_out(width, BF16)] * 3
        + [token_out(local, BF16)] * 2
        + [token_out(width, BF16)] * 2
        + [token_out(1, F32)],
        [weight_scratch] * 5
        + [f32_tokens(width)] * 4
        + [low_tokens(width), pltpu.SemaphoreType.DMA((10,))],
        2 * all_tokens * width * width * 5 + attention_flops,
    )

    (attended,) = run(
        partial(cross_kernel, step_rows, length),
        steps,
        [image, corners],
        [token_in(queries), whole(keys), whole(values)],
        [token_out(width, BF16)],
        [f32_tokens(width)] * 2,
        attention_flops * 4,
    )

    result = run(
        partial(feed_kernel, steps, step_rows, local, hidden, length),
        steps,
        [where],
        [
            whole(upstream_in),
            token_in(attended),
            token_in(unit_one),
            (attention_out, ANY),
            (aout_mate, ANY),
            (up_weight, ANY),
            (up_mate, ANY),
            (down_weight, ANY),
            (down_mate, ANY),
            whole(output_bias),
            whole(norm_gain),
            whole(norm_bias),
            whole(up_bias_own),
            whole(up_bias_mate),
        ],
        [block_out]
        + [token_out(width, BF16)] * 3
        + [token_out(width, F32)]
        + [token_out(local, BF16)] * 2
        + [token_out(hidden, BF16)] * 4
        + [
            token_out(width, BF16),
            ((steps, 8, width), F32, rows_spec((1, 8, width), 0)),
            ((steps, 2, hidden), F32, rows_spec((1, 2, hidden), 0)),
        ],
        [weight_scratch]
        + [
            pltpu.VMEM((hidden // TILE, width, 2 * TILE), BF16),
            pltpu.VMEM((hidden // TILE, 2 * TILE, width), BF16),
        ]
        + [f32_tokens(width)] * 3
        + [f32_tokens(1), low_tokens(width), low_tokens(width)]
        + [f32_tokens(2 * TILE)] * 2
        + [pltpu.VMEM((hidden // TILE, tokens, 2 * TILE), F32)]
        + [pltpu.VMEM((8, 8, width), F32), pltpu.VMEM((2, 8, hidden), F32)]
        + [pltpu.SemaphoreType.DMA((2 + 4 * hidden // TILE,))],
        2 * all_tokens * width * (2 * width + 8 * hidden),
    )
    merged_out, cross_low, grad_ffn, grad_cross, dz_two, a_own, a_mate = result[:7]
    g_own, g_mate, du_own, du_mate, grad_att, feed_sums, up_sums = result[7:]

    bits = devices.bit_length() - 1

    def partner_bits(value, mask):
        return lax.ppermute(value, "dp", [(d, d ^ mask) for d in range(devices)])

    def opened(value):
        return value.reshape((2,) * bits + (value.shape[0] // devices, value.shape[1]))

    def swap(value, axis, bit):
        mine = (me >> bit) & 1
        away = lax.dynamic_index_in_dim(value, 1 - mine, axis, keepdims=False)
        stay = lax.dynamic_index_in_dim(value, mine, axis, keepdims=False)
        return stay, partner_bits(away, 1 << bit)

    def first_swaps(by_x, by_y):
        return swap(opened(by_x), bits - 1, 0) + swap(opened(by_y), bits - 2, 1)

    def second_swaps(stay_x, got_x, stay_y, got_y):
        return swap(add(stay_x, got_x), bits - 2, 1) + swap(add(stay_y, got_y), bits - 2, 0)

    def add(stay, got):
        return add_low(stay, got)

    def last_parts(values, after):
        count = values[0].size // values[0].shape[-1]
        shape = (count, sum(value.shape[-1] for value in values[::2]))
        values = [value.reshape(count, value.shape[-1]) for value in values]
        (joined,) = run(
            join_kernel,
            1,
            [],
            [whole(value) for value in values],
            [(shape, BF16, whole_spec(shape))],
            [],
            0,
            after,
        )
        return joined.reshape(devices // 4, count // (devices // 4), shape[1])

    def last_sum(both, *widths):
        groups = [[low + 4 * n for n in range(devices // 4)] for low in range(4)]
        both = lax.all_to_all(
            both, "dp", split_axis=0, concat_axis=0, axis_index_groups=groups, tiled=True
        )
        total = jnp.sum(both.astype(F32), axis=0)
        ends = [sum(widths[:n]) for n in range(len(widths) + 1)]
        return [total[:, start:stop] for start, stop in zip(ends, ends[1:])]

    def low_tn(left, right):
        return dot_tn(left, right).astype(BF16)

    merged_in = exchange(merged_out)
    up_away, down_away = low_tn(cross_low, du_mate), low_tn(grad_ffn, g_mate)
    grad_att, queries, up_away, down_away = tie(grad_att, queries, up_away, down_away)
    up_got, down_got = mate(up_away), mate(down_away)

    half_shape = (2, own_images, patch_pad, width)
    image_acc = pltpu.VMEM(image_shape, F32)
    piece, piece_out, grad_queries = run(
        partial(cross_grad_kernel, steps, step_rows, length),
        steps,
        [image, corners],
        [token_in(queries), token_in(grad_att), whole(keys), whole(values)],
        [(half_shape, BF16, whole_spec(half_shape))] * 2 + [token_out(width, BF16)],
        [f32_tokens(width)] * 3 + [image_acc] * 2,
        attention_flops * 12,
    )
    piece_mate = mate(piece_out)

    up_part = (dot_tn(cross_low, du_own) + up_got.astype(F32)).astype(BF16)
    down_part = (dot_tn(grad_ffn, g_own) + down_got.astype(F32)).astype(BF16)
    grad_queries, up_part, down_part = tie(grad_queries, up_part, down_part)
    feed_stage = first_swaps(up_part, down_part)

    result = run(
        partial(self_grad_kernel, steps, step_rows, local, length),
        steps,
        [lens, where],
        [
            token_in(grad_queries),
            token_in(unit_one),
            token_in(rstd_one),
            token_in(dz_two),
            token_in(q_self),
            token_in(k_self),
            token_in(v_self),
            (attention_in, ANY),
            (ain_mate, ANY),
            (attention_out, ANY),
            (aout_mate, ANY),
            whole(norm_gain),
        ],
        [block_out]
        + [token_out(width, BF16)]
        + [token_out(local, BF16)] * 2
        + [token_out(3 * local, BF16)] * 2
        + [((steps, 8, width), F32, rows_spec((1, 8, width), 0))],
        [weight_scratch] * 5
        + [f32_tokens(width)] * 2
        + [low_tokens(width)] * 3
        + [f32_tokens(width)] * 3
        + [pltpu.VMEM((8, 8, width), F32), pltpu.SemaphoreType.DMA((10,))],
        2 * all_tokens * width * width * 5 + attention_flops * 2,
    )
    text_out, grad_self, dq_own, dq_mate, qkv_own, qkv_mate, self_sums = result
    text_in = exchange(text_out)

    token_shape = (length // 2, slots, width)
    final_shape = (length // 2, rows, width)

    def halves(value, after):
        own, away = run(
            partial(halve_kernel, slots, length),
            1,
            [core_scalar, where],
            [whole(value)],
            [(token_shape, BF16, whole_spec(token_shape))] * 2,
            [slabs(all_tokens)],
            0,
            after,
        )
        return own, mate(away)

    def placed(own, got, after):
        (out,) = run(
            place_kernel,
            1,
            [],
            [whole(own), whole(got), whole(place)],
            [(final_shape, BF16, whole_spec(final_shape))],
            [],
            0,
            after,
        )
        return out

    self_away = jnp.concatenate(
        [
            low_tn(x, qkv_mate),
            low_tn(grad_self, att_mate),
            low_tn(grad_cross, a_mate),
            low_tn(self_low, dq_mate),
        ],
        axis=1,
    )
    self_got = mate(self_away)
    feed_stage = tie(self_away, *feed_stage)[1:]
    feed_stage = second_swaps(*feed_stage)
    self_own = jnp.concatenate(
        [
            dot_tn(x, qkv_own),
            dot_tn(grad_self, att_own),
            dot_tn(grad_cross, a_own),
            dot_tn(self_low, dq_own),
        ],
        axis=1,
    )
    self_part = (self_own + self_got.astype(F32)).astype(BF16)
    half_width = self_part.shape[1] // 2
    self_stage = first_swaps(self_part[:, :half_width], self_part[:, half_width:])
    merged_own, merged_got = halves(merged_in, [self_part])

    flat_images = own_images * patch_pad
    patch_grad_shape = (patch_count, own_images, vision)
    kv_own, kv_mate, patch_grad, proj_weight_sum, image_sums = run(
        partial(image_kernel, images, patch_count, local),
        1,
        [core_scalar],
        [
            whole(piece),
            whole(piece_mate),
            (by_patch, ANY),
            whole(proj_weight),
            (attention_in, ANY),
            (ain_mate, ANY),
        ],
        [
            ((flat_images, width), BF16, whole_spec((flat_images, width))),
            ((flat_images, width), BF16, whole_spec((flat_images, width))),
            (patch_grad_shape, BF16, whole_spec(patch_grad_shape)),
            ((vision, width), F32, whole_spec((vision, width))),
            ((8, width), F32, whole_spec((8, width))),
        ],
        [
            slabs(patch_count * own_images),
            slabs(patch_count * images),
            patch_scratch,
            weight_scratch,
            weight_scratch,
            pltpu.VMEM((2, 8, width), F32),
            pltpu.SemaphoreType.DMA((parts,)),
            pltpu.SemaphoreType.DMA((4,)),
        ],
        2 * flat_images * width * (2 * width + 2 * vision),
        [self_part],
    )

    self_got_x, self_got_y = self_stage[1], self_stage[3]
    self_stage = second_swaps(*self_stage)
    kv_low = proj.reshape(flat_images, width)
    kv_away = low_tn(kv_low, kv_mate)
    kv_got = mate(kv_away)
    proj_away = lax.dynamic_slice_in_dim(proj_weight_sum, (1 - core) * local, local, 1)
    proj_got = mate(proj_away.astype(BF16))
    kv_part = (dot_tn(kv_low, kv_own) + kv_got.astype(F32)).astype(BF16)
    proj_own = lax.dynamic_slice_in_dim(proj_weight_sum, core * local, local, 1)
    proj_part = (proj_own + proj_got.astype(F32)).astype(BF16)
    proj_part = proj_part.reshape(width, vision * local // width)
    image_stage = first_swaps(kv_part, proj_part)
    image_stage = second_swaps(*image_stage)
    text_own, text_got = halves(text_in, [kv_own])
    up_grad, down_grad = last_sum(last_parts(feed_stage, [text_own]), hidden, hidden)
    merged_final = placed(merged_own, merged_got, [kv_part])
    text_final = placed(text_own, text_got, [kv_part, proj_part])

    lines = 23 + hidden // local
    packed_shape = (-(-lines // 8) * 8, local)
    small, small_out = run(
        partial(pack_kernel, local, hidden),
        1,
        [core_scalar],
        [whole(feed_sums), whole(up_sums), whole(self_sums), whole(image_sums)],
        [(packed_shape, F32, whole_spec(packed_shape))] * 2,
        [],
        0,
        [kv_part, proj_part, self_got_x, self_got_y],
    )
    small = small + mate(small_out)
    for bit in range(bits):
        small = small + partner_bits(small, 1 << bit)
    self_one, self_two, kv_grad, proj_grad = last_sum(
        last_parts(self_stage + image_stage, [merged_final, text_final, small, up_grad]),
        half_width,
        half_width,
        width,
        vision * local // width,
    )
    proj_grad = proj_grad.reshape(vision // devices, local)
    common = small[:18].reshape(3, 3, width)
    bias_grad = small[18:22].reshape(2, 2, local)
    up_bias_grad = small[22 : 22 + hidden // local].reshape(hidden)
    proj_bias_grad = small[22 + hidden // local]

    ready = [self_one[:, at * local : (at + 1) * local] for at in range(3)]
    out_self, out_cross, query_cross = [
        self_two[:, at * local : (at + 1) * local] for at in range(3)
    ]
    in_grad = jnp.stack(
        ready + [query_cross, kv_grad[:, :local], kv_grad[:, local:]]
    ).reshape(2, 3, width // devices, local)
    out_grad = jnp.stack([out_self.T, out_cross.T])

    return (
        jnp.transpose(merged_final, (1, 0, 2)),
        jnp.transpose(text_final, (1, 0, 2)),
        jnp.transpose(patch_grad, (1, 0, 2)),
        proj_grad,
        proj_bias_grad,
        in_grad,
        bias_grad,
        out_grad,
        common[0],
        common[1],
        common[2],
        up_grad,
        up_bias_grad,
        down_grad.T,
    )


def solution(mesh):
    placed = (
        P("dp", None, None),
        P("dp", None, None),
        P("dp"),
        P("dp", None),
        P("dp", None),
        P("dp"),
        P("dp", None, None),
        P(),
        P(),
        P(None, None, None, "mp"),
        P(None, None, "mp"),
        P(None, "mp", None),
        P(),
        P(),
        P(),
        P(None, "mp"),
        P("mp"),
        P("mp", None),
    )
    return jax.shard_map(
        body,
        mesh=mesh,
        in_specs=placed,
        out_specs=(
            P("dp", "mp", None),
            P("dp", "mp", None),
            P(("dp", "mp"), None, None),
            P("dp", "mp"),
            P("mp"),
            P(None, None, "dp", "mp"),
            P(None, None, "mp"),
            P(None, "mp", "dp"),
            P(),
            P(),
            P(),
            P("dp", "mp"),
            P("mp"),
            P("mp", "dp"),
        ),
        check_vma=False,
    )
```

```python
import math
from functools import partial

import jax
import jax.numpy as jnp
from jax import lax
from jax.experimental import pallas as pl
from jax.experimental.pallas import tpu as pltpu
from jax.sharding import PartitionSpec as P

HEAD_DIM = 64
GRID = 12
EPS = 1e-12
NEG = -1e30
SCALE = HEAD_DIM ** (-0.5)

F32 = jnp.float32
BF16 = jnp.bfloat16

GROUP = 4 * HEAD_DIM
BAND = 32
BANDS = 5
LANES = 128
TILE = 256
PAIRED = 4
VMEM_LIMIT = 58 << 20


def dot(left, right):
    return lax.dot_general(left, right, (((1,), (0,)), ((), ())), preferred_element_type=F32)


def dot_nt(left, right):
    return lax.dot_general(left, right, (((1,), (1,)), ((), ())), preferred_element_type=F32)


def dot_tn(left, right):
    return lax.dot_general(left, right, (((0,), (0,)), ((), ())), preferred_element_type=F32)


def rows_spec(block, offset):
    rank = len(block)
    return pl.BlockSpec(block, lambda s, *_: (s + offset,) + (0,) * (rank - 1))


def whole_spec(shape):
    rank = len(shape)
    return pl.BlockSpec(shape, lambda s, *_: (0,) * rank, pipeline_mode=pl.Buffered(1))


ANY = pl.BlockSpec(memory_space=pl.ANY)


def run(body, steps, scalars, ins, outs, scratch, flops, after=()):
    ns, ni, no = len(scalars), len(ins), len(outs)

    def kernel(*refs):
        rest = refs[ns + ni + len(after) :]
        body(refs[:ns], refs[ns : ns + ni], rest[:no], rest[no:])

    moved = sum(math.prod(a.shape) * a.dtype.itemsize for a, _ in ins)
    ins = list(ins) + [(array, ANY) for array in after]
    moved += sum(math.prod(shape) * jnp.dtype(dtype).itemsize for shape, dtype, _ in outs)
    return pl.pallas_call(
        kernel,
        grid_spec=pltpu.PrefetchScalarGridSpec(
            num_scalar_prefetch=ns,
            grid=(steps,),
            in_specs=[spec for _, spec in ins],
            out_specs=[spec for _, _, spec in outs],
            scratch_shapes=scratch,
        ),
        out_shape=[jax.ShapeDtypeStruct(shape, dtype) for shape, dtype, _ in outs],
        compiler_params=pltpu.CompilerParams(
            dimension_semantics=("arbitrary",), vmem_limit_bytes=VMEM_LIMIT
        ),
        cost_estimate=pl.CostEstimate(flops=flops, bytes_accessed=moved, transcendentals=0),
    )(*scalars, *[array for array, _ in ins])


class Loads:
    def __init__(self, steps, sems, pairs):
        self.steps = steps
        self.copies = [
            pltpu.make_async_copy(source, target, sems.at[at])
            for at, (source, target) in enumerate(pairs)
        ]

    def first(self, action):
        if self.steps == 1:
            action()
        else:
            pl.when(pl.program_id(0) == 0)(action)

    def start(self):
        self.first(lambda: [copy.start() for copy in self.copies] and None)

    def wait(self, *which):
        self.first(lambda: [self.copies[at].wait() for at in which] and None)


def side_by_side(own, mate, target, width):
    return [(own, target.at[:, pl.ds(0, width)]), (mate, target.at[:, pl.ds(width, width)])]


def one_above(own, mate, target, height):
    return [(own, target.at[pl.ds(0, height)]), (mate, target.at[pl.ds(height, height)])]


def moments(z):
    center = z - jnp.mean(z, axis=-1, keepdims=True)
    rstd = lax.rsqrt(jnp.mean(center * center, axis=-1, keepdims=True) + EPS)
    return center * rstd, rstd


def norm_grad(unit, rstd, gain, grad):
    inner = grad * gain
    return rstd * (
        inner
        - jnp.mean(inner, axis=-1, keepdims=True)
        - unit * jnp.mean(inner * unit, axis=-1, keepdims=True)
    )


def fold(block):
    return jnp.sum(block.reshape(block.shape[0] // 8, 8, block.shape[1]), axis=0)


def gelu(u):
    bell = jnp.exp2(u * u * (-0.5 / math.log(2.0)))
    t = 1.0 / (1.0 + (0.3275911 * 0.5**0.5) * jnp.abs(u))
    poly = t * (
        0.5 * 0.254829592
        + t
        * (
            0.5 * -0.284496736
            + t * (0.5 * 1.421413741 + t * (0.5 * -1.453152027 + t * (0.5 * 1.061405429)))
        )
    )
    tail = poly * bell
    phi = jnp.where(u >= 0.0, 1.0 - tail, tail)
    return u * phi, phi + u * (bell * (1.0 / math.sqrt(2.0 * math.pi)))


def spread_heads(block, lane_head):
    parts = [jnp.where(lane_head == h, block, 0.0) for h in range(GROUP // HEAD_DIM)]
    return jnp.concatenate(parts, axis=0).astype(BF16)


def gather_heads(block, lane_head, tokens):
    total = jnp.where(lane_head == 0, block[0:tokens], 0.0)
    for h in range(1, GROUP // HEAD_DIM):
        total = jnp.where(lane_head == h, block[h * tokens : (h + 1) * tokens], total)
    return total


def lane_heads():
    return lax.broadcasted_iota(jnp.int32, (1, GROUP), 1) // HEAD_DIM


def attend(items):
    scores = [dot_nt(qm, kb) for qm, kb, vb, keep in items]
    weights = []
    for score, (qm, kb, vb, keep) in zip(scores, items):
        score = jnp.where(keep, score, NEG)
        top = jnp.max(score, axis=1, keepdims=True)
        weight = jnp.exp(score - top)
        weight = weight * (1.0 / jnp.sum(weight, axis=1, keepdims=True))
        weights.append(weight.astype(BF16))
    return [dot(weight, vb) for weight, (qm, kb, vb, keep) in zip(weights, items)]


def attend_grad(items):
    scores = [dot_nt(kb, qm) for qm, kb, vb, dom, keep in items]
    grads = [dot_nt(vb, dom) for qm, kb, vb, dom, keep in items]
    middle = []
    for score, grad, (qm, kb, vb, dom, keep) in zip(scores, grads, items):
        score = jnp.where(keep, score, NEG)
        top = jnp.max(score, axis=0, keepdims=True)
        weight = jnp.exp(score - top)
        weight = weight * (1.0 / jnp.sum(weight, axis=0, keepdims=True))
        inner = jnp.sum(weight * grad, axis=0, keepdims=True)
        grad_score = weight * (grad - inner)
        middle.append(
            (weight.astype(BF16), grad_score.astype(BF16), jnp.transpose(grad_score).astype(BF16))
        )
    results = []
    for (weight, grad_score, turned), (qm, kb, vb, dom, keep) in zip(middle, items):
        results.append((dot(turned, kb), dot(grad_score, qm), dot(weight, dom)))
    return results


def box_keep(corners, slot, shape, axis):
    index = lax.broadcasted_iota(jnp.int32, shape, axis) - 1
    grid_row = (index * 2731) >> 15
    grid_col = index - grid_row * GRID
    inside = (grid_col >= corners[slot * 4]) & (grid_col < corners[slot * 4 + 1])
    inside = inside & (grid_row >= corners[slot * 4 + 2]) & (grid_row < corners[slot * 4 + 3])
    return (inside & (index >= 0)) | (index < 0)


def band_loop(total, body, part=None):
    @pl.loop(0, total // (BAND * BANDS))
    def _(step):
        sums = []
        for band in range(BANDS):
            start = pl.multiple_of(step * (BAND * BANDS) + band * BAND, BAND)
            folded = body(pl.ds(start, BAND))
            if folded is not None:
                sums.append(folded)
        for terms in zip(*sums):
            at = terms[0][0]
            part[at] += sum(value for _, value in terms[1:]) + terms[0][1]


def by_columns(left, weight, finish, transposed=False):
    count = weight.shape[0] if transposed else weight.shape[1]
    for start in range(0, count, GROUP):
        cols = slice(start, start + GROUP)
        value = dot_nt(left, weight[cols, :]) if transposed else dot(left, weight[:, cols])
        finish(cols, value)


def both_halves(own, mate, at):
    return jnp.concatenate([own[at[0], at[1] : at[1] + 1], mate[at[0], at[1] : at[1] + 1]], axis=1)


def row_pairs(source, where, first, count, length, finish):
    for at in range(0, count, 2):
        both = [source[where[first + at + n]].astype(F32) for n in range(2)]
        finish(slice(at * length, (at + 2) * length), jnp.concatenate(both, axis=0))


def split_lanes(target, rows, start, value):
    for lane in range(0, value.shape[1], LANES):
        target[(start + lane) // LANES, rows, :] = value[:, lane : lane + LANES]


def join_lanes(source, rows):
    return jnp.concatenate([source[lane, rows, :] for lane in range(source.shape[0])], axis=1)


def fetch_kernel(count, scalars, ins, outs, scratch):
    (source,) = scalars
    (sems,) = scratch
    copies = [
        pltpu.make_async_copy(table.at[source[at]], out.at[at], sems.at[which * count + at])
        for which, (table, out) in enumerate(zip(ins, outs))
        for at in range(count)
    ]
    for copy in copies:
        copy.start()
    for copy in copies:
        copy.wait()


def project_kernel(images, own_images, patch_pad, patch_count, local, scalars, ins, outs, scratch):
    (core,) = scalars
    patches, proj_weight, proj_bias, ain, ain_mate, bias_own, bias_mate = ins
    proj, keys, values = outs
    taken, raw, w1, w2, sems, weight_sems = scratch
    loads = Loads(
        1,
        weight_sems,
        side_by_side(ain.at[1, 1], ain_mate.at[1, 1], w1, local)
        + side_by_side(ain.at[1, 2], ain_mate.at[1, 2], w2, local),
    )
    parts, span = taken.shape[0], taken.shape[1]
    arrivals = Loads(
        1, sems, [(patches.at[pl.ds(n * span, span)], taken.at[n]) for n in range(parts)]
    )
    arrivals.start()
    loads.start()
    rows = span * images
    width = raw.shape[0] * LANES
    for n in range(parts):
        arrivals.wait(n)
        flat = taken[n].reshape(rows, taken.shape[3])
        for start in range(0, width, GROUP):
            cols = slice(start, start + GROUP)
            split_lanes(
                raw,
                slice(n * rows, (n + 1) * rows),
                start,
                dot(flat, proj_weight[:, cols]) + proj_bias[:, cols],
            )
    loads.wait(0, 1, 2, 3)
    bias = both_halves(bias_own, bias_mate, (1, 1))
    first = core[0] * own_images
    rest = jnp.zeros((patch_pad - patch_count, width), F32)

    group = 4

    @pl.loop(0, images // group)
    def _(step):
        both = []
        for at in range(group):
            which = lax.rem(step * group + at + first, images)
            own = jnp.concatenate(
                [
                    raw[lane, pl.ds(which, patch_count, stride=images), :]
                    for lane in range(raw.shape[0])
                ],
                axis=1,
            )
            both.append(jnp.concatenate([own, rest], axis=0))
        low = jnp.concatenate(both, axis=0).astype(BF16)
        some = pl.ds(step * group, group)

        @pl.when(step < own_images // group)
        def _():
            proj[some] = low.reshape(group, patch_pad, width)

        shape = (group, patch_pad, GROUP)
        for start in range(0, width, GROUP):
            cols = slice(start, start + GROUP)
            keys[some, :, cols] = dot(low, w1[:, cols]).astype(BF16).reshape(shape)
            values[some, :, cols] = (
                (dot(low, w2[:, cols]) + bias[:, cols]).astype(BF16).reshape(shape)
            )


def self_kernel(steps, rows, local, length, scalars, ins, outs, scratch):
    lens, where = scalars
    x_in, ain, ain_mate, aout, aout_mate, bias_own, bias_mate, out_bias, gain, shift = ins
    x_out, unit_one, q_out, k_out, v_out, att_own, att_mate, low_out, cross_q, rstd_one = outs
    wq, wk, wv, wo, wc, qs, ks, vs, acc, low, sems = scratch
    total = rows * length
    loads = Loads(
        steps,
        sems,
        side_by_side(ain.at[0, 0], ain_mate.at[0, 0], wq, local)
        + side_by_side(ain.at[0, 1], ain_mate.at[0, 1], wk, local)
        + side_by_side(ain.at[0, 2], ain_mate.at[0, 2], wv, local)
        + one_above(aout.at[0], aout_mate.at[0], wo, local)
        + side_by_side(ain.at[1, 0], ain_mate.at[1, 0], wc, local),
    )
    loads.start()
    bias_q = both_halves(bias_own, bias_mate, (0, 0))
    bias_v = both_halves(bias_own, bias_mate, (0, 1))
    bias_c = both_halves(bias_own, bias_mate, (1, 0))

    def put(at, both):
        x_out[at] = both.astype(BF16)

    base = pl.program_id(0) * rows
    row_pairs(x_in, where, base, rows, length, put)
    xb = x_out[...]

    def keep_q(cols, value):
        value = (value + bias_q[:, cols]).astype(BF16)
        q_out[:, cols] = value
        qs[:, cols] = value.astype(F32) * SCALE

    def keep_k(cols, value):
        value = value.astype(BF16)
        k_out[:, cols] = value
        ks[:, cols] = value.astype(F32)

    def keep_v(cols, value):
        value = (value + bias_v[:, cols]).astype(BF16)
        v_out[:, cols] = value
        vs[:, cols] = value.astype(F32)

    loads.wait(0, 1)
    by_columns(xb, wq, keep_q)
    loads.wait(2, 3)
    by_columns(xb, wk, keep_k)
    loads.wait(4, 5)
    by_columns(xb, wv, keep_v)
    lane_head = lane_heads()
    key_index = lax.broadcasted_iota(jnp.int32, (1, length), 1)

    @pl.loop(0, rows // PAIRED)
    def _(step):
        items, places = [], []
        for row in range(PAIRED):
            row = step * PAIRED + row
            at = pl.ds(pl.multiple_of(row * length, 8), length)
            keep = key_index < lens[base + row]
            for g in range(qs.shape[1] // GROUP):
                lanes = slice(g * GROUP, (g + 1) * GROUP)
                items.append(
                    (
                        spread_heads(qs[at, lanes], lane_head),
                        ks[at, lanes].astype(BF16),
                        vs[at, lanes].astype(BF16),
                        keep,
                    )
                )
                places.append((at, lanes))
        for (at, lanes), result in zip(places, attend(items)):
            acc[at, lanes] = gather_heads(result, lane_head, length)

    def cast(at):
        value = acc[at].astype(BF16)
        low[at] = value
        att_own[at] = value[:, :local]
        att_mate[at] = value[:, local:]

    def to_acc(cols, value):
        acc[:, cols] = value

    band_loop(total, cast)
    loads.wait(6, 7)
    by_columns(low[...], wo, to_acc)

    def norm(at):
        z = x_out[at].astype(F32) + acc[at] + out_bias[0:1]
        unit, rstd = moments(z)
        unit_one[at] = unit
        rstd_one[at] = rstd
        h = (unit * gain[0:1] + shift[0:1]).astype(BF16)
        low[at] = h
        low_out[at] = h

    band_loop(total, norm)
    loads.wait(8, 9)

    def to_query(cols, value):
        cross_q[:, cols] = (value + bias_c[:, cols]).astype(BF16)

    by_columns(low[...], wc, to_query)


def cross_kernel(rows, length, scalars, ins, outs, scratch):
    image, corners = scalars
    queries, keys, values = ins
    (att,) = outs
    qs, acc = scratch
    patch_pad = keys.shape[1]
    lane_head = lane_heads()
    base = pl.program_id(0) * rows

    def spread(at):
        qs[at] = queries[at].astype(F32) * SCALE

    band_loop(rows * length, spread)

    @pl.loop(0, rows // PAIRED)
    def _(step):
        items, places = [], []
        for row in range(PAIRED):
            row = step * PAIRED + row
            at = pl.ds(pl.multiple_of(row * length, 8), length)
            which = image[base + row]
            keep = box_keep(corners, base + row, (1, patch_pad), 1)
            for g in range(qs.shape[1] // GROUP):
                lanes = slice(g * GROUP, (g + 1) * GROUP)
                items.append(
                    (
                        spread_heads(qs[at, lanes], lane_head),
                        keys[which, :, lanes],
                        values[which, :, lanes],
                        keep,
                    )
                )
                places.append((at, lanes))
        for (at, lanes), result in zip(places, attend(items)):
            acc[at, lanes] = gather_heads(result, lane_head, length)

    def cast(at):
        att[at] = acc[at].astype(BF16)

    band_loop(rows * length, cast)


def feed_kernel(steps, rows, local, hidden, length, scalars, ins, outs, scratch):
    (where,) = scalars
    grad_in, att, unit_one, aout, aout_mate, up, up_mate, down, down_mate = ins[:9]
    out_bias, gains, shift, up_bias, up_bias_mate = ins[9:]
    merged, low_out, df_out, do_out, dz_out, a_own, a_mate = outs[:7]
    g_out, du_out = outs[7:9], outs[9:11]
    da_out, sums, up_sums = outs[11:]
    wo, wu, wd, acc, kept, unit_two, rstd_two, low, upstream, even, odd, slope = scratch[:12]
    part, up_part, sems = scratch[12:]
    tiles = hidden // TILE
    total = rows * length
    loads = Loads(
        steps,
        sems,
        one_above(aout.at[1], aout_mate.at[1], wo, local)
        + [
            (source.at[:, pl.ds(t * TILE, TILE)], wu.at[t, :, pl.ds(half * TILE, TILE)])
            for t in range(tiles)
            for half, source in enumerate((up, up_mate))
        ]
        + [
            (source.at[pl.ds(t * TILE, TILE)], wd.at[t, pl.ds(half * TILE, TILE)])
            for t in range(tiles)
            for half, source in enumerate((down, down_mate))
        ],
    )
    loads.start()
    part[...] = jnp.zeros_like(part)

    def put(at, both):
        upstream[at] = both.astype(BF16)

    base = pl.program_id(0) * rows
    row_pairs(grad_in, where, base, rows, length, put)

    def to_acc(cols, value):
        acc[:, cols] = value

    a_own[...] = att[:, :local]
    a_mate[...] = att[:, local:]
    loads.wait(0, 1)
    by_columns(att[...], wo, to_acc)

    def norm_two(at):
        h_one = unit_one[at] * gains[0:1] + shift[0:1]
        unit, rstd = moments(h_one + acc[at] + out_bias[1:2])
        h_two = unit * gains[1:2] + shift[1:2]
        unit_two[at] = unit
        rstd_two[at] = rstd
        kept[at] = h_two
        h_low = h_two.astype(BF16)
        low[at] = h_low
        low_out[at] = h_low

    band_loop(total, norm_two)
    acc[...] = jnp.zeros_like(acc)
    loads.wait(*range(2, 2 + 4 * tiles))
    biases = (up_bias, up_bias_mate)

    def activate(units, t):
        cols = slice(t * TILE, (t + 1) * TILE)
        for half in range(2):
            lanes = slice(half * TILE, (half + 1) * TILE)
            bias = biases[half][:, cols]
            for start in range(0, total, BAND):
                at = slice(start, start + BAND)
                active, sloped = gelu(units[at, lanes] + bias)
                g_out[half][at, cols] = active.astype(BF16)
                slope[t, at, lanes] = sloped

    def add_down(t):
        cols = slice(t * TILE, (t + 1) * TILE)
        both = jnp.concatenate([g_out[0][:, cols], g_out[1][:, cols]], axis=1)
        acc[...] += dot(both, wd[t])

    units = (even, odd)
    even[...] = dot(low[...], wu[0])
    for t in range(tiles):
        if t + 1 < tiles:
            units[(t + 1) % 2][...] = dot(low[...], wu[t + 1])
        activate(units[t % 2], t)
        add_down(t)

    def norm_three(at):
        unit, rstd = moments(kept[at] + acc[at] + out_bias[2:3])
        gain = gains[2:3]
        unit_three = unit * gain + shift[2:3]
        grad = upstream[at].astype(F32)
        dz = norm_grad(unit, rstd, gain, grad)
        kept[at] = dz
        acc[at] = unit_three
        dz_low = dz.astype(BF16)
        low[at] = dz_low
        df_out[at] = dz_low
        return (
            (0, fold(dz_low.astype(F32))),
            (1, fold(grad * unit)),
            (2, fold(grad)),
        )

    band_loop(total, norm_three, part)

    for row in range(rows):
        merged[where[base + row]] = acc[row * length : (row + 1) * length].astype(BF16)
    acc[...] = jnp.zeros_like(acc)

    for t in range(tiles):
        cols = slice(t * TILE, (t + 1) * TILE)
        grads = dot_nt(low[...], wd[t])
        for half in range(2):
            lanes = slice(half * TILE, (half + 1) * TILE)
            folded = 0.0
            for start in range(0, total, BAND):
                at = slice(start, start + BAND)
                du = (grads[at, lanes] * slope[t, at, lanes]).astype(BF16)
                du_out[half][at, cols] = du
                folded = folded + fold(du.astype(F32))
            up_part[half, :, cols] = folded
        both = jnp.concatenate([du_out[0][:, cols], du_out[1][:, cols]], axis=1)
        acc[...] += dot_nt(both, wu[t])

    def norm_two_back(at):
        grad = kept[at] + acc[at]
        unit = unit_two[at]
        dz = norm_grad(unit, rstd_two[at], gains[1:2], grad)
        dz_out[at] = dz
        dz_low = dz.astype(BF16)
        low[at] = dz_low
        do_out[at] = dz_low
        return (
            (3, fold(dz_low.astype(F32))),
            (4, fold(grad * unit)),
            (5, fold(grad)),
        )

    band_loop(total, norm_two_back, part)

    def to_grad(cols, value):
        da_out[:, cols] = value.astype(BF16)

    by_columns(low[...], wo, to_grad, transposed=True)
    for at in range(8):
        sums[0, at : at + 1] = jnp.sum(part[at], axis=0, keepdims=True)
    for half in range(2):
        up_sums[0, half : half + 1] = jnp.sum(up_part[half], axis=0, keepdims=True)


def cross_grad_kernel(steps, rows, length, scalars, ins, outs, scratch):
    image, corners = scalars
    queries, grads, keys, values = ins
    own, mate, grad_queries = outs
    qs, gs, acc, dk, dv = scratch
    patch_pad = keys.shape[1]

    def clear():
        @pl.loop(0, dk.shape[0])
        def _(at):
            dk[at] = jnp.zeros(dk.shape[1:], F32)
            dv[at] = jnp.zeros(dv.shape[1:], F32)

    pl.when(pl.program_id(0) == 0)(clear)

    def spread(at):
        qs[at] = queries[at].astype(F32) * SCALE
        gs[at] = grads[at].astype(F32)

    band_loop(rows * length, spread)
    lane_head = lane_heads()
    base = pl.program_id(0) * rows

    @pl.loop(0, rows // PAIRED)
    def _(step):
        items, places = [], []
        for row in range(PAIRED):
            row = step * PAIRED + row
            at = pl.ds(pl.multiple_of(row * length, 8), length)
            which = image[base + row]
            keep = box_keep(corners, base + row, (patch_pad, 1), 0)
            for g in range(qs.shape[1] // GROUP):
                lanes = slice(g * GROUP, (g + 1) * GROUP)
                items.append(
                    (
                        spread_heads(qs[at, lanes], lane_head),
                        keys[which, :, lanes],
                        values[which, :, lanes],
                        spread_heads(gs[at, lanes], lane_head),
                        keep,
                    )
                )
                places.append((at, which, lanes))
        for (at, which, lanes), (grad_q, grad_k, grad_v) in zip(places, attend_grad(items)):
            acc[at, lanes] = gather_heads(grad_q, lane_head, length) * SCALE
            dk[which, :, lanes] += grad_k
            dv[which, :, lanes] += grad_v

    def cast(at):
        grad_queries[at] = acc[at].astype(BF16)

    band_loop(rows * length, cast)

    @pl.when(pl.program_id(0) == steps - 1)
    def _():
        half = own.shape[1]

        @pl.loop(0, half)
        def _(at):
            own[0, at] = dk[at].astype(BF16)
            own[1, at] = dv[at].astype(BF16)
            mate[0, at] = dk[half + at].astype(BF16)
            mate[1, at] = dv[half + at].astype(BF16)


def image_kernel(images, patch_count, local, scalars, ins, outs, scratch):
    (core,) = scalars
    piece, piece_mate, patches, proj_weight, ain, ain_mate = ins
    kv_own, kv_mate, patch_grad, weight_grad, sums = outs
    narrow, wide, taken, w1, w2, part, sems, weight_sems = scratch
    parts, span = taken.shape[0], taken.shape[1]
    loads = Loads(
        1,
        weight_sems,
        side_by_side(ain.at[1, 1], ain_mate.at[1, 1], w1, local)
        + side_by_side(ain.at[1, 2], ain_mate.at[1, 2], w2, local),
    )
    arrivals = Loads(
        1, sems, [(patches.at[pl.ds(n * span, span)], taken.at[n]) for n in range(parts)]
    )
    loads.start()
    arrivals.start()
    part[...] = jnp.zeros_like(part)
    own_images, patch_pad = piece.shape[1], piece.shape[2]
    width = w1.shape[0]

    slab = 80

    @pl.loop(0, wide.shape[1] // slab)
    def _(step):
        at = pl.ds(pl.multiple_of(step * slab, slab), slab)
        for lane in range(wide.shape[0]):
            wide[lane, at] = jnp.zeros((slab, LANES), F32)

    loads.wait(0, 1, 2, 3)
    first = core[0] * own_images

    @pl.loop(0, own_images // 2)
    def _(step):
        pair = pl.ds(step * 2, 2)
        halves = []
        for half in (slice(0, local), slice(local, width)):
            swapped = slice(width - half.stop, width - half.start)
            both = piece[:, pair, :, half].astype(F32) + piece_mate[:, pair, :, swapped].astype(F32)
            both = both.astype(BF16)
            halves.append([both[at].reshape(2 * patch_pad, local) for at in range(2)])
        (dk_own, dv_own), (dk_mate, dv_mate) = halves
        rows = pl.ds(pl.multiple_of(step * 2 * patch_pad, 2 * patch_pad), 2 * patch_pad)
        kv_own[rows, :local] = dk_own
        kv_own[rows, local:] = dv_own
        kv_mate[rows, :local] = dk_mate
        kv_mate[rows, local:] = dv_mate
        dk = jnp.concatenate([dk_own, dk_mate], axis=1)
        dv = jnp.concatenate([dv_own, dv_mate], axis=1)
        part[1] += fold(dv.astype(F32))
        for start in range(0, width, GROUP):
            cols = slice(start, start + GROUP)
            grad = dot_nt(dk, w1[cols, :]) + dot_nt(dv, w2[cols, :])
            grad = grad.astype(BF16).astype(F32)
            part[0, :, cols] += fold(grad)
            for at in range(2):
                one = grad[at * patch_pad : at * patch_pad + patch_count]
                which = step * 2 + at
                spot = pl.ds(which, patch_count, stride=own_images)
                split_lanes(narrow, spot, start, one)
                split_lanes(wide, pl.ds(which + first, patch_count, stride=images), start, one)

    for n in range(parts):
        arrivals.wait(n)
        few = slice(n * span * own_images, (n + 1) * span * own_images)
        some = join_lanes(narrow, few).astype(BF16)
        for start in range(0, proj_weight.shape[0], GROUP):
            cols = slice(start, start + GROUP)
            back = dot_nt(some, proj_weight[cols, :]).astype(BF16)
            patch_grad[n * span : (n + 1) * span, :, cols] = back.reshape(span, own_images, GROUP)
        flat = taken[n].reshape(span * images, taken.shape[3])
        grad = join_lanes(wide, slice(n * span * images, (n + 1) * span * images)).astype(BF16)
        product = dot_tn(flat, grad)
        if n == 0:
            weight_grad[...] = product
        else:
            weight_grad[...] += product
    for at in range(2):
        sums[at : at + 1] = jnp.sum(part[at], axis=0, keepdims=True)


def self_grad_kernel(steps, rows, local, length, scalars, ins, outs, scratch):
    lens, where = scalars
    dq2, unit_one, rstd_one, dz_two, q_in, k_in, v_in, ain, ain_mate, aout, aout_mate, gain = ins
    text_grad, do_out, dq2_own, dq2_mate, qkv_own, qkv_mate, sums = outs
    wc, wo, wq, wk, wv, acc, kept, low, low_k, low_v, qs, ks, vs, part, sems = scratch
    total = rows * length
    loads = Loads(
        steps,
        sems,
        side_by_side(ain.at[1, 0], ain_mate.at[1, 0], wc, local)
        + one_above(aout.at[0], aout_mate.at[0], wo, local)
        + side_by_side(ain.at[0, 0], ain_mate.at[0, 0], wq, local)
        + side_by_side(ain.at[0, 1], ain_mate.at[0, 1], wk, local)
        + side_by_side(ain.at[0, 2], ain_mate.at[0, 2], wv, local),
    )
    loads.start()
    part[...] = jnp.zeros_like(part)

    def to_acc(cols, value):
        acc[:, cols] = value

    loads.wait(0, 1)
    by_columns(dq2[...], wc, to_acc, transposed=True)

    def norm_back(at):
        unit = unit_one[at]
        grad = dz_two[at] + acc[at]
        dz = norm_grad(unit, rstd_one[at], gain[0:1], grad)
        kept[at] = dz
        dz_low = dz.astype(BF16)
        low[at] = dz_low
        do_out[at] = dz_low
        qs[at] = q_in[at].astype(F32) * SCALE
        ks[at] = k_in[at].astype(F32)
        vs[at] = v_in[at].astype(F32)
        query = dq2[at]
        dq2_own[at] = query[:, :local]
        dq2_mate[at] = query[:, local:]
        return (
            (0, fold(dz_low.astype(F32))),
            (1, fold(grad * unit)),
            (2, fold(grad)),
            (5, fold(query.astype(F32))),
        )

    band_loop(total, norm_back, part)
    loads.wait(2, 3)
    by_columns(low[...], wo, to_acc, transposed=True)
    lane_head = lane_heads()
    key_index = lax.broadcasted_iota(jnp.int32, (length, 1), 0)
    base = pl.program_id(0) * rows

    @pl.loop(0, rows // PAIRED)
    def _(step):
        items, places = [], []
        for row in range(PAIRED):
            row = step * PAIRED + row
            at = pl.ds(pl.multiple_of(row * length, 8), length)
            keep = key_index < lens[base + row]
            for g in range(qs.shape[1] // GROUP):
                lanes = slice(g * GROUP, (g + 1) * GROUP)
                items.append(
                    (
                        spread_heads(qs[at, lanes], lane_head),
                        ks[at, lanes].astype(BF16),
                        vs[at, lanes].astype(BF16),
                        spread_heads(acc[at, lanes], lane_head),
                        keep,
                    )
                )
                places.append((at, lanes))
        for (at, lanes), (grad_q, grad_k, grad_v) in zip(places, attend_grad(items)):
            qs[at, lanes] = gather_heads(grad_q, lane_head, length) * SCALE
            ks[at, lanes] = grad_k
            vs[at, lanes] = grad_v

    def cast(at):
        sums = []
        for slot, (source, target) in enumerate(((qs, low), (ks, low_k), (vs, low_v))):
            value = source[at].astype(BF16)
            target[at] = value
            qkv_own[at, slot * local : (slot + 1) * local] = value[:, :local]
            qkv_mate[at, slot * local : (slot + 1) * local] = value[:, local:]
            if slot != 1:
                sums.append((3 + slot // 2, fold(value.astype(F32))))
        return sums

    band_loop(total, cast, part)
    loads.wait(4, 5, 6, 7, 8, 9)
    for start in range(0, kept.shape[1], GROUP):
        cols = slice(start, start + GROUP)
        acc[:, cols] = (
            kept[:, cols]
            + dot_nt(low[...], wq[cols, :])
            + dot_nt(low_k[...], wk[cols, :])
            + dot_nt(low_v[...], wv[cols, :])
        )

    for row in range(rows):
        text_grad[where[base + row]] = acc[row * length : (row + 1) * length].astype(BF16)
    for at in range(8):
        sums[0, at : at + 1] = jnp.sum(part[at], axis=0, keepdims=True)


def pack_kernel(local, hidden, scalars, ins, outs, scratch):
    (core,) = scalars
    feed, up, self_, image = ins
    feed_sum = jnp.sum(feed[...], axis=0)
    self_sum = jnp.sum(self_[...], axis=0)
    up_sum = jnp.sum(up[...], axis=0)
    common = [(0, 0), (1, 3), (1, 0), (0, 1), (1, 4), (1, 1), (0, 2), (1, 5), (1, 2)]
    even = core[0] == 0
    for out, mine in zip(outs, (True, False)):
        out[...] = jnp.zeros_like(out)
        at = 0
        for which, row in common:
            source = feed_sum if which else self_sum
            for half in range(2):
                out[at : at + 1] = source[row : row + 1, half * local : (half + 1) * local]
                at += 1
        lanes = slice(0, local) if mine else slice(local, 2 * local)
        for row in (3, 4, 5):
            out[at : at + 1] = self_sum[row : row + 1, lanes]
            at += 1
        out[at : at + 1] = image[1:2, lanes]
        at += 1
        half = 0 if mine else 1
        for start in range(0, hidden, local):
            out[at : at + 1] = up_sum[half : half + 1, start : start + local]
            at += 1
        low, high = image[0:1, :local], image[0:1, local:]
        out[at : at + 1] = jnp.where(even == mine, low, high)


def halve_kernel(rows, length, scalars, ins, outs, scratch):
    core, where = scalars
    (tall,) = scratch

    def put(at, both):
        split_lanes(tall, at, 0, both)

    row_pairs(ins[0], where, 0, rows, length, put)
    half = length // 2
    for out, first in zip(outs, (core[0] * half, (1 - core[0]) * half)):
        for token in range(half):
            out[token] = join_lanes(
                tall, pl.ds(first + token, rows, stride=length)
            ).astype(BF16)


def place_kernel(scalars, ins, outs, scratch):
    own, mate, place = ins
    (out,) = outs
    count, slots = out.shape[1], own.shape[1]
    index = lax.broadcasted_iota(jnp.int32, (count, slots), 1)
    from_own = jnp.where(place[...] == index, 1.0, 0.0).astype(BF16)
    from_mate = jnp.where(place[...] == index + slots, 1.0, 0.0).astype(BF16)
    for token in range(out.shape[0]):
        out[token] = (dot(from_own, own[token]) + dot(from_mate, mate[token])).astype(BF16)


def body(
    text,
    cotangent,
    lengths,
    box_corners,
    box_counts,
    region_box,
    patches,
    proj_weight,
    proj_bias,
    attention_in,
    attention_bias,
    attention_out,
    output_bias,
    norm_gain,
    norm_bias,
    up_weight,
    up_bias,
    down_weight,
):
    rows, length, width = text.shape
    images, patch_count, vision = patches.shape
    local = attention_in.shape[-1]
    hidden = up_weight.shape[-1]
    devices = lax.axis_size("dp")
    me, core = lax.axis_index("dp"), lax.axis_index("mp")
    pair = -(-rows // devices)
    each, odd = pair // 2, pair % 2
    deep = each + odd
    slots = devices * each + devices // 2 * odd
    patch_pad = -(-patch_count // 16) * 16
    own_images = images // 2
    step_rows = 12 if slots % 12 == 0 else 8
    steps = slots // step_rows
    tokens = step_rows * length
    all_tokens = slots * length
    full = slots * 2 == rows
    core_scalar = core.astype(jnp.int32).reshape(1)

    def mate(value):
        return lax.ppermute(value, "mp", [(0, 1), (1, 0)])

    def tie(*values):
        return lax.optimization_barrier(values)

    def exchange(value):
        return lax.all_to_all(value, "dp", split_axis=0, concat_axis=0, tiled=True)

    ain_mate = mate(attention_in)
    bias_mate = mate(attention_bias)
    aout_mate = mate(attention_out)
    up_bias_own = up_bias.reshape(1, hidden)
    up_bias_mate = mate(up_bias_own)
    up_mate = mate(up_weight)
    down_mate = mate(down_weight)

    number = jnp.arange(rows, dtype=jnp.int32)
    target = region_box // rows
    earlier = (target[:, None] == target[None, :]) & (number[None, :] < number[:, None])
    nth = jnp.sum(earlier.astype(jnp.int32), axis=1)
    even_part = nth < 2 * each
    row_core = jnp.where(even_part, nth // max(each, 1), (target ^ me) & 1)
    depth = jnp.where(even_part, nth % max(each, 1), each)
    spot = jnp.arange(devices * deep, dtype=jnp.int32)
    hit = (spot[:, None] == (target * deep + depth)[None, :]) & (row_core == core)[None, :]
    source = jnp.sum(jnp.where(hit, number[None, :], 0), axis=1)
    slot = jnp.where(even_part, target * each + depth, devices * each + (target >> 1))
    place = jnp.where(row_core == core, slot, slot + slots)[:, None]
    order = jnp.arange(slots, dtype=jnp.int32)
    late = order - devices * each
    where = jnp.where(
        late < 0,
        order // max(each, 1) * deep + order % max(each, 1),
        (2 * late + ((me & 1) ^ core)) * deep + each,
    )
    meta = jnp.concatenate(
        [(region_box % rows)[:, None], lengths[:, None], box_corners], axis=1
    )
    meta_out = jnp.sum(jnp.where(hit[:, :, None], meta[None], 0), axis=1)
    if not full:
        empty = jnp.array([0, 1, 0, 1, 0, 1], jnp.int32)
        meta_out = jnp.where(jnp.any(hit, axis=1)[:, None], meta_out, empty[None])
    arrived = exchange(meta_out)[where]
    ends = jnp.cumsum(box_counts[0])
    image = jnp.sum((ends[None, :] <= arrived[:, 0:1]).astype(jnp.int32), axis=1)
    image = (image + own_images * core) % images
    lens = arrived[:, 1]
    corners = arrived[:, 2:].reshape(-1)

    block_shape = (devices * deep, length, width)
    if full:
        x_out, upstream_out = run(
            partial(fetch_kernel, devices * deep),
            1,
            [source],
            [(text, ANY), (cotangent, ANY)],
            [(block_shape, BF16, whole_spec(block_shape))] * 2,
            [pltpu.SemaphoreType.DMA((2 * devices * deep,))],
            0,
        )
    else:
        valid = jnp.any(hit, axis=1)[:, None, None]
        x_out = jnp.where(valid, text[source], 0)
        upstream_out = jnp.where(valid, cotangent[source], 0)
    x_in = exchange(x_out)

    patches, aout_mate, image, corners, lens = tie(patches, aout_mate, image, corners, lens)
    by_patch = jnp.transpose(patches, (1, 0, 2))
    parts = next(n for n in (5, 4, 3, 2, 1) if patch_count % n == 0)
    weight_scratch = pltpu.VMEM((width, width), BF16)

    def slabs(count):
        return pltpu.VMEM((width // LANES, count, LANES), F32)

    patch_scratch = pltpu.VMEM((parts, patch_count // parts, images, vision), BF16)
    image_shape = (images, patch_pad, width)
    proj, keys, values = run(
        partial(project_kernel, images, own_images, patch_pad, patch_count, local),
        1,
        [core_scalar],
        [
            (by_patch, ANY),
            (proj_weight, whole_spec(proj_weight.shape)),
            (proj_bias.reshape(1, width), whole_spec((1, width))),
            (attention_in, ANY),
            (ain_mate, ANY),
            (attention_bias, whole_spec(attention_bias.shape)),
            (bias_mate, whole_spec(bias_mate.shape)),
        ],
        [((own_images,) + image_shape[1:], BF16, whole_spec((own_images,) + image_shape[1:]))]
        + [(image_shape, BF16, whole_spec(image_shape))] * 2,
        [
            patch_scratch,
            slabs(patch_count * images),
            weight_scratch,
            weight_scratch,
            pltpu.SemaphoreType.DMA((parts,)),
            pltpu.SemaphoreType.DMA((4,)),
        ],
        2 * images * patch_pad * width * (vision + 2 * width),
    )

    upstream_out, proj, keys, values = tie(upstream_out, proj, keys, values)
    upstream_in = exchange(upstream_out)

    def token_in(value):
        return (value, rows_spec((tokens, value.shape[1]), 0))

    def token_out(cols, dtype):
        return ((all_tokens, cols), dtype, rows_spec((tokens, cols), 0))

    block_out = (block_shape, BF16, whole_spec(block_shape))

    def f32_tokens(cols):
        return pltpu.VMEM((tokens, cols), F32)

    def low_tokens(cols):
        return pltpu.VMEM((tokens, cols), BF16)

    def whole(value):
        return (value, whole_spec(value.shape))

    attention_flops = 4 * 4 * all_tokens * width * 64

    x, unit_one, q_self, k_self, v_self, att_own, att_mate, self_low, queries, rstd_one = run(
        partial(self_kernel, steps, step_rows, local, length),
        steps,
        [lens, where],
        [
            whole(x_in),
            (attention_in, ANY),
            (ain_mate, ANY),
            (attention_out, ANY),
            (aout_mate, ANY),
            whole(attention_bias),
            whole(bias_mate),
            whole(output_bias),
            whole(norm_gain),
            whole(norm_bias),
        ],
        [token_out(width, BF16), token_out(width, F32)]
        + [token_out(width, BF16)] * 3
        + [token_out(local, BF16)] * 2
        + [token_out(width, BF16)] * 2
        + [token_out(1, F32)],
        [weight_scratch] * 5
        + [f32_tokens(width)] * 4
        + [low_tokens(width), pltpu.SemaphoreType.DMA((10,))],
        2 * all_tokens * width * width * 5 + attention_flops,
    )

    (attended,) = run(
        partial(cross_kernel, step_rows, length),
        steps,
        [image, corners],
        [token_in(queries), whole(keys), whole(values)],
        [token_out(width, BF16)],
        [f32_tokens(width)] * 2,
        attention_flops * 4,
    )

    result = run(
        partial(feed_kernel, steps, step_rows, local, hidden, length),
        steps,
        [where],
        [
            whole(upstream_in),
            token_in(attended),
            token_in(unit_one),
            (attention_out, ANY),
            (aout_mate, ANY),
            (up_weight, ANY),
            (up_mate, ANY),
            (down_weight, ANY),
            (down_mate, ANY),
            whole(output_bias),
            whole(norm_gain),
            whole(norm_bias),
            whole(up_bias_own),
            whole(up_bias_mate),
        ],
        [block_out]
        + [token_out(width, BF16)] * 3
        + [token_out(width, F32)]
        + [token_out(local, BF16)] * 2
        + [token_out(hidden, BF16)] * 4
        + [
            token_out(width, BF16),
            ((steps, 8, width), F32, rows_spec((1, 8, width), 0)),
            ((steps, 2, hidden), F32, rows_spec((1, 2, hidden), 0)),
        ],
        [weight_scratch]
        + [
            pltpu.VMEM((hidden // TILE, width, 2 * TILE), BF16),
            pltpu.VMEM((hidden // TILE, 2 * TILE, width), BF16),
        ]
        + [f32_tokens(width)] * 3
        + [f32_tokens(1), low_tokens(width), low_tokens(width)]
        + [f32_tokens(2 * TILE)] * 2
        + [pltpu.VMEM((hidden // TILE, tokens, 2 * TILE), F32)]
        + [pltpu.VMEM((8, 8, width), F32), pltpu.VMEM((2, 8, hidden), F32)]
        + [pltpu.SemaphoreType.DMA((2 + 4 * hidden // TILE,))],
        2 * all_tokens * width * (2 * width + 8 * hidden),
    )
    merged_out, cross_low, grad_ffn, grad_cross, dz_two, a_own, a_mate = result[:7]
    g_own, g_mate, du_own, du_mate, grad_att, feed_sums, up_sums = result[7:]

    bits = devices.bit_length() - 1

    def partner_bits(value, mask):
        return lax.ppermute(value, "dp", [(d, d ^ mask) for d in range(devices)])

    def opened(value):
        return value.reshape((2,) * bits + (value.shape[0] // devices, value.shape[1]))

    def swap(value, axis, bit):
        mine = (me >> bit) & 1
        away = lax.dynamic_index_in_dim(value, 1 - mine, axis, keepdims=False)
        stay = lax.dynamic_index_in_dim(value, mine, axis, keepdims=False)
        return stay, partner_bits(away, 1 << bit)

    def first_swaps(by_x, by_y):
        return swap(opened(by_x), bits - 1, 0) + swap(opened(by_y), bits - 2, 1)

    def second_swaps(stay_x, got_x, stay_y, got_y):
        return swap(add(stay_x, got_x), bits - 2, 1) + swap(add(stay_y, got_y), bits - 2, 0)

    def add(stay, got):
        return (stay.astype(F32) + got.astype(F32)).astype(BF16)

    def last_parts(stay_x, got_x, stay_y, got_y):
        parts = [add(stay_x, got_x), add(stay_y, got_y)]
        return jnp.concatenate(
            [part.reshape((devices // 4,) + part.shape[-2:]) for part in parts], axis=2
        )

    def last_sum(both, first_width):
        groups = [[low + 4 * n for n in range(devices // 4)] for low in range(4)]
        both = lax.all_to_all(
            both, "dp", split_axis=0, concat_axis=0, axis_index_groups=groups, tiled=True
        )
        total = jnp.sum(both.astype(F32), axis=0)
        return total[:, :first_width], total[:, first_width:]

    def low_tn(left, right):
        return dot_tn(left, right).astype(BF16)

    merged_in = exchange(merged_out)
    up_away, down_away = low_tn(cross_low, du_mate), low_tn(grad_ffn, g_mate)
    grad_att, queries, up_away, down_away = tie(grad_att, queries, up_away, down_away)
    up_got, down_got = mate(up_away), mate(down_away)

    half_shape = (2, own_images, patch_pad, width)
    image_acc = pltpu.VMEM(image_shape, F32)
    piece, piece_out, grad_queries = run(
        partial(cross_grad_kernel, steps, step_rows, length),
        steps,
        [image, corners],
        [token_in(queries), token_in(grad_att), whole(keys), whole(values)],
        [(half_shape, BF16, whole_spec(half_shape))] * 2 + [token_out(width, BF16)],
        [f32_tokens(width)] * 3 + [image_acc] * 2,
        attention_flops * 12,
    )
    piece_mate = mate(piece_out)

    up_part = (dot_tn(cross_low, du_own) + up_got.astype(F32)).astype(BF16)
    down_part = (dot_tn(grad_ffn, g_own) + down_got.astype(F32)).astype(BF16)
    grad_queries, up_part, down_part = tie(grad_queries, up_part, down_part)
    feed_stage = first_swaps(up_part, down_part)

    result = run(
        partial(self_grad_kernel, steps, step_rows, local, length),
        steps,
        [lens, where],
        [
            token_in(grad_queries),
            token_in(unit_one),
            token_in(rstd_one),
            token_in(dz_two),
            token_in(q_self),
            token_in(k_self),
            token_in(v_self),
            (attention_in, ANY),
            (ain_mate, ANY),
            (attention_out, ANY),
            (aout_mate, ANY),
            whole(norm_gain),
        ],
        [block_out]
        + [token_out(width, BF16)]
        + [token_out(local, BF16)] * 2
        + [token_out(3 * local, BF16)] * 2
        + [((steps, 8, width), F32, rows_spec((1, 8, width), 0))],
        [weight_scratch] * 5
        + [f32_tokens(width)] * 2
        + [low_tokens(width)] * 3
        + [f32_tokens(width)] * 3
        + [pltpu.VMEM((8, 8, width), F32), pltpu.SemaphoreType.DMA((10,))],
        2 * all_tokens * width * width * 5 + attention_flops * 2,
    )
    text_out, grad_self, dq_own, dq_mate, qkv_own, qkv_mate, self_sums = result
    text_in = exchange(text_out)

    self_away = jnp.concatenate(
        [
            low_tn(x, qkv_mate),
            low_tn(grad_self, att_mate),
            low_tn(grad_cross, a_mate),
            low_tn(self_low, dq_mate),
        ],
        axis=1,
    )
    self_got = mate(self_away)
    feed_stage = tie(self_away, *feed_stage)[1:]
    feed_stage = second_swaps(*feed_stage)
    self_own = jnp.concatenate(
        [
            dot_tn(x, qkv_own),
            dot_tn(grad_self, att_own),
            dot_tn(grad_cross, a_own),
            dot_tn(self_low, dq_own),
        ],
        axis=1,
    )
    self_part = (self_own + self_got.astype(F32)).astype(BF16)
    half_width = self_part.shape[1] // 2
    self_stage = first_swaps(self_part[:, :half_width], self_part[:, half_width:])
    feed_parts = last_parts(*feed_stage)
    piece, piece_mate, self_part, feed_parts = tie(piece, piece_mate, self_part, feed_parts)

    flat_images = own_images * patch_pad
    patch_grad_shape = (patch_count, own_images, vision)
    kv_own, kv_mate, patch_grad, proj_weight_sum, image_sums = run(
        partial(image_kernel, images, patch_count, local),
        1,
        [core_scalar],
        [
            whole(piece),
            whole(piece_mate),
            (by_patch, ANY),
            whole(proj_weight),
            (attention_in, ANY),
            (ain_mate, ANY),
        ],
        [
            ((flat_images, width), BF16, whole_spec((flat_images, width))),
            ((flat_images, width), BF16, whole_spec((flat_images, width))),
            (patch_grad_shape, BF16, whole_spec(patch_grad_shape)),
            ((vision, width), F32, whole_spec((vision, width))),
            ((8, width), F32, whole_spec((8, width))),
        ],
        [
            slabs(patch_count * own_images),
            slabs(patch_count * images),
            patch_scratch,
            weight_scratch,
            weight_scratch,
            pltpu.VMEM((2, 8, width), F32),
            pltpu.SemaphoreType.DMA((parts,)),
            pltpu.SemaphoreType.DMA((4,)),
        ],
        2 * flat_images * width * (2 * width + 2 * vision),
        [text_in],
    )

    up_grad, down_grad = last_sum(feed_parts, hidden)
    self_stage = second_swaps(*self_stage)
    kv_low = proj.reshape(flat_images, width)
    kv_away = low_tn(kv_low, kv_mate)
    kv_got = mate(kv_away)
    proj_away = lax.dynamic_slice_in_dim(proj_weight_sum, (1 - core) * local, local, 1)
    proj_got = mate(proj_away.astype(BF16))
    kv_part = (dot_tn(kv_low, kv_own) + kv_got.astype(F32)).astype(BF16)
    proj_own = lax.dynamic_slice_in_dim(proj_weight_sum, core * local, local, 1)
    proj_part = (proj_own + proj_got.astype(F32)).astype(BF16)
    proj_part = proj_part.reshape(width, vision * local // width)
    image_stage = first_swaps(kv_part, proj_part)
    self_one, self_two = last_sum(last_parts(*self_stage), half_width)
    image_stage = second_swaps(*image_stage)
    kv_grad, proj_grad = last_sum(last_parts(*image_stage), width)
    proj_grad = proj_grad.reshape(vision // devices, local)

    lines = 23 + hidden // local
    packed_shape = (-(-lines // 8) * 8, local)
    small, small_out = run(
        partial(pack_kernel, local, hidden),
        1,
        [core_scalar],
        [whole(feed_sums), whole(up_sums), whole(self_sums), whole(image_sums)],
        [(packed_shape, F32, whole_spec(packed_shape))] * 2,
        [],
        0,
        [up_grad, kv_part, proj_part],
    )
    small = small + mate(small_out)
    for bit in range(bits):
        small = small + partner_bits(small, 1 << bit)
    common = small[:18].reshape(3, 3, width)
    bias_grad = small[18:22].reshape(2, 2, local)
    up_bias_grad = small[22 : 22 + hidden // local].reshape(hidden)
    proj_bias_grad = small[22 + hidden // local]

    ready = [self_one[:, at * local : (at + 1) * local] for at in range(3)]
    out_self, out_cross, query_cross = [
        self_two[:, at * local : (at + 1) * local] for at in range(3)
    ]
    in_grad = jnp.stack(
        ready + [query_cross, kv_grad[:, :local], kv_grad[:, local:]]
    ).reshape(2, 3, width // devices, local)
    out_grad = jnp.stack([out_self.T, out_cross.T])

    def tokens_out(value, after, after_place):
        shape = (length // 2, slots, width)
        own, away = run(
            partial(halve_kernel, slots, length),
            1,
            [core_scalar, where],
            [whole(value)],
            [(shape, BF16, whole_spec(shape))] * 2,
            [slabs(all_tokens)],
            0,
            after,
        )
        shape = (length // 2, rows, width)
        (out,) = run(
            place_kernel,
            1,
            [],
            [whole(own), whole(mate(away)), whole(place)],
            [(shape, BF16, whole_spec(shape))],
            [],
            0,
            after_place,
        )
        return jnp.transpose(out, (1, 0, 2))

    return (
        tokens_out(merged_in, [self_part], [kv_part]),
        tokens_out(text_in, [kv_away], [kv_part, proj_part]),
        jnp.transpose(patch_grad, (1, 0, 2)),
        proj_grad,
        proj_bias_grad,
        in_grad,
        bias_grad,
        out_grad,
        common[0],
        common[1],
        common[2],
        up_grad,
        up_bias_grad,
        down_grad.T,
    )


def solution(mesh):
    placed = (
        P("dp", None, None),
        P("dp", None, None),
        P("dp"),
        P("dp", None),
        P("dp", None),
        P("dp"),
        P("dp", None, None),
        P(),
        P(),
        P(None, None, None, "mp"),
        P(None, None, "mp"),
        P(None, "mp", None),
        P(),
        P(),
        P(),
        P(None, "mp"),
        P("mp"),
        P("mp", None),
    )
    return jax.shard_map(
        body,
        mesh=mesh,
        in_specs=placed,
        out_specs=(
            P("dp", "mp", None),
            P("dp", "mp", None),
            P(("dp", "mp"), None, None),
            P("dp", "mp"),
            P("mp"),
            P(None, None, "dp", "mp"),
            P(None, None, "mp"),
            P(None, "mp", "dp"),
            P(),
            P(),
            P(),
            P("dp", "mp"),
            P("mp"),
            P("mp", "dp"),
        ),
        check_vma=False,
    )
```

```python
import math
from functools import partial

import jax
import jax.numpy as jnp
from jax import lax
from jax.experimental import pallas as pl
from jax.experimental.pallas import tpu as pltpu
from jax.sharding import PartitionSpec as P

HEAD_DIM = 64
GRID = 12
EPS = 1e-12
NEG = -1e30
SCALE = HEAD_DIM ** (-0.5)

F32 = jnp.float32
BF16 = jnp.bfloat16

GROUP = 4 * HEAD_DIM
BAND = 32
BANDS = 5
LANES = 128
TILE = 256
PAIRED = 4
VMEM_LIMIT = 58 << 20


def dot(left, right):
    return lax.dot_general(left, right, (((1,), (0,)), ((), ())), preferred_element_type=F32)


def dot_nt(left, right):
    return lax.dot_general(left, right, (((1,), (1,)), ((), ())), preferred_element_type=F32)


def dot_tn(left, right):
    return lax.dot_general(left, right, (((0,), (0,)), ((), ())), preferred_element_type=F32)


def rows_spec(block, offset):
    rank = len(block)
    return pl.BlockSpec(block, lambda s, *_: (s + offset,) + (0,) * (rank - 1))


def whole_spec(shape):
    rank = len(shape)
    return pl.BlockSpec(shape, lambda s, *_: (0,) * rank, pipeline_mode=pl.Buffered(1))


ANY = pl.BlockSpec(memory_space=pl.ANY)


def run(body, steps, scalars, ins, outs, scratch, flops, after=(), through=()):
    ns, ni, no, nt = len(scalars), len(ins), len(outs), len(through)

    def kernel(*refs):
        rest = refs[ns + ni + len(after) + nt :]
        body(refs[:ns], refs[ns : ns + ni], rest[:no], rest[no + nt :])

    moved = sum(math.prod(a.shape) * a.dtype.itemsize for a, _ in ins)
    first = ns + ni + len(after)
    ins = list(ins) + [(array, ANY) for array in list(after) + list(through)]
    moved += sum(math.prod(shape) * jnp.dtype(dtype).itemsize for shape, dtype, _ in outs)
    outs = list(outs) + [(array.shape, array.dtype, ANY) for array in through]
    return pl.pallas_call(
        kernel,
        grid_spec=pltpu.PrefetchScalarGridSpec(
            num_scalar_prefetch=ns,
            grid=(steps,),
            in_specs=[spec for _, spec in ins],
            out_specs=[spec for _, _, spec in outs],
            scratch_shapes=scratch,
        ),
        out_shape=[jax.ShapeDtypeStruct(shape, dtype) for shape, dtype, _ in outs],
        input_output_aliases={first + at: no + at for at in range(nt)},
        compiler_params=pltpu.CompilerParams(
            dimension_semantics=("arbitrary",), vmem_limit_bytes=VMEM_LIMIT
        ),
        cost_estimate=pl.CostEstimate(flops=flops, bytes_accessed=moved, transcendentals=0),
    )(*scalars, *[array for array, _ in ins])


class Loads:
    def __init__(self, steps, sems, pairs):
        self.steps = steps
        self.copies = [
            pltpu.make_async_copy(source, target, sems.at[at])
            for at, (source, target) in enumerate(pairs)
        ]

    def first(self, action):
        if self.steps == 1:
            action()
        else:
            pl.when(pl.program_id(0) == 0)(action)

    def start(self):
        self.first(lambda: [copy.start() for copy in self.copies] and None)

    def wait(self, *which):
        self.first(lambda: [self.copies[at].wait() for at in which] and None)


def side_by_side(own, mate, target, width):
    return [(own, target.at[:, pl.ds(0, width)]), (mate, target.at[:, pl.ds(width, width)])]


def one_above(own, mate, target, height):
    return [(own, target.at[pl.ds(0, height)]), (mate, target.at[pl.ds(height, height)])]


def moments(z):
    center = z - jnp.mean(z, axis=-1, keepdims=True)
    rstd = lax.rsqrt(jnp.mean(center * center, axis=-1, keepdims=True) + EPS)
    return center * rstd, rstd


def norm_grad(unit, rstd, gain, grad):
    inner = grad * gain
    return rstd * (
        inner
        - jnp.mean(inner, axis=-1, keepdims=True)
        - unit * jnp.mean(inner * unit, axis=-1, keepdims=True)
    )


def fold(block):
    return jnp.sum(block.reshape(block.shape[0] // 8, 8, block.shape[1]), axis=0)


def gelu(u):
    bell = jnp.exp2(u * u * (-0.5 / math.log(2.0)))
    t = 1.0 / (1.0 + (0.3275911 * 0.5**0.5) * jnp.abs(u))
    poly = t * (
        0.5 * 0.254829592
        + t
        * (
            0.5 * -0.284496736
            + t * (0.5 * 1.421413741 + t * (0.5 * -1.453152027 + t * (0.5 * 1.061405429)))
        )
    )
    tail = poly * bell
    phi = jnp.where(u >= 0.0, 1.0 - tail, tail)
    return u * phi, phi + u * (bell * (1.0 / math.sqrt(2.0 * math.pi)))


def spread_heads(block, lane_head):
    parts = [jnp.where(lane_head == h, block, 0.0) for h in range(GROUP // HEAD_DIM)]
    return jnp.concatenate(parts, axis=0).astype(BF16)


def gather_heads(block, lane_head, tokens):
    total = jnp.where(lane_head == 0, block[0:tokens], 0.0)
    for h in range(1, GROUP // HEAD_DIM):
        total = jnp.where(lane_head == h, block[h * tokens : (h + 1) * tokens], total)
    return total


def lane_heads():
    return lax.broadcasted_iota(jnp.int32, (1, GROUP), 1) // HEAD_DIM


def attend(items):
    scores = [dot_nt(qm, kb) for qm, kb, vb, keep in items]
    weights = []
    for score, (qm, kb, vb, keep) in zip(scores, items):
        score = jnp.where(keep, score, NEG)
        top = jnp.max(score, axis=1, keepdims=True)
        weight = jnp.exp(score - top)
        weight = weight * (1.0 / jnp.sum(weight, axis=1, keepdims=True))
        weights.append(weight.astype(BF16))
    return [dot(weight, vb) for weight, (qm, kb, vb, keep) in zip(weights, items)]


def attend_grad(items):
    scores = [dot_nt(kb, qm) for qm, kb, vb, dom, keep in items]
    grads = [dot_nt(vb, dom) for qm, kb, vb, dom, keep in items]
    middle = []
    for score, grad, (qm, kb, vb, dom, keep) in zip(scores, grads, items):
        score = jnp.where(keep, score, NEG)
        top = jnp.max(score, axis=0, keepdims=True)
        weight = jnp.exp(score - top)
        weight = weight * (1.0 / jnp.sum(weight, axis=0, keepdims=True))
        inner = jnp.sum(weight * grad, axis=0, keepdims=True)
        grad_score = weight * (grad - inner)
        middle.append(
            (weight.astype(BF16), grad_score.astype(BF16), jnp.transpose(grad_score).astype(BF16))
        )
    results = []
    for (weight, grad_score, turned), (qm, kb, vb, dom, keep) in zip(middle, items):
        results.append((dot(turned, kb), dot(grad_score, qm), dot(weight, dom)))
    return results


def box_keep(corners, slot, shape, axis):
    index = lax.broadcasted_iota(jnp.int32, shape, axis) - 1
    grid_row = (index * 2731) >> 15
    grid_col = index - grid_row * GRID
    inside = (grid_col >= corners[slot * 4]) & (grid_col < corners[slot * 4 + 1])
    inside = inside & (grid_row >= corners[slot * 4 + 2]) & (grid_row < corners[slot * 4 + 3])
    return (inside & (index >= 0)) | (index < 0)


def band_loop(total, body, part=None):
    @pl.loop(0, total // (BAND * BANDS))
    def _(step):
        sums = []
        for band in range(BANDS):
            start = pl.multiple_of(step * (BAND * BANDS) + band * BAND, BAND)
            folded = body(pl.ds(start, BAND))
            if folded is not None:
                sums.append(folded)
        for terms in zip(*sums):
            at = terms[0][0]
            part[at] += sum(value for _, value in terms[1:]) + terms[0][1]


def by_columns(left, weight, finish, transposed=False):
    count = weight.shape[0] if transposed else weight.shape[1]
    for start in range(0, count, GROUP):
        cols = slice(start, start + GROUP)
        value = dot_nt(left, weight[cols, :]) if transposed else dot(left, weight[:, cols])
        finish(cols, value)


def both_halves(own, mate, at):
    return jnp.concatenate([own[at[0], at[1] : at[1] + 1], mate[at[0], at[1] : at[1] + 1]], axis=1)


def row_pairs(source, where, first, count, length, finish):
    for at in range(0, count, 2):
        both = [source[where[first + at + n]].astype(F32) for n in range(2)]
        finish(slice(at * length, (at + 2) * length), jnp.concatenate(both, axis=0))


def split_lanes(target, rows, start, value):
    for lane in range(0, value.shape[1], LANES):
        target[(start + lane) // LANES, rows, :] = value[:, lane : lane + LANES]


def join_lanes(source, rows):
    return jnp.concatenate([source[lane, rows, :] for lane in range(source.shape[0])], axis=1)


def fetch_kernel(count, scalars, ins, outs, scratch):
    (source,) = scalars
    (sems,) = scratch
    copies = [
        pltpu.make_async_copy(table.at[source[at]], out.at[at], sems.at[which * count + at])
        for which, (table, out) in enumerate(zip(ins, outs))
        for at in range(count)
    ]
    for copy in copies:
        copy.start()
    for copy in copies:
        copy.wait()


def project_kernel(images, own_images, patch_pad, patch_count, local, scalars, ins, outs, scratch):
    (core,) = scalars
    patches, proj_weight, proj_bias, ain, ain_mate, bias_own, bias_mate = ins
    proj, keys, values = outs
    taken, raw, w1, w2, sems, weight_sems = scratch
    loads = Loads(
        1,
        weight_sems,
        side_by_side(ain.at[1, 1], ain_mate.at[1, 1], w1, local)
        + side_by_side(ain.at[1, 2], ain_mate.at[1, 2], w2, local),
    )
    parts, span = taken.shape[0], taken.shape[1]
    arrivals = Loads(
        1, sems, [(patches.at[pl.ds(n * span, span)], taken.at[n]) for n in range(parts)]
    )
    arrivals.start()
    loads.start()
    rows = span * images
    width = raw.shape[0] * LANES
    for n in range(parts):
        arrivals.wait(n)
        flat = taken[n].reshape(rows, taken.shape[3])
        for start in range(0, width, GROUP):
            cols = slice(start, start + GROUP)
            split_lanes(
                raw,
                slice(n * rows, (n + 1) * rows),
                start,
                dot(flat, proj_weight[:, cols]) + proj_bias[:, cols],
            )
    loads.wait(0, 1, 2, 3)
    bias = both_halves(bias_own, bias_mate, (1, 1))
    first = core[0] * own_images
    rest = jnp.zeros((patch_pad - patch_count, width), F32)

    group = 4

    @pl.loop(0, images // group)
    def _(step):
        both = []
        for at in range(group):
            which = lax.rem(step * group + at + first, images)
            own = jnp.concatenate(
                [
                    raw[lane, pl.ds(which, patch_count, stride=images), :]
                    for lane in range(raw.shape[0])
                ],
                axis=1,
            )
            both.append(jnp.concatenate([own, rest], axis=0))
        low = jnp.concatenate(both, axis=0).astype(BF16)
        some = pl.ds(step * group, group)

        @pl.when(step < own_images // group)
        def _():
            proj[some] = low.reshape(group, patch_pad, width)

        shape = (group, patch_pad, GROUP)
        for start in range(0, width, GROUP):
            cols = slice(start, start + GROUP)
            keys[some, :, cols] = dot(low, w1[:, cols]).astype(BF16).reshape(shape)
            values[some, :, cols] = (
                (dot(low, w2[:, cols]) + bias[:, cols]).astype(BF16).reshape(shape)
            )


def self_kernel(steps, rows, local, length, scalars, ins, outs, scratch):
    lens, where = scalars
    x_in, ain, ain_mate, aout, aout_mate, bias_own, bias_mate, out_bias, gain, shift = ins
    x_out, unit_one, q_out, k_out, v_out, att_own, att_mate, low_out, cross_q, rstd_one = outs
    wq, wk, wv, wo, wc, qs, ks, vs, acc, low, sems = scratch
    total = rows * length
    loads = Loads(
        steps,
        sems,
        side_by_side(ain.at[0, 0], ain_mate.at[0, 0], wq, local)
        + side_by_side(ain.at[0, 1], ain_mate.at[0, 1], wk, local)
        + side_by_side(ain.at[0, 2], ain_mate.at[0, 2], wv, local)
        + one_above(aout.at[0], aout_mate.at[0], wo, local)
        + side_by_side(ain.at[1, 0], ain_mate.at[1, 0], wc, local),
    )
    loads.start()
    bias_q = both_halves(bias_own, bias_mate, (0, 0))
    bias_v = both_halves(bias_own, bias_mate, (0, 1))
    bias_c = both_halves(bias_own, bias_mate, (1, 0))

    def put(at, both):
        x_out[at] = both.astype(BF16)

    base = pl.program_id(0) * rows
    row_pairs(x_in, where, base, rows, length, put)
    xb = x_out[...]

    def keep_q(cols, value):
        value = (value + bias_q[:, cols]).astype(BF16)
        q_out[:, cols] = value
        qs[:, cols] = value.astype(F32) * SCALE

    def keep_k(cols, value):
        value = value.astype(BF16)
        k_out[:, cols] = value
        ks[:, cols] = value.astype(F32)

    def keep_v(cols, value):
        value = (value + bias_v[:, cols]).astype(BF16)
        v_out[:, cols] = value
        vs[:, cols] = value.astype(F32)

    loads.wait(0, 1)
    by_columns(xb, wq, keep_q)
    loads.wait(2, 3)
    by_columns(xb, wk, keep_k)
    loads.wait(4, 5)
    by_columns(xb, wv, keep_v)
    lane_head = lane_heads()
    key_index = lax.broadcasted_iota(jnp.int32, (1, length), 1)

    @pl.loop(0, rows // PAIRED)
    def _(step):
        items, places = [], []
        for row in range(PAIRED):
            row = step * PAIRED + row
            at = pl.ds(pl.multiple_of(row * length, 8), length)
            keep = key_index < lens[base + row]
            for g in range(qs.shape[1] // GROUP):
                lanes = slice(g * GROUP, (g + 1) * GROUP)
                items.append(
                    (
                        spread_heads(qs[at, lanes], lane_head),
                        ks[at, lanes].astype(BF16),
                        vs[at, lanes].astype(BF16),
                        keep,
                    )
                )
                places.append((at, lanes))
        for (at, lanes), result in zip(places, attend(items)):
            acc[at, lanes] = gather_heads(result, lane_head, length)

    def cast(at):
        value = acc[at].astype(BF16)
        low[at] = value
        att_own[at] = value[:, :local]
        att_mate[at] = value[:, local:]

    def to_acc(cols, value):
        acc[:, cols] = value

    band_loop(total, cast)
    loads.wait(6, 7)
    by_columns(low[...], wo, to_acc)

    def norm(at):
        z = x_out[at].astype(F32) + acc[at] + out_bias[0:1]
        unit, rstd = moments(z)
        unit_one[at] = unit
        rstd_one[at] = rstd
        h = (unit * gain[0:1] + shift[0:1]).astype(BF16)
        low[at] = h
        low_out[at] = h

    band_loop(total, norm)
    loads.wait(8, 9)

    def to_query(cols, value):
        cross_q[:, cols] = (value + bias_c[:, cols]).astype(BF16)

    by_columns(low[...], wc, to_query)


def cross_kernel(rows, length, scalars, ins, outs, scratch):
    image, corners = scalars
    queries, keys, values = ins
    (att,) = outs
    qs, acc = scratch
    patch_pad = keys.shape[1]
    lane_head = lane_heads()
    base = pl.program_id(0) * rows

    def spread(at):
        qs[at] = queries[at].astype(F32) * SCALE

    band_loop(rows * length, spread)

    @pl.loop(0, rows // PAIRED)
    def _(step):
        items, places = [], []
        for row in range(PAIRED):
            row = step * PAIRED + row
            at = pl.ds(pl.multiple_of(row * length, 8), length)
            which = image[base + row]
            keep = box_keep(corners, base + row, (1, patch_pad), 1)
            for g in range(qs.shape[1] // GROUP):
                lanes = slice(g * GROUP, (g + 1) * GROUP)
                items.append(
                    (
                        spread_heads(qs[at, lanes], lane_head),
                        keys[which, :, lanes],
                        values[which, :, lanes],
                        keep,
                    )
                )
                places.append((at, lanes))
        for (at, lanes), result in zip(places, attend(items)):
            acc[at, lanes] = gather_heads(result, lane_head, length)

    def cast(at):
        att[at] = acc[at].astype(BF16)

    band_loop(rows * length, cast)


def feed_kernel(steps, rows, local, hidden, length, scalars, ins, outs, scratch):
    (where,) = scalars
    grad_in, att, unit_one, aout, aout_mate, up, up_mate, down, down_mate = ins[:9]
    out_bias, gains, shift, up_bias, up_bias_mate = ins[9:]
    merged, low_out, df_out, do_out, dz_out, a_own, a_mate = outs[:7]
    g_out, du_out = outs[7:9], outs[9:11]
    da_out, sums, up_sums = outs[11:]
    wo, wu, wd, acc, kept, unit_two, rstd_two, low, upstream, even, odd, slope = scratch[:12]
    part, up_part, sems = scratch[12:]
    tiles = hidden // TILE
    total = rows * length
    loads = Loads(
        steps,
        sems,
        one_above(aout.at[1], aout_mate.at[1], wo, local)
        + [
            (source.at[:, pl.ds(t * TILE, TILE)], wu.at[t, :, pl.ds(half * TILE, TILE)])
            for t in range(tiles)
            for half, source in enumerate((up, up_mate))
        ]
        + [
            (source.at[pl.ds(t * TILE, TILE)], wd.at[t, pl.ds(half * TILE, TILE)])
            for t in range(tiles)
            for half, source in enumerate((down, down_mate))
        ],
    )
    loads.start()
    part[...] = jnp.zeros_like(part)

    def put(at, both):
        upstream[at] = both.astype(BF16)

    base = pl.program_id(0) * rows
    row_pairs(grad_in, where, base, rows, length, put)

    def to_acc(cols, value):
        acc[:, cols] = value

    a_own[...] = att[:, :local]
    a_mate[...] = att[:, local:]
    loads.wait(0, 1)
    by_columns(att[...], wo, to_acc)

    def norm_two(at):
        h_one = unit_one[at] * gains[0:1] + shift[0:1]
        unit, rstd = moments(h_one + acc[at] + out_bias[1:2])
        h_two = unit * gains[1:2] + shift[1:2]
        unit_two[at] = unit
        rstd_two[at] = rstd
        kept[at] = h_two
        h_low = h_two.astype(BF16)
        low[at] = h_low
        low_out[at] = h_low

    band_loop(total, norm_two)
    acc[...] = jnp.zeros_like(acc)
    loads.wait(*range(2, 2 + 4 * tiles))
    biases = (up_bias, up_bias_mate)

    def activate(units, t):
        cols = slice(t * TILE, (t + 1) * TILE)
        for half in range(2):
            lanes = slice(half * TILE, (half + 1) * TILE)
            bias = biases[half][:, cols]
            for start in range(0, total, BAND):
                at = slice(start, start + BAND)
                active, sloped = gelu(units[at, lanes] + bias)
                g_out[half][at, cols] = active.astype(BF16)
                slope[t, at, lanes] = sloped

    def add_down(t):
        cols = slice(t * TILE, (t + 1) * TILE)
        both = jnp.concatenate([g_out[0][:, cols], g_out[1][:, cols]], axis=1)
        acc[...] += dot(both, wd[t])

    units = (even, odd)
    even[...] = dot(low[...], wu[0])
    for t in range(tiles):
        if t + 1 < tiles:
            units[(t + 1) % 2][...] = dot(low[...], wu[t + 1])
        activate(units[t % 2], t)
        add_down(t)

    def norm_three(at):
        unit, rstd = moments(kept[at] + acc[at] + out_bias[2:3])
        gain = gains[2:3]
        unit_three = unit * gain + shift[2:3]
        grad = upstream[at].astype(F32)
        dz = norm_grad(unit, rstd, gain, grad)
        kept[at] = dz
        acc[at] = unit_three
        dz_low = dz.astype(BF16)
        low[at] = dz_low
        df_out[at] = dz_low
        return (
            (0, fold(dz_low.astype(F32))),
            (1, fold(grad * unit)),
            (2, fold(grad)),
        )

    band_loop(total, norm_three, part)

    for row in range(rows):
        merged[where[base + row]] = acc[row * length : (row + 1) * length].astype(BF16)
    acc[...] = jnp.zeros_like(acc)

    for t in range(tiles):
        cols = slice(t * TILE, (t + 1) * TILE)
        grads = dot_nt(low[...], wd[t])
        for half in range(2):
            lanes = slice(half * TILE, (half + 1) * TILE)
            folded = 0.0
            for start in range(0, total, BAND):
                at = slice(start, start + BAND)
                du = (grads[at, lanes] * slope[t, at, lanes]).astype(BF16)
                du_out[half][at, cols] = du
                folded = folded + fold(du.astype(F32))
            up_part[half, :, cols] = folded
        both = jnp.concatenate([du_out[0][:, cols], du_out[1][:, cols]], axis=1)
        acc[...] += dot_nt(both, wu[t])

    def norm_two_back(at):
        grad = kept[at] + acc[at]
        unit = unit_two[at]
        dz = norm_grad(unit, rstd_two[at], gains[1:2], grad)
        dz_out[at] = dz
        dz_low = dz.astype(BF16)
        low[at] = dz_low
        do_out[at] = dz_low
        return (
            (3, fold(dz_low.astype(F32))),
            (4, fold(grad * unit)),
            (5, fold(grad)),
        )

    band_loop(total, norm_two_back, part)

    def to_grad(cols, value):
        da_out[:, cols] = value.astype(BF16)

    by_columns(low[...], wo, to_grad, transposed=True)
    for at in range(8):
        sums[0, at : at + 1] = jnp.sum(part[at], axis=0, keepdims=True)
    for half in range(2):
        up_sums[0, half : half + 1] = jnp.sum(up_part[half], axis=0, keepdims=True)


def cross_grad_kernel(steps, rows, length, scalars, ins, outs, scratch):
    image, corners = scalars
    queries, grads, keys, values = ins
    own, mate, grad_queries = outs
    qs, gs, acc, dk, dv = scratch
    patch_pad = keys.shape[1]

    def clear():
        @pl.loop(0, dk.shape[0])
        def _(at):
            dk[at] = jnp.zeros(dk.shape[1:], F32)
            dv[at] = jnp.zeros(dv.shape[1:], F32)

    pl.when(pl.program_id(0) == 0)(clear)

    def spread(at):
        qs[at] = queries[at].astype(F32) * SCALE
        gs[at] = grads[at].astype(F32)

    band_loop(rows * length, spread)
    lane_head = lane_heads()
    base = pl.program_id(0) * rows

    @pl.loop(0, rows // PAIRED)
    def _(step):
        items, places = [], []
        for row in range(PAIRED):
            row = step * PAIRED + row
            at = pl.ds(pl.multiple_of(row * length, 8), length)
            which = image[base + row]
            keep = box_keep(corners, base + row, (patch_pad, 1), 0)
            for g in range(qs.shape[1] // GROUP):
                lanes = slice(g * GROUP, (g + 1) * GROUP)
                items.append(
                    (
                        spread_heads(qs[at, lanes], lane_head),
                        keys[which, :, lanes],
                        values[which, :, lanes],
                        spread_heads(gs[at, lanes], lane_head),
                        keep,
                    )
                )
                places.append((at, which, lanes))
        for (at, which, lanes), (grad_q, grad_k, grad_v) in zip(places, attend_grad(items)):
            acc[at, lanes] = gather_heads(grad_q, lane_head, length) * SCALE
            dk[which, :, lanes] += grad_k
            dv[which, :, lanes] += grad_v

    def cast(at):
        grad_queries[at] = acc[at].astype(BF16)

    band_loop(rows * length, cast)

    @pl.when(pl.program_id(0) == steps - 1)
    def _():
        half = own.shape[1]

        @pl.loop(0, half)
        def _(at):
            own[0, at] = dk[at].astype(BF16)
            own[1, at] = dv[at].astype(BF16)
            mate[0, at] = dk[half + at].astype(BF16)
            mate[1, at] = dv[half + at].astype(BF16)


def image_kernel(images, patch_count, local, scalars, ins, outs, scratch):
    (core,) = scalars
    piece, piece_mate, patches, proj_weight, ain, ain_mate = ins
    kv_own, kv_mate, patch_grad, weight_grad, sums = outs
    narrow, wide, taken, w1, w2, part, sems, weight_sems = scratch
    parts, span = taken.shape[0], taken.shape[1]
    loads = Loads(
        1,
        weight_sems,
        side_by_side(ain.at[1, 1], ain_mate.at[1, 1], w1, local)
        + side_by_side(ain.at[1, 2], ain_mate.at[1, 2], w2, local),
    )
    arrivals = Loads(
        1, sems, [(patches.at[pl.ds(n * span, span)], taken.at[n]) for n in range(parts)]
    )
    loads.start()
    arrivals.start()
    part[...] = jnp.zeros_like(part)
    own_images, patch_pad = piece.shape[1], piece.shape[2]
    width = w1.shape[0]

    slab = 80

    @pl.loop(0, wide.shape[1] // slab)
    def _(step):
        at = pl.ds(pl.multiple_of(step * slab, slab), slab)
        for lane in range(wide.shape[0]):
            wide[lane, at] = jnp.zeros((slab, LANES), F32)

    loads.wait(0, 1, 2, 3)
    first = core[0] * own_images

    @pl.loop(0, own_images // 2)
    def _(step):
        pair = pl.ds(step * 2, 2)
        halves = []
        for half in (slice(0, local), slice(local, width)):
            swapped = slice(width - half.stop, width - half.start)
            both = piece[:, pair, :, half].astype(F32) + piece_mate[:, pair, :, swapped].astype(F32)
            both = both.astype(BF16)
            halves.append([both[at].reshape(2 * patch_pad, local) for at in range(2)])
        (dk_own, dv_own), (dk_mate, dv_mate) = halves
        rows = pl.ds(pl.multiple_of(step * 2 * patch_pad, 2 * patch_pad), 2 * patch_pad)
        kv_own[rows, :local] = dk_own
        kv_own[rows, local:] = dv_own
        kv_mate[rows, :local] = dk_mate
        kv_mate[rows, local:] = dv_mate
        dk = jnp.concatenate([dk_own, dk_mate], axis=1)
        dv = jnp.concatenate([dv_own, dv_mate], axis=1)
        part[1] += fold(dv.astype(F32))
        for start in range(0, width, GROUP):
            cols = slice(start, start + GROUP)
            grad = dot_nt(dk, w1[cols, :]) + dot_nt(dv, w2[cols, :])
            grad = grad.astype(BF16).astype(F32)
            part[0, :, cols] += fold(grad)
            for at in range(2):
                one = grad[at * patch_pad : at * patch_pad + patch_count]
                which = step * 2 + at
                spot = pl.ds(which, patch_count, stride=own_images)
                split_lanes(narrow, spot, start, one)
                split_lanes(wide, pl.ds(which + first, patch_count, stride=images), start, one)

    for n in range(parts):
        arrivals.wait(n)
        few = slice(n * span * own_images, (n + 1) * span * own_images)
        some = join_lanes(narrow, few).astype(BF16)
        for start in range(0, proj_weight.shape[0], GROUP):
            cols = slice(start, start + GROUP)
            back = dot_nt(some, proj_weight[cols, :]).astype(BF16)
            patch_grad[n * span : (n + 1) * span, :, cols] = back.reshape(span, own_images, GROUP)
        flat = taken[n].reshape(span * images, taken.shape[3])
        grad = join_lanes(wide, slice(n * span * images, (n + 1) * span * images)).astype(BF16)
        product = dot_tn(flat, grad)
        if n == 0:
            weight_grad[...] = product
        else:
            weight_grad[...] += product
    for at in range(2):
        sums[at : at + 1] = jnp.sum(part[at], axis=0, keepdims=True)


def self_grad_kernel(steps, rows, local, length, scalars, ins, outs, scratch):
    lens, where = scalars
    dq2, unit_one, rstd_one, dz_two, q_in, k_in, v_in, ain, ain_mate, aout, aout_mate, gain = ins
    text_grad, do_out, dq2_own, dq2_mate, qkv_own, qkv_mate, sums = outs
    wc, wo, wq, wk, wv, acc, kept, low, low_k, low_v, qs, ks, vs, part, sems = scratch
    total = rows * length
    loads = Loads(
        steps,
        sems,
        side_by_side(ain.at[1, 0], ain_mate.at[1, 0], wc, local)
        + one_above(aout.at[0], aout_mate.at[0], wo, local)
        + side_by_side(ain.at[0, 0], ain_mate.at[0, 0], wq, local)
        + side_by_side(ain.at[0, 1], ain_mate.at[0, 1], wk, local)
        + side_by_side(ain.at[0, 2], ain_mate.at[0, 2], wv, local),
    )
    loads.start()
    part[...] = jnp.zeros_like(part)

    def to_acc(cols, value):
        acc[:, cols] = value

    loads.wait(0, 1)
    by_columns(dq2[...], wc, to_acc, transposed=True)

    def norm_back(at):
        unit = unit_one[at]
        grad = dz_two[at] + acc[at]
        dz = norm_grad(unit, rstd_one[at], gain[0:1], grad)
        kept[at] = dz
        dz_low = dz.astype(BF16)
        low[at] = dz_low
        do_out[at] = dz_low
        qs[at] = q_in[at].astype(F32) * SCALE
        ks[at] = k_in[at].astype(F32)
        vs[at] = v_in[at].astype(F32)
        query = dq2[at]
        dq2_own[at] = query[:, :local]
        dq2_mate[at] = query[:, local:]
        return (
            (0, fold(dz_low.astype(F32))),
            (1, fold(grad * unit)),
            (2, fold(grad)),
            (5, fold(query.astype(F32))),
        )

    band_loop(total, norm_back, part)
    loads.wait(2, 3)
    by_columns(low[...], wo, to_acc, transposed=True)
    lane_head = lane_heads()
    key_index = lax.broadcasted_iota(jnp.int32, (length, 1), 0)
    base = pl.program_id(0) * rows

    @pl.loop(0, rows // PAIRED)
    def _(step):
        items, places = [], []
        for row in range(PAIRED):
            row = step * PAIRED + row
            at = pl.ds(pl.multiple_of(row * length, 8), length)
            keep = key_index < lens[base + row]
            for g in range(qs.shape[1] // GROUP):
                lanes = slice(g * GROUP, (g + 1) * GROUP)
                items.append(
                    (
                        spread_heads(qs[at, lanes], lane_head),
                        ks[at, lanes].astype(BF16),
                        vs[at, lanes].astype(BF16),
                        spread_heads(acc[at, lanes], lane_head),
                        keep,
                    )
                )
                places.append((at, lanes))
        for (at, lanes), (grad_q, grad_k, grad_v) in zip(places, attend_grad(items)):
            qs[at, lanes] = gather_heads(grad_q, lane_head, length) * SCALE
            ks[at, lanes] = grad_k
            vs[at, lanes] = grad_v

    def cast(at):
        sums = []
        for slot, (source, target) in enumerate(((qs, low), (ks, low_k), (vs, low_v))):
            value = source[at].astype(BF16)
            target[at] = value
            qkv_own[at, slot * local : (slot + 1) * local] = value[:, :local]
            qkv_mate[at, slot * local : (slot + 1) * local] = value[:, local:]
            if slot != 1:
                sums.append((3 + slot // 2, fold(value.astype(F32))))
        return sums

    band_loop(total, cast, part)
    loads.wait(4, 5, 6, 7, 8, 9)
    for start in range(0, kept.shape[1], GROUP):
        cols = slice(start, start + GROUP)
        acc[:, cols] = (
            kept[:, cols]
            + dot_nt(low[...], wq[cols, :])
            + dot_nt(low_k[...], wk[cols, :])
            + dot_nt(low_v[...], wv[cols, :])
        )

    for row in range(rows):
        text_grad[where[base + row]] = acc[row * length : (row + 1) * length].astype(BF16)
    for at in range(8):
        sums[0, at : at + 1] = jnp.sum(part[at], axis=0, keepdims=True)


def pack_kernel(local, hidden, scalars, ins, outs, scratch):
    (core,) = scalars
    feed, up, self_, image = ins
    feed_sum = jnp.sum(feed[...], axis=0)
    self_sum = jnp.sum(self_[...], axis=0)
    up_sum = jnp.sum(up[...], axis=0)
    common = [(0, 0), (1, 3), (1, 0), (0, 1), (1, 4), (1, 1), (0, 2), (1, 5), (1, 2)]
    even = core[0] == 0
    for out, mine in zip(outs, (True, False)):
        out[...] = jnp.zeros_like(out)
        at = 0
        for which, row in common:
            source = feed_sum if which else self_sum
            for half in range(2):
                out[at : at + 1] = source[row : row + 1, half * local : (half + 1) * local]
                at += 1
        lanes = slice(0, local) if mine else slice(local, 2 * local)
        for row in (3, 4, 5):
            out[at : at + 1] = self_sum[row : row + 1, lanes]
            at += 1
        out[at : at + 1] = image[1:2, lanes]
        at += 1
        half = 0 if mine else 1
        for start in range(0, hidden, local):
            out[at : at + 1] = up_sum[half : half + 1, start : start + local]
            at += 1
        low, high = image[0:1, :local], image[0:1, local:]
        out[at : at + 1] = jnp.where(even == mine, low, high)


def halve_kernel(rows, length, scalars, ins, outs, scratch):
    core, where = scalars
    (tall,) = scratch

    def put(at, both):
        split_lanes(tall, at, 0, both)

    row_pairs(ins[0], where, 0, rows, length, put)
    half = length // 2
    for out, first in zip(outs, (core[0] * half, (1 - core[0]) * half)):
        for token in range(half):
            out[token] = join_lanes(
                tall, pl.ds(first + token, rows, stride=length)
            ).astype(BF16)


def place_kernel(scalars, ins, outs, scratch):
    own, mate, place = ins
    (out,) = outs
    count, slots = out.shape[1], own.shape[1]
    index = lax.broadcasted_iota(jnp.int32, (count, slots), 1)
    from_own = jnp.where(place[...] == index, 1.0, 0.0).astype(BF16)
    from_mate = jnp.where(place[...] == index + slots, 1.0, 0.0).astype(BF16)
    for token in range(out.shape[0]):
        out[token] = (dot(from_own, own[token]) + dot(from_mate, mate[token])).astype(BF16)


def body(
    text,
    cotangent,
    lengths,
    box_corners,
    box_counts,
    region_box,
    patches,
    proj_weight,
    proj_bias,
    attention_in,
    attention_bias,
    attention_out,
    output_bias,
    norm_gain,
    norm_bias,
    up_weight,
    up_bias,
    down_weight,
):
    rows, length, width = text.shape
    images, patch_count, vision = patches.shape
    local = attention_in.shape[-1]
    hidden = up_weight.shape[-1]
    devices = lax.axis_size("dp")
    me, core = lax.axis_index("dp"), lax.axis_index("mp")
    pair = -(-rows // devices)
    each, odd = pair // 2, pair % 2
    deep = each + odd
    slots = devices * each + devices // 2 * odd
    patch_pad = -(-patch_count // 16) * 16
    own_images = images // 2
    step_rows = 12 if slots % 12 == 0 else 8
    steps = slots // step_rows
    tokens = step_rows * length
    all_tokens = slots * length
    full = slots * 2 == rows
    core_scalar = core.astype(jnp.int32).reshape(1)

    def mate(value):
        return lax.ppermute(value, "mp", [(0, 1), (1, 0)])

    def tie(*values):
        return lax.optimization_barrier(values)

    def exchange(value):
        return lax.all_to_all(value, "dp", split_axis=0, concat_axis=0, tiled=True)

    ain_mate = mate(attention_in)
    bias_mate = mate(attention_bias)
    aout_mate = mate(attention_out)
    up_bias_own = up_bias.reshape(1, hidden)
    up_bias_mate = mate(up_bias_own)
    up_mate = mate(up_weight)
    down_mate = mate(down_weight)

    number = jnp.arange(rows, dtype=jnp.int32)
    target = region_box // rows
    earlier = (target[:, None] == target[None, :]) & (number[None, :] < number[:, None])
    nth = jnp.sum(earlier.astype(jnp.int32), axis=1)
    even_part = nth < 2 * each
    row_core = jnp.where(even_part, nth // max(each, 1), (target ^ me) & 1)
    depth = jnp.where(even_part, nth % max(each, 1), each)
    spot = jnp.arange(devices * deep, dtype=jnp.int32)
    hit = (spot[:, None] == (target * deep + depth)[None, :]) & (row_core == core)[None, :]
    source = jnp.sum(jnp.where(hit, number[None, :], 0), axis=1)
    slot = jnp.where(even_part, target * each + depth, devices * each + (target >> 1))
    place = jnp.where(row_core == core, slot, slot + slots)[:, None]
    order = jnp.arange(slots, dtype=jnp.int32)
    late = order - devices * each
    where = jnp.where(
        late < 0,
        order // max(each, 1) * deep + order % max(each, 1),
        (2 * late + ((me & 1) ^ core)) * deep + each,
    )
    meta = jnp.concatenate(
        [(region_box % rows)[:, None], lengths[:, None], box_corners], axis=1
    )
    meta_out = jnp.sum(jnp.where(hit[:, :, None], meta[None], 0), axis=1)
    if not full:
        empty = jnp.array([0, 1, 0, 1, 0, 1], jnp.int32)
        meta_out = jnp.where(jnp.any(hit, axis=1)[:, None], meta_out, empty[None])
    arrived = exchange(meta_out)[where]
    ends = jnp.cumsum(box_counts[0])
    image = jnp.sum((ends[None, :] <= arrived[:, 0:1]).astype(jnp.int32), axis=1)
    image = (image + own_images * core) % images
    lens = arrived[:, 1]
    corners = arrived[:, 2:].reshape(-1)

    block_shape = (devices * deep, length, width)
    if full:
        x_out, upstream_out = run(
            partial(fetch_kernel, devices * deep),
            1,
            [source],
            [(text, ANY), (cotangent, ANY)],
            [(block_shape, BF16, whole_spec(block_shape))] * 2,
            [pltpu.SemaphoreType.DMA((2 * devices * deep,))],
            0,
        )
    else:
        valid = jnp.any(hit, axis=1)[:, None, None]
        x_out = jnp.where(valid, text[source], 0)
        upstream_out = jnp.where(valid, cotangent[source], 0)
    x_in = exchange(x_out)

    patches, aout_mate, image, corners, lens = tie(patches, aout_mate, image, corners, lens)
    by_patch = jnp.transpose(patches, (1, 0, 2))
    parts = next(n for n in (5, 4, 3, 2, 1) if patch_count % n == 0)
    weight_scratch = pltpu.VMEM((width, width), BF16)

    def slabs(count):
        return pltpu.VMEM((width // LANES, count, LANES), F32)

    patch_scratch = pltpu.VMEM((parts, patch_count // parts, images, vision), BF16)
    image_shape = (images, patch_pad, width)
    proj, keys, values = run(
        partial(project_kernel, images, own_images, patch_pad, patch_count, local),
        1,
        [core_scalar],
        [
            (by_patch, ANY),
            (proj_weight, whole_spec(proj_weight.shape)),
            (proj_bias.reshape(1, width), whole_spec((1, width))),
            (attention_in, ANY),
            (ain_mate, ANY),
            (attention_bias, whole_spec(attention_bias.shape)),
            (bias_mate, whole_spec(bias_mate.shape)),
        ],
        [((own_images,) + image_shape[1:], BF16, whole_spec((own_images,) + image_shape[1:]))]
        + [(image_shape, BF16, whole_spec(image_shape))] * 2,
        [
            patch_scratch,
            slabs(patch_count * images),
            weight_scratch,
            weight_scratch,
            pltpu.SemaphoreType.DMA((parts,)),
            pltpu.SemaphoreType.DMA((4,)),
        ],
        2 * images * patch_pad * width * (vision + 2 * width),
    )

    upstream_out, proj, keys, values = tie(upstream_out, proj, keys, values)
    upstream_in = exchange(upstream_out)

    def token_in(value):
        return (value, rows_spec((tokens, value.shape[1]), 0))

    def token_out(cols, dtype):
        return ((all_tokens, cols), dtype, rows_spec((tokens, cols), 0))

    block_out = (block_shape, BF16, whole_spec(block_shape))

    def f32_tokens(cols):
        return pltpu.VMEM((tokens, cols), F32)

    def low_tokens(cols):
        return pltpu.VMEM((tokens, cols), BF16)

    def whole(value):
        return (value, whole_spec(value.shape))

    attention_flops = 4 * 4 * all_tokens * width * 64

    x, unit_one, q_self, k_self, v_self, att_own, att_mate, self_low, queries, rstd_one = run(
        partial(self_kernel, steps, step_rows, local, length),
        steps,
        [lens, where],
        [
            whole(x_in),
            (attention_in, ANY),
            (ain_mate, ANY),
            (attention_out, ANY),
            (aout_mate, ANY),
            whole(attention_bias),
            whole(bias_mate),
            whole(output_bias),
            whole(norm_gain),
            whole(norm_bias),
        ],
        [token_out(width, BF16), token_out(width, F32)]
        + [token_out(width, BF16)] * 3
        + [token_out(local, BF16)] * 2
        + [token_out(width, BF16)] * 2
        + [token_out(1, F32)],
        [weight_scratch] * 5
        + [f32_tokens(width)] * 4
        + [low_tokens(width), pltpu.SemaphoreType.DMA((10,))],
        2 * all_tokens * width * width * 5 + attention_flops,
    )

    (attended,) = run(
        partial(cross_kernel, step_rows, length),
        steps,
        [image, corners],
        [token_in(queries), whole(keys), whole(values)],
        [token_out(width, BF16)],
        [f32_tokens(width)] * 2,
        attention_flops * 4,
    )

    result = run(
        partial(feed_kernel, steps, step_rows, local, hidden, length),
        steps,
        [where],
        [
            whole(upstream_in),
            token_in(attended),
            token_in(unit_one),
            (attention_out, ANY),
            (aout_mate, ANY),
            (up_weight, ANY),
            (up_mate, ANY),
            (down_weight, ANY),
            (down_mate, ANY),
            whole(output_bias),
            whole(norm_gain),
            whole(norm_bias),
            whole(up_bias_own),
            whole(up_bias_mate),
        ],
        [block_out]
        + [token_out(width, BF16)] * 3
        + [token_out(width, F32)]
        + [token_out(local, BF16)] * 2
        + [token_out(hidden, BF16)] * 4
        + [
            token_out(width, BF16),
            ((steps, 8, width), F32, rows_spec((1, 8, width), 0)),
            ((steps, 2, hidden), F32, rows_spec((1, 2, hidden), 0)),
        ],
        [weight_scratch]
        + [
            pltpu.VMEM((hidden // TILE, width, 2 * TILE), BF16),
            pltpu.VMEM((hidden // TILE, 2 * TILE, width), BF16),
        ]
        + [f32_tokens(width)] * 3
        + [f32_tokens(1), low_tokens(width), low_tokens(width)]
        + [f32_tokens(2 * TILE)] * 2
        + [pltpu.VMEM((hidden // TILE, tokens, 2 * TILE), F32)]
        + [pltpu.VMEM((8, 8, width), F32), pltpu.VMEM((2, 8, hidden), F32)]
        + [pltpu.SemaphoreType.DMA((2 + 4 * hidden // TILE,))],
        2 * all_tokens * width * (2 * width + 8 * hidden),
    )
    merged_out, cross_low, grad_ffn, grad_cross, dz_two, a_own, a_mate = result[:7]
    g_own, g_mate, du_own, du_mate, grad_att, feed_sums, up_sums = result[7:]

    bits = devices.bit_length() - 1

    def partner_bits(value, mask):
        return lax.ppermute(value, "dp", [(d, d ^ mask) for d in range(devices)])

    def opened(value):
        return value.reshape((2,) * bits + (value.shape[0] // devices, value.shape[1]))

    def swap(value, axis, bit):
        mine = (me >> bit) & 1
        away = lax.dynamic_index_in_dim(value, 1 - mine, axis, keepdims=False)
        stay = lax.dynamic_index_in_dim(value, mine, axis, keepdims=False)
        return stay, partner_bits(away, 1 << bit)

    def first_swaps(by_x, by_y):
        return swap(opened(by_x), bits - 1, 0) + swap(opened(by_y), bits - 2, 1)

    def second_swaps(stay_x, got_x, stay_y, got_y):
        return swap(add(stay_x, got_x), bits - 2, 1) + swap(add(stay_y, got_y), bits - 2, 0)

    def add(stay, got):
        return (stay.astype(F32) + got.astype(F32)).astype(BF16)

    def last_parts(stay_x, got_x, stay_y, got_y):
        parts = [add(stay_x, got_x), add(stay_y, got_y)]
        return jnp.concatenate(
            [part.reshape((devices // 4,) + part.shape[-2:]) for part in parts], axis=2
        )

    def last_sum(both, first_width):
        groups = [[low + 4 * n for n in range(devices // 4)] for low in range(4)]
        both = lax.all_to_all(
            both, "dp", split_axis=0, concat_axis=0, axis_index_groups=groups, tiled=True
        )
        total = jnp.sum(both.astype(F32), axis=0)
        return total[:, :first_width], total[:, first_width:]

    def low_tn(left, right):
        return dot_tn(left, right).astype(BF16)

    merged_in = exchange(merged_out)
    up_away, down_away = low_tn(cross_low, du_mate), low_tn(grad_ffn, g_mate)
    grad_att, queries, up_away, down_away = tie(grad_att, queries, up_away, down_away)
    up_got, down_got = mate(up_away), mate(down_away)

    half_shape = (2, own_images, patch_pad, width)
    image_acc = pltpu.VMEM(image_shape, F32)
    piece, piece_out, grad_queries = run(
        partial(cross_grad_kernel, steps, step_rows, length),
        steps,
        [image, corners],
        [token_in(queries), token_in(grad_att), whole(keys), whole(values)],
        [(half_shape, BF16, whole_spec(half_shape))] * 2 + [token_out(width, BF16)],
        [f32_tokens(width)] * 3 + [image_acc] * 2,
        attention_flops * 12,
    )
    piece_mate = mate(piece_out)

    up_part = (dot_tn(cross_low, du_own) + up_got.astype(F32)).astype(BF16)
    down_part = (dot_tn(grad_ffn, g_own) + down_got.astype(F32)).astype(BF16)
    grad_queries, up_part, down_part = tie(grad_queries, up_part, down_part)
    feed_stage = first_swaps(up_part, down_part)

    result = run(
        partial(self_grad_kernel, steps, step_rows, local, length),
        steps,
        [lens, where],
        [
            token_in(grad_queries),
            token_in(unit_one),
            token_in(rstd_one),
            token_in(dz_two),
            token_in(q_self),
            token_in(k_self),
            token_in(v_self),
            (attention_in, ANY),
            (ain_mate, ANY),
            (attention_out, ANY),
            (aout_mate, ANY),
            whole(norm_gain),
        ],
        [block_out]
        + [token_out(width, BF16)]
        + [token_out(local, BF16)] * 2
        + [token_out(3 * local, BF16)] * 2
        + [((steps, 8, width), F32, rows_spec((1, 8, width), 0))],
        [weight_scratch] * 5
        + [f32_tokens(width)] * 2
        + [low_tokens(width)] * 3
        + [f32_tokens(width)] * 3
        + [pltpu.VMEM((8, 8, width), F32), pltpu.SemaphoreType.DMA((10,))],
        2 * all_tokens * width * width * 5 + attention_flops * 2,
    )
    text_out, grad_self, dq_own, dq_mate, qkv_own, qkv_mate, self_sums = result
    text_in = exchange(text_out)

    flat_images = own_images * patch_pad
    patch_grad_shape = (patch_count, own_images, vision)
    result = run(
        partial(image_kernel, images, patch_count, local),
        1,
        [core_scalar],
        [
            whole(piece),
            whole(piece_mate),
            (by_patch, ANY),
            whole(proj_weight),
            (attention_in, ANY),
            (ain_mate, ANY),
        ],
        [
            ((flat_images, width), BF16, whole_spec((flat_images, width))),
            ((flat_images, width), BF16, whole_spec((flat_images, width))),
            (patch_grad_shape, BF16, whole_spec(patch_grad_shape)),
            ((vision, width), F32, whole_spec((vision, width))),
            ((8, width), F32, whole_spec((8, width))),
        ],
        [
            slabs(patch_count * own_images),
            slabs(patch_count * images),
            patch_scratch,
            weight_scratch,
            weight_scratch,
            pltpu.VMEM((2, 8, width), F32),
            pltpu.SemaphoreType.DMA((parts,)),
            pltpu.SemaphoreType.DMA((4,)),
        ],
        2 * flat_images * width * (2 * width + 2 * vision),
        (),
        [qkv_mate, qkv_own, grad_self, dq_mate, dq_own],
    )
    kv_own, kv_mate, patch_grad, proj_weight_sum, image_sums = result[:5]
    qkv_mate, qkv_own, grad_self, dq_mate, dq_own = result[5:]

    self_away = jnp.concatenate(
        [
            low_tn(x, qkv_mate),
            low_tn(grad_self, att_mate),
            low_tn(grad_cross, a_mate),
            low_tn(self_low, dq_mate),
        ],
        axis=1,
    )
    self_got = mate(self_away)
    feed_stage = tie(self_away, *feed_stage)[1:]
    feed_stage = second_swaps(*feed_stage)
    self_own = jnp.concatenate(
        [
            dot_tn(x, qkv_own),
            dot_tn(grad_self, att_own),
            dot_tn(grad_cross, a_own),
            dot_tn(self_low, dq_own),
        ],
        axis=1,
    )
    self_part = (self_own + self_got.astype(F32)).astype(BF16)
    half_width = self_part.shape[1] // 2
    self_stage = first_swaps(self_part[:, :half_width], self_part[:, half_width:])
    feed_parts = last_parts(*feed_stage)

    up_grad, down_grad = last_sum(feed_parts, hidden)
    self_got_x, self_got_y = self_stage[1], self_stage[3]
    self_stage = second_swaps(*self_stage)
    kv_low = proj.reshape(flat_images, width)
    kv_away = low_tn(kv_low, kv_mate)
    kv_got = mate(kv_away)
    proj_away = lax.dynamic_slice_in_dim(proj_weight_sum, (1 - core) * local, local, 1)
    proj_got = mate(proj_away.astype(BF16))
    kv_part = (dot_tn(kv_low, kv_own) + kv_got.astype(F32)).astype(BF16)
    proj_own = lax.dynamic_slice_in_dim(proj_weight_sum, core * local, local, 1)
    proj_part = (proj_own + proj_got.astype(F32)).astype(BF16)
    proj_part = proj_part.reshape(width, vision * local // width)
    image_stage = first_swaps(kv_part, proj_part)
    self_one, self_two = last_sum(last_parts(*self_stage), half_width)
    image_stage = second_swaps(*image_stage)
    kv_grad, proj_grad = last_sum(last_parts(*image_stage), width)
    proj_grad = proj_grad.reshape(vision // devices, local)

    lines = 23 + hidden // local
    packed_shape = (-(-lines // 8) * 8, local)
    small, small_out = run(
        partial(pack_kernel, local, hidden),
        1,
        [core_scalar],
        [whole(feed_sums), whole(up_sums), whole(self_sums), whole(image_sums)],
        [(packed_shape, F32, whole_spec(packed_shape))] * 2,
        [],
        0,
        [kv_part, proj_part, self_got_x, self_got_y],
    )
    small = small + mate(small_out)
    for bit in range(bits):
        small = small + partner_bits(small, 1 << bit)
    common = small[:18].reshape(3, 3, width)
    bias_grad = small[18:22].reshape(2, 2, local)
    up_bias_grad = small[22 : 22 + hidden // local].reshape(hidden)
    proj_bias_grad = small[22 + hidden // local]

    ready = [self_one[:, at * local : (at + 1) * local] for at in range(3)]
    out_self, out_cross, query_cross = [
        self_two[:, at * local : (at + 1) * local] for at in range(3)
    ]
    in_grad = jnp.stack(
        ready + [query_cross, kv_grad[:, :local], kv_grad[:, local:]]
    ).reshape(2, 3, width // devices, local)
    out_grad = jnp.stack([out_self.T, out_cross.T])

    def tokens_out(value, after, after_place):
        shape = (length // 2, slots, width)
        own, away = run(
            partial(halve_kernel, slots, length),
            1,
            [core_scalar, where],
            [whole(value)],
            [(shape, BF16, whole_spec(shape))] * 2,
            [slabs(all_tokens)],
            0,
            after,
        )
        shape = (length // 2, rows, width)
        (out,) = run(
            place_kernel,
            1,
            [],
            [whole(own), whole(mate(away)), whole(place)],
            [(shape, BF16, whole_spec(shape))],
            [],
            0,
            after_place,
        )
        return jnp.transpose(out, (1, 0, 2))

    return (
        tokens_out(merged_in, [self_part], [kv_part]),
        tokens_out(text_in, [kv_away, self_part], [kv_part, proj_part]),
        jnp.transpose(patch_grad, (1, 0, 2)),
        proj_grad,
        proj_bias_grad,
        in_grad,
        bias_grad,
        out_grad,
        common[0],
        common[1],
        common[2],
        up_grad,
        up_bias_grad,
        down_grad.T,
    )


def solution(mesh):
    placed = (
        P("dp", None, None),
        P("dp", None, None),
        P("dp"),
        P("dp", None),
        P("dp", None),
        P("dp"),
        P("dp", None, None),
        P(),
        P(),
        P(None, None, None, "mp"),
        P(None, None, "mp"),
        P(None, "mp", None),
        P(),
        P(),
        P(),
        P(None, "mp"),
        P("mp"),
        P("mp", None),
    )
    return jax.shard_map(
        body,
        mesh=mesh,
        in_specs=placed,
        out_specs=(
            P("dp", "mp", None),
            P("dp", "mp", None),
            P(("dp", "mp"), None, None),
            P("dp", "mp"),
            P("mp"),
            P(None, None, "dp", "mp"),
            P(None, None, "mp"),
            P(None, "mp", "dp"),
            P(),
            P(),
            P(),
            P("dp", "mp"),
            P("mp"),
            P("mp", "dp"),
        ),
        check_vma=False,
    )
```

```python
import math
from functools import partial

import jax
import jax.numpy as jnp
from jax import lax
from jax.experimental import pallas as pl
from jax.experimental.pallas import tpu as pltpu
from jax.sharding import PartitionSpec as P

HEAD_DIM = 64
GRID = 12
EPS = 1e-12
NEG = -1e30
SCALE = HEAD_DIM ** (-0.5)

F32 = jnp.float32
BF16 = jnp.bfloat16

GROUP = 4 * HEAD_DIM
BAND = 32
BANDS = 5
LANES = 128
TILE = 256
PAIRED = 4
VMEM_LIMIT = 58 << 20


def dot(left, right):
    return lax.dot_general(left, right, (((1,), (0,)), ((), ())), preferred_element_type=F32)


def dot_nt(left, right):
    return lax.dot_general(left, right, (((1,), (1,)), ((), ())), preferred_element_type=F32)


def dot_tn(left, right):
    return lax.dot_general(left, right, (((0,), (0,)), ((), ())), preferred_element_type=F32)


def rows_spec(block, offset):
    rank = len(block)
    return pl.BlockSpec(block, lambda s, *_: (s + offset,) + (0,) * (rank - 1))


def whole_spec(shape):
    rank = len(shape)
    return pl.BlockSpec(shape, lambda s, *_: (0,) * rank, pipeline_mode=pl.Buffered(1))


ANY = pl.BlockSpec(memory_space=pl.ANY)


def run(body, steps, scalars, ins, outs, scratch, flops, after=(), through=()):
    ns, ni, no, nt = len(scalars), len(ins), len(outs), len(through)

    def kernel(*refs):
        rest = refs[ns + ni + len(after) + nt :]
        body(refs[:ns], refs[ns : ns + ni], rest[:no], rest[no + nt :])

    moved = sum(math.prod(a.shape) * a.dtype.itemsize for a, _ in ins)
    first = ns + ni + len(after)
    ins = list(ins) + [(array, ANY) for array in list(after) + list(through)]
    moved += sum(math.prod(shape) * jnp.dtype(dtype).itemsize for shape, dtype, _ in outs)
    outs = list(outs) + [(array.shape, array.dtype, ANY) for array in through]
    return pl.pallas_call(
        kernel,
        grid_spec=pltpu.PrefetchScalarGridSpec(
            num_scalar_prefetch=ns,
            grid=(steps,),
            in_specs=[spec for _, spec in ins],
            out_specs=[spec for _, _, spec in outs],
            scratch_shapes=scratch,
        ),
        out_shape=[jax.ShapeDtypeStruct(shape, dtype) for shape, dtype, _ in outs],
        input_output_aliases={first + at: no + at for at in range(nt)},
        compiler_params=pltpu.CompilerParams(
            dimension_semantics=("arbitrary",), vmem_limit_bytes=VMEM_LIMIT
        ),
        cost_estimate=pl.CostEstimate(flops=flops, bytes_accessed=moved, transcendentals=0),
    )(*scalars, *[array for array, _ in ins])


class Loads:
    def __init__(self, steps, sems, pairs):
        self.steps = steps
        self.copies = [
            pltpu.make_async_copy(source, target, sems.at[at])
            for at, (source, target) in enumerate(pairs)
        ]

    def first(self, action):
        if self.steps == 1:
            action()
        else:
            pl.when(pl.program_id(0) == 0)(action)

    def start(self):
        self.first(lambda: [copy.start() for copy in self.copies] and None)

    def wait(self, *which):
        self.first(lambda: [self.copies[at].wait() for at in which] and None)


def side_by_side(own, mate, target, width):
    return [(own, target.at[:, pl.ds(0, width)]), (mate, target.at[:, pl.ds(width, width)])]


def one_above(own, mate, target, height):
    return [(own, target.at[pl.ds(0, height)]), (mate, target.at[pl.ds(height, height)])]


def moments(z):
    center = z - jnp.mean(z, axis=-1, keepdims=True)
    rstd = lax.rsqrt(jnp.mean(center * center, axis=-1, keepdims=True) + EPS)
    return center * rstd, rstd


def norm_grad(unit, rstd, gain, grad):
    inner = grad * gain
    return rstd * (
        inner
        - jnp.mean(inner, axis=-1, keepdims=True)
        - unit * jnp.mean(inner * unit, axis=-1, keepdims=True)
    )


def fold(block):
    return jnp.sum(block.reshape(block.shape[0] // 8, 8, block.shape[1]), axis=0)


def gelu(u):
    bell = jnp.exp2(u * u * (-0.5 / math.log(2.0)))
    t = 1.0 / (1.0 + (0.3275911 * 0.5**0.5) * jnp.abs(u))
    poly = t * (
        0.5 * 0.254829592
        + t
        * (
            0.5 * -0.284496736
            + t * (0.5 * 1.421413741 + t * (0.5 * -1.453152027 + t * (0.5 * 1.061405429)))
        )
    )
    tail = poly * bell
    phi = jnp.where(u >= 0.0, 1.0 - tail, tail)
    return u * phi, phi + u * (bell * (1.0 / math.sqrt(2.0 * math.pi)))


def spread_heads(block, lane_head):
    parts = [jnp.where(lane_head == h, block, 0.0) for h in range(GROUP // HEAD_DIM)]
    return jnp.concatenate(parts, axis=0).astype(BF16)


def gather_heads(block, lane_head, tokens):
    total = jnp.where(lane_head == 0, block[0:tokens], 0.0)
    for h in range(1, GROUP // HEAD_DIM):
        total = jnp.where(lane_head == h, block[h * tokens : (h + 1) * tokens], total)
    return total


def lane_heads():
    return lax.broadcasted_iota(jnp.int32, (1, GROUP), 1) // HEAD_DIM


def attend(items):
    scores = [dot_nt(qm, kb) for qm, kb, vb, keep in items]
    weights = []
    for score, (qm, kb, vb, keep) in zip(scores, items):
        score = jnp.where(keep, score, NEG)
        top = jnp.max(score, axis=1, keepdims=True)
        weight = jnp.exp(score - top)
        weight = weight * (1.0 / jnp.sum(weight, axis=1, keepdims=True))
        weights.append(weight.astype(BF16))
    return [dot(weight, vb) for weight, (qm, kb, vb, keep) in zip(weights, items)]


def attend_grad(items):
    scores = [dot_nt(kb, qm) for qm, kb, vb, dom, keep in items]
    grads = [dot_nt(vb, dom) for qm, kb, vb, dom, keep in items]
    middle = []
    for score, grad, (qm, kb, vb, dom, keep) in zip(scores, grads, items):
        score = jnp.where(keep, score, NEG)
        top = jnp.max(score, axis=0, keepdims=True)
        weight = jnp.exp(score - top)
        weight = weight * (1.0 / jnp.sum(weight, axis=0, keepdims=True))
        inner = jnp.sum(weight * grad, axis=0, keepdims=True)
        grad_score = weight * (grad - inner)
        middle.append(
            (weight.astype(BF16), grad_score.astype(BF16), jnp.transpose(grad_score).astype(BF16))
        )
    results = []
    for (weight, grad_score, turned), (qm, kb, vb, dom, keep) in zip(middle, items):
        results.append((dot(turned, kb), dot(grad_score, qm), dot(weight, dom)))
    return results


def box_keep(corners, slot, shape, axis):
    index = lax.broadcasted_iota(jnp.int32, shape, axis) - 1
    grid_row = (index * 2731) >> 15
    grid_col = index - grid_row * GRID
    inside = (grid_col >= corners[slot * 4]) & (grid_col < corners[slot * 4 + 1])
    inside = inside & (grid_row >= corners[slot * 4 + 2]) & (grid_row < corners[slot * 4 + 3])
    return (inside & (index >= 0)) | (index < 0)


def band_loop(total, body, part=None):
    @pl.loop(0, total // (BAND * BANDS))
    def _(step):
        sums = []
        for band in range(BANDS):
            start = pl.multiple_of(step * (BAND * BANDS) + band * BAND, BAND)
            folded = body(pl.ds(start, BAND))
            if folded is not None:
                sums.append(folded)
        for terms in zip(*sums):
            at = terms[0][0]
            part[at] += sum(value for _, value in terms[1:]) + terms[0][1]


def by_columns(left, weight, finish, transposed=False):
    count = weight.shape[0] if transposed else weight.shape[1]
    for start in range(0, count, GROUP):
        cols = slice(start, start + GROUP)
        value = dot_nt(left, weight[cols, :]) if transposed else dot(left, weight[:, cols])
        finish(cols, value)


def both_halves(own, mate, at):
    return jnp.concatenate([own[at[0], at[1] : at[1] + 1], mate[at[0], at[1] : at[1] + 1]], axis=1)


def row_pairs(source, where, first, count, length, finish):
    for at in range(0, count, 2):
        both = [source[where[first + at + n]].astype(F32) for n in range(2)]
        finish(slice(at * length, (at + 2) * length), jnp.concatenate(both, axis=0))


def split_lanes(target, rows, start, value):
    for lane in range(0, value.shape[1], LANES):
        target[(start + lane) // LANES, rows, :] = value[:, lane : lane + LANES]


def join_lanes(source, rows):
    return jnp.concatenate([source[lane, rows, :] for lane in range(source.shape[0])], axis=1)


def fetch_kernel(count, scalars, ins, outs, scratch):
    (source,) = scalars
    (sems,) = scratch
    copies = [
        pltpu.make_async_copy(table.at[source[at]], out.at[at], sems.at[which * count + at])
        for which, (table, out) in enumerate(zip(ins, outs))
        for at in range(count)
    ]
    for copy in copies:
        copy.start()
    for copy in copies:
        copy.wait()


def project_kernel(images, own_images, patch_pad, patch_count, local, scalars, ins, outs, scratch):
    (core,) = scalars
    patches, proj_weight, proj_bias, ain, ain_mate, bias_own, bias_mate = ins
    proj, keys, values = outs
    taken, raw, w1, w2, sems, weight_sems = scratch
    loads = Loads(
        1,
        weight_sems,
        side_by_side(ain.at[1, 1], ain_mate.at[1, 1], w1, local)
        + side_by_side(ain.at[1, 2], ain_mate.at[1, 2], w2, local),
    )
    parts, span = taken.shape[0], taken.shape[1]
    arrivals = Loads(
        1, sems, [(patches.at[pl.ds(n * span, span)], taken.at[n]) for n in range(parts)]
    )
    arrivals.start()
    loads.start()
    rows = span * images
    width = raw.shape[0] * LANES
    for n in range(parts):
        arrivals.wait(n)
        flat = taken[n].reshape(rows, taken.shape[3])
        for start in range(0, width, GROUP):
            cols = slice(start, start + GROUP)
            split_lanes(
                raw,
                slice(n * rows, (n + 1) * rows),
                start,
                dot(flat, proj_weight[:, cols]) + proj_bias[:, cols],
            )
    loads.wait(0, 1, 2, 3)
    bias = both_halves(bias_own, bias_mate, (1, 1))
    first = core[0] * own_images
    rest = jnp.zeros((patch_pad - patch_count, width), F32)

    group = 4

    @pl.loop(0, images // group)
    def _(step):
        both = []
        for at in range(group):
            which = lax.rem(step * group + at + first, images)
            own = jnp.concatenate(
                [
                    raw[lane, pl.ds(which, patch_count, stride=images), :]
                    for lane in range(raw.shape[0])
                ],
                axis=1,
            )
            both.append(jnp.concatenate([own, rest], axis=0))
        low = jnp.concatenate(both, axis=0).astype(BF16)
        some = pl.ds(step * group, group)

        @pl.when(step < own_images // group)
        def _():
            proj[some] = low.reshape(group, patch_pad, width)

        shape = (group, patch_pad, GROUP)
        for start in range(0, width, GROUP):
            cols = slice(start, start + GROUP)
            keys[some, :, cols] = dot(low, w1[:, cols]).astype(BF16).reshape(shape)
            values[some, :, cols] = (
                (dot(low, w2[:, cols]) + bias[:, cols]).astype(BF16).reshape(shape)
            )


def self_kernel(steps, rows, local, length, scalars, ins, outs, scratch):
    lens, where = scalars
    x_in, ain, ain_mate, aout, aout_mate, bias_own, bias_mate, out_bias, gain, shift = ins
    x_out, unit_one, q_out, k_out, v_out, att_own, att_mate, low_out, cross_q, rstd_one = outs
    wq, wk, wv, wo, wc, qs, ks, vs, acc, low, sems = scratch
    total = rows * length
    loads = Loads(
        steps,
        sems,
        side_by_side(ain.at[0, 0], ain_mate.at[0, 0], wq, local)
        + side_by_side(ain.at[0, 1], ain_mate.at[0, 1], wk, local)
        + side_by_side(ain.at[0, 2], ain_mate.at[0, 2], wv, local)
        + one_above(aout.at[0], aout_mate.at[0], wo, local)
        + side_by_side(ain.at[1, 0], ain_mate.at[1, 0], wc, local),
    )
    loads.start()
    bias_q = both_halves(bias_own, bias_mate, (0, 0))
    bias_v = both_halves(bias_own, bias_mate, (0, 1))
    bias_c = both_halves(bias_own, bias_mate, (1, 0))

    def put(at, both):
        x_out[at] = both.astype(BF16)

    base = pl.program_id(0) * rows
    row_pairs(x_in, where, base, rows, length, put)
    xb = x_out[...]

    def keep_q(cols, value):
        value = (value + bias_q[:, cols]).astype(BF16)
        q_out[:, cols] = value
        qs[:, cols] = value.astype(F32) * SCALE

    def keep_k(cols, value):
        value = value.astype(BF16)
        k_out[:, cols] = value
        ks[:, cols] = value.astype(F32)

    def keep_v(cols, value):
        value = (value + bias_v[:, cols]).astype(BF16)
        v_out[:, cols] = value
        vs[:, cols] = value.astype(F32)

    loads.wait(0, 1)
    by_columns(xb, wq, keep_q)
    loads.wait(2, 3)
    by_columns(xb, wk, keep_k)
    loads.wait(4, 5)
    by_columns(xb, wv, keep_v)
    lane_head = lane_heads()
    key_index = lax.broadcasted_iota(jnp.int32, (1, length), 1)

    @pl.loop(0, rows // PAIRED)
    def _(step):
        items, places = [], []
        for row in range(PAIRED):
            row = step * PAIRED + row
            at = pl.ds(pl.multiple_of(row * length, 8), length)
            keep = key_index < lens[base + row]
            for g in range(qs.shape[1] // GROUP):
                lanes = slice(g * GROUP, (g + 1) * GROUP)
                items.append(
                    (
                        spread_heads(qs[at, lanes], lane_head),
                        ks[at, lanes].astype(BF16),
                        vs[at, lanes].astype(BF16),
                        keep,
                    )
                )
                places.append((at, lanes))
        for (at, lanes), result in zip(places, attend(items)):
            acc[at, lanes] = gather_heads(result, lane_head, length)

    def cast(at):
        value = acc[at].astype(BF16)
        low[at] = value
        att_own[at] = value[:, :local]
        att_mate[at] = value[:, local:]

    def to_acc(cols, value):
        acc[:, cols] = value

    band_loop(total, cast)
    loads.wait(6, 7)
    by_columns(low[...], wo, to_acc)

    def norm(at):
        z = x_out[at].astype(F32) + acc[at] + out_bias[0:1]
        unit, rstd = moments(z)
        unit_one[at] = unit
        rstd_one[at] = rstd
        h = (unit * gain[0:1] + shift[0:1]).astype(BF16)
        low[at] = h
        low_out[at] = h

    band_loop(total, norm)
    loads.wait(8, 9)

    def to_query(cols, value):
        cross_q[:, cols] = (value + bias_c[:, cols]).astype(BF16)

    by_columns(low[...], wc, to_query)


def cross_kernel(rows, length, scalars, ins, outs, scratch):
    image, corners = scalars
    queries, keys, values = ins
    (att,) = outs
    qs, acc = scratch
    patch_pad = keys.shape[1]
    lane_head = lane_heads()
    base = pl.program_id(0) * rows

    def spread(at):
        qs[at] = queries[at].astype(F32) * SCALE

    band_loop(rows * length, spread)

    @pl.loop(0, rows // PAIRED)
    def _(step):
        items, places = [], []
        for row in range(PAIRED):
            row = step * PAIRED + row
            at = pl.ds(pl.multiple_of(row * length, 8), length)
            which = image[base + row]
            keep = box_keep(corners, base + row, (1, patch_pad), 1)
            for g in range(qs.shape[1] // GROUP):
                lanes = slice(g * GROUP, (g + 1) * GROUP)
                items.append(
                    (
                        spread_heads(qs[at, lanes], lane_head),
                        keys[which, :, lanes],
                        values[which, :, lanes],
                        keep,
                    )
                )
                places.append((at, lanes))
        for (at, lanes), result in zip(places, attend(items)):
            acc[at, lanes] = gather_heads(result, lane_head, length)

    def cast(at):
        att[at] = acc[at].astype(BF16)

    band_loop(rows * length, cast)


def feed_kernel(steps, rows, local, hidden, length, scalars, ins, outs, scratch):
    (where,) = scalars
    grad_in, att, unit_one, aout, aout_mate, up, up_mate, down, down_mate = ins[:9]
    out_bias, gains, shift, up_bias, up_bias_mate = ins[9:]
    merged, low_out, df_out, do_out, dz_out, a_own, a_mate = outs[:7]
    g_out, du_out = outs[7:9], outs[9:11]
    da_out, sums, up_sums = outs[11:]
    wo, wu, wd, acc, kept, unit_two, rstd_two, low, upstream, even, odd, slope = scratch[:12]
    part, up_part, sems = scratch[12:]
    tiles = hidden // TILE
    total = rows * length
    loads = Loads(
        steps,
        sems,
        one_above(aout.at[1], aout_mate.at[1], wo, local)
        + [
            (source.at[:, pl.ds(t * TILE, TILE)], wu.at[t, :, pl.ds(half * TILE, TILE)])
            for t in range(tiles)
            for half, source in enumerate((up, up_mate))
        ]
        + [
            (source.at[pl.ds(t * TILE, TILE)], wd.at[t, pl.ds(half * TILE, TILE)])
            for t in range(tiles)
            for half, source in enumerate((down, down_mate))
        ],
    )
    loads.start()
    part[...] = jnp.zeros_like(part)

    def put(at, both):
        upstream[at] = both.astype(BF16)

    base = pl.program_id(0) * rows
    row_pairs(grad_in, where, base, rows, length, put)

    def to_acc(cols, value):
        acc[:, cols] = value

    a_own[...] = att[:, :local]
    a_mate[...] = att[:, local:]
    loads.wait(0, 1)
    by_columns(att[...], wo, to_acc)

    def norm_two(at):
        h_one = unit_one[at] * gains[0:1] + shift[0:1]
        unit, rstd = moments(h_one + acc[at] + out_bias[1:2])
        h_two = unit * gains[1:2] + shift[1:2]
        unit_two[at] = unit
        rstd_two[at] = rstd
        kept[at] = h_two
        h_low = h_two.astype(BF16)
        low[at] = h_low
        low_out[at] = h_low

    band_loop(total, norm_two)
    acc[...] = jnp.zeros_like(acc)
    loads.wait(*range(2, 2 + 4 * tiles))
    biases = (up_bias, up_bias_mate)

    def activate(units, t):
        cols = slice(t * TILE, (t + 1) * TILE)
        for half in range(2):
            lanes = slice(half * TILE, (half + 1) * TILE)
            bias = biases[half][:, cols]
            for start in range(0, total, BAND):
                at = slice(start, start + BAND)
                active, sloped = gelu(units[at, lanes] + bias)
                g_out[half][at, cols] = active.astype(BF16)
                slope[t, at, lanes] = sloped

    def add_down(t):
        cols = slice(t * TILE, (t + 1) * TILE)
        both = jnp.concatenate([g_out[0][:, cols], g_out[1][:, cols]], axis=1)
        acc[...] += dot(both, wd[t])

    units = (even, odd)
    even[...] = dot(low[...], wu[0])
    for t in range(tiles):
        if t + 1 < tiles:
            units[(t + 1) % 2][...] = dot(low[...], wu[t + 1])
        activate(units[t % 2], t)
        add_down(t)

    def norm_three(at):
        unit, rstd = moments(kept[at] + acc[at] + out_bias[2:3])
        gain = gains[2:3]
        unit_three = unit * gain + shift[2:3]
        grad = upstream[at].astype(F32)
        dz = norm_grad(unit, rstd, gain, grad)
        kept[at] = dz
        acc[at] = unit_three
        dz_low = dz.astype(BF16)
        low[at] = dz_low
        df_out[at] = dz_low
        return (
            (0, fold(dz_low.astype(F32))),
            (1, fold(grad * unit)),
            (2, fold(grad)),
        )

    band_loop(total, norm_three, part)

    for row in range(rows):
        merged[where[base + row]] = acc[row * length : (row + 1) * length].astype(BF16)
    acc[...] = jnp.zeros_like(acc)

    for t in range(tiles):
        cols = slice(t * TILE, (t + 1) * TILE)
        grads = dot_nt(low[...], wd[t])
        for half in range(2):
            lanes = slice(half * TILE, (half + 1) * TILE)
            folded = 0.0
            for start in range(0, total, BAND):
                at = slice(start, start + BAND)
                du = (grads[at, lanes] * slope[t, at, lanes]).astype(BF16)
                du_out[half][at, cols] = du
                folded = folded + fold(du.astype(F32))
            up_part[half, :, cols] = folded
        both = jnp.concatenate([du_out[0][:, cols], du_out[1][:, cols]], axis=1)
        acc[...] += dot_nt(both, wu[t])

    def norm_two_back(at):
        grad = kept[at] + acc[at]
        unit = unit_two[at]
        dz = norm_grad(unit, rstd_two[at], gains[1:2], grad)
        dz_out[at] = dz
        dz_low = dz.astype(BF16)
        low[at] = dz_low
        do_out[at] = dz_low
        return (
            (3, fold(dz_low.astype(F32))),
            (4, fold(grad * unit)),
            (5, fold(grad)),
        )

    band_loop(total, norm_two_back, part)

    def to_grad(cols, value):
        da_out[:, cols] = value.astype(BF16)

    by_columns(low[...], wo, to_grad, transposed=True)
    for at in range(8):
        sums[0, at : at + 1] = jnp.sum(part[at], axis=0, keepdims=True)
    for half in range(2):
        up_sums[0, half : half + 1] = jnp.sum(up_part[half], axis=0, keepdims=True)


def cross_grad_kernel(steps, rows, length, scalars, ins, outs, scratch):
    image, corners = scalars
    queries, grads, keys, values = ins
    own, mate, grad_queries = outs
    qs, gs, acc, dk, dv = scratch
    patch_pad = keys.shape[1]

    def clear():
        @pl.loop(0, dk.shape[0])
        def _(at):
            dk[at] = jnp.zeros(dk.shape[1:], F32)
            dv[at] = jnp.zeros(dv.shape[1:], F32)

    pl.when(pl.program_id(0) == 0)(clear)

    def spread(at):
        qs[at] = queries[at].astype(F32) * SCALE
        gs[at] = grads[at].astype(F32)

    band_loop(rows * length, spread)
    lane_head = lane_heads()
    base = pl.program_id(0) * rows

    @pl.loop(0, rows // PAIRED)
    def _(step):
        items, places = [], []
        for row in range(PAIRED):
            row = step * PAIRED + row
            at = pl.ds(pl.multiple_of(row * length, 8), length)
            which = image[base + row]
            keep = box_keep(corners, base + row, (patch_pad, 1), 0)
            for g in range(qs.shape[1] // GROUP):
                lanes = slice(g * GROUP, (g + 1) * GROUP)
                items.append(
                    (
                        spread_heads(qs[at, lanes], lane_head),
                        keys[which, :, lanes],
                        values[which, :, lanes],
                        spread_heads(gs[at, lanes], lane_head),
                        keep,
                    )
                )
                places.append((at, which, lanes))
        for (at, which, lanes), (grad_q, grad_k, grad_v) in zip(places, attend_grad(items)):
            acc[at, lanes] = gather_heads(grad_q, lane_head, length) * SCALE
            dk[which, :, lanes] += grad_k
            dv[which, :, lanes] += grad_v

    def cast(at):
        grad_queries[at] = acc[at].astype(BF16)

    band_loop(rows * length, cast)

    @pl.when(pl.program_id(0) == steps - 1)
    def _():
        half = own.shape[1]

        @pl.loop(0, half)
        def _(at):
            own[0, at] = dk[at].astype(BF16)
            own[1, at] = dv[at].astype(BF16)
            mate[0, at] = dk[half + at].astype(BF16)
            mate[1, at] = dv[half + at].astype(BF16)


def image_kernel(images, patch_count, local, scalars, ins, outs, scratch):
    (core,) = scalars
    piece, piece_mate, patches, proj_weight, ain, ain_mate = ins
    kv_own, kv_mate, patch_grad, weight_grad, sums = outs
    narrow, wide, taken, w1, w2, part, sems, weight_sems = scratch
    parts, span = taken.shape[0], taken.shape[1]
    loads = Loads(
        1,
        weight_sems,
        side_by_side(ain.at[1, 1], ain_mate.at[1, 1], w1, local)
        + side_by_side(ain.at[1, 2], ain_mate.at[1, 2], w2, local),
    )
    arrivals = Loads(
        1, sems, [(patches.at[pl.ds(n * span, span)], taken.at[n]) for n in range(parts)]
    )
    loads.start()
    arrivals.start()
    part[...] = jnp.zeros_like(part)
    own_images, patch_pad = piece.shape[1], piece.shape[2]
    width = w1.shape[0]

    slab = 80

    @pl.loop(0, wide.shape[1] // slab)
    def _(step):
        at = pl.ds(pl.multiple_of(step * slab, slab), slab)
        for lane in range(wide.shape[0]):
            wide[lane, at] = jnp.zeros((slab, LANES), F32)

    loads.wait(0, 1, 2, 3)
    first = core[0] * own_images

    @pl.loop(0, own_images // 2)
    def _(step):
        pair = pl.ds(step * 2, 2)
        halves = []
        for half in (slice(0, local), slice(local, width)):
            swapped = slice(width - half.stop, width - half.start)
            both = piece[:, pair, :, half].astype(F32) + piece_mate[:, pair, :, swapped].astype(F32)
            both = both.astype(BF16)
            halves.append([both[at].reshape(2 * patch_pad, local) for at in range(2)])
        (dk_own, dv_own), (dk_mate, dv_mate) = halves
        rows = pl.ds(pl.multiple_of(step * 2 * patch_pad, 2 * patch_pad), 2 * patch_pad)
        kv_own[rows, :local] = dk_own
        kv_own[rows, local:] = dv_own
        kv_mate[rows, :local] = dk_mate
        kv_mate[rows, local:] = dv_mate
        dk = jnp.concatenate([dk_own, dk_mate], axis=1)
        dv = jnp.concatenate([dv_own, dv_mate], axis=1)
        part[1] += fold(dv.astype(F32))
        for start in range(0, width, GROUP):
            cols = slice(start, start + GROUP)
            grad = dot_nt(dk, w1[cols, :]) + dot_nt(dv, w2[cols, :])
            grad = grad.astype(BF16).astype(F32)
            part[0, :, cols] += fold(grad)
            for at in range(2):
                one = grad[at * patch_pad : at * patch_pad + patch_count]
                which = step * 2 + at
                spot = pl.ds(which, patch_count, stride=own_images)
                split_lanes(narrow, spot, start, one)
                split_lanes(wide, pl.ds(which + first, patch_count, stride=images), start, one)

    for n in range(parts):
        arrivals.wait(n)
        few = slice(n * span * own_images, (n + 1) * span * own_images)
        some = join_lanes(narrow, few).astype(BF16)
        for start in range(0, proj_weight.shape[0], GROUP):
            cols = slice(start, start + GROUP)
            back = dot_nt(some, proj_weight[cols, :]).astype(BF16)
            patch_grad[n * span : (n + 1) * span, :, cols] = back.reshape(span, own_images, GROUP)
        flat = taken[n].reshape(span * images, taken.shape[3])
        grad = join_lanes(wide, slice(n * span * images, (n + 1) * span * images)).astype(BF16)
        product = dot_tn(flat, grad)
        if n == 0:
            weight_grad[...] = product
        else:
            weight_grad[...] += product
    for at in range(2):
        sums[at : at + 1] = jnp.sum(part[at], axis=0, keepdims=True)


def self_grad_kernel(steps, rows, local, length, scalars, ins, outs, scratch):
    lens, where = scalars
    dq2, unit_one, rstd_one, dz_two, q_in, k_in, v_in, ain, ain_mate, aout, aout_mate, gain = ins
    text_grad, do_out, dq2_own, dq2_mate, qkv_own, qkv_mate, sums = outs
    wc, wo, wq, wk, wv, acc, kept, low, low_k, low_v, qs, ks, vs, part, sems = scratch
    total = rows * length
    loads = Loads(
        steps,
        sems,
        side_by_side(ain.at[1, 0], ain_mate.at[1, 0], wc, local)
        + one_above(aout.at[0], aout_mate.at[0], wo, local)
        + side_by_side(ain.at[0, 0], ain_mate.at[0, 0], wq, local)
        + side_by_side(ain.at[0, 1], ain_mate.at[0, 1], wk, local)
        + side_by_side(ain.at[0, 2], ain_mate.at[0, 2], wv, local),
    )
    loads.start()
    part[...] = jnp.zeros_like(part)

    def to_acc(cols, value):
        acc[:, cols] = value

    loads.wait(0, 1)
    by_columns(dq2[...], wc, to_acc, transposed=True)

    def norm_back(at):
        unit = unit_one[at]
        grad = dz_two[at] + acc[at]
        dz = norm_grad(unit, rstd_one[at], gain[0:1], grad)
        kept[at] = dz
        dz_low = dz.astype(BF16)
        low[at] = dz_low
        do_out[at] = dz_low
        qs[at] = q_in[at].astype(F32) * SCALE
        ks[at] = k_in[at].astype(F32)
        vs[at] = v_in[at].astype(F32)
        query = dq2[at]
        dq2_own[at] = query[:, :local]
        dq2_mate[at] = query[:, local:]
        return (
            (0, fold(dz_low.astype(F32))),
            (1, fold(grad * unit)),
            (2, fold(grad)),
            (5, fold(query.astype(F32))),
        )

    band_loop(total, norm_back, part)
    loads.wait(2, 3)
    by_columns(low[...], wo, to_acc, transposed=True)
    lane_head = lane_heads()
    key_index = lax.broadcasted_iota(jnp.int32, (length, 1), 0)
    base = pl.program_id(0) * rows

    @pl.loop(0, rows // PAIRED)
    def _(step):
        items, places = [], []
        for row in range(PAIRED):
            row = step * PAIRED + row
            at = pl.ds(pl.multiple_of(row * length, 8), length)
            keep = key_index < lens[base + row]
            for g in range(qs.shape[1] // GROUP):
                lanes = slice(g * GROUP, (g + 1) * GROUP)
                items.append(
                    (
                        spread_heads(qs[at, lanes], lane_head),
                        ks[at, lanes].astype(BF16),
                        vs[at, lanes].astype(BF16),
                        spread_heads(acc[at, lanes], lane_head),
                        keep,
                    )
                )
                places.append((at, lanes))
        for (at, lanes), (grad_q, grad_k, grad_v) in zip(places, attend_grad(items)):
            qs[at, lanes] = gather_heads(grad_q, lane_head, length) * SCALE
            ks[at, lanes] = grad_k
            vs[at, lanes] = grad_v

    def cast(at):
        sums = []
        for slot, (source, target) in enumerate(((qs, low), (ks, low_k), (vs, low_v))):
            value = source[at].astype(BF16)
            target[at] = value
            qkv_own[at, slot * local : (slot + 1) * local] = value[:, :local]
            qkv_mate[at, slot * local : (slot + 1) * local] = value[:, local:]
            if slot != 1:
                sums.append((3 + slot // 2, fold(value.astype(F32))))
        return sums

    band_loop(total, cast, part)
    loads.wait(4, 5, 6, 7, 8, 9)
    for start in range(0, kept.shape[1], GROUP):
        cols = slice(start, start + GROUP)
        acc[:, cols] = (
            kept[:, cols]
            + dot_nt(low[...], wq[cols, :])
            + dot_nt(low_k[...], wk[cols, :])
            + dot_nt(low_v[...], wv[cols, :])
        )

    for row in range(rows):
        text_grad[where[base + row]] = acc[row * length : (row + 1) * length].astype(BF16)
    for at in range(8):
        sums[0, at : at + 1] = jnp.sum(part[at], axis=0, keepdims=True)


def pack_kernel(local, hidden, scalars, ins, outs, scratch):
    (core,) = scalars
    feed, up, self_, image = ins
    feed_sum = jnp.sum(feed[...], axis=0)
    self_sum = jnp.sum(self_[...], axis=0)
    up_sum = jnp.sum(up[...], axis=0)
    common = [(0, 0), (1, 3), (1, 0), (0, 1), (1, 4), (1, 1), (0, 2), (1, 5), (1, 2)]
    even = core[0] == 0
    for out, mine in zip(outs, (True, False)):
        out[...] = jnp.zeros_like(out)
        at = 0
        for which, row in common:
            source = feed_sum if which else self_sum
            for half in range(2):
                out[at : at + 1] = source[row : row + 1, half * local : (half + 1) * local]
                at += 1
        lanes = slice(0, local) if mine else slice(local, 2 * local)
        for row in (3, 4, 5):
            out[at : at + 1] = self_sum[row : row + 1, lanes]
            at += 1
        out[at : at + 1] = image[1:2, lanes]
        at += 1
        half = 0 if mine else 1
        for start in range(0, hidden, local):
            out[at : at + 1] = up_sum[half : half + 1, start : start + local]
            at += 1
        low, high = image[0:1, :local], image[0:1, local:]
        out[at : at + 1] = jnp.where(even == mine, low, high)


def halve_kernel(rows, length, scalars, ins, outs, scratch):
    core, where = scalars
    (tall,) = scratch

    def put(at, both):
        split_lanes(tall, at, 0, both)

    row_pairs(ins[0], where, 0, rows, length, put)
    half = length // 2
    for out, first in zip(outs, (core[0] * half, (1 - core[0]) * half)):
        for token in range(half):
            out[token] = join_lanes(
                tall, pl.ds(first + token, rows, stride=length)
            ).astype(BF16)


def place_kernel(scalars, ins, outs, scratch):
    own, mate, place = ins
    (out,) = outs
    count, slots = out.shape[1], own.shape[1]
    index = lax.broadcasted_iota(jnp.int32, (count, slots), 1)
    from_own = jnp.where(place[...] == index, 1.0, 0.0).astype(BF16)
    from_mate = jnp.where(place[...] == index + slots, 1.0, 0.0).astype(BF16)
    for token in range(out.shape[0]):
        out[token] = (dot(from_own, own[token]) + dot(from_mate, mate[token])).astype(BF16)


def body(
    text,
    cotangent,
    lengths,
    box_corners,
    box_counts,
    region_box,
    patches,
    proj_weight,
    proj_bias,
    attention_in,
    attention_bias,
    attention_out,
    output_bias,
    norm_gain,
    norm_bias,
    up_weight,
    up_bias,
    down_weight,
):
    rows, length, width = text.shape
    images, patch_count, vision = patches.shape
    local = attention_in.shape[-1]
    hidden = up_weight.shape[-1]
    devices = lax.axis_size("dp")
    me, core = lax.axis_index("dp"), lax.axis_index("mp")
    pair = -(-rows // devices)
    each, odd = pair // 2, pair % 2
    deep = each + odd
    slots = devices * each + devices // 2 * odd
    patch_pad = -(-patch_count // 16) * 16
    own_images = images // 2
    step_rows = 12 if slots % 12 == 0 else 8
    steps = slots // step_rows
    tokens = step_rows * length
    all_tokens = slots * length
    full = slots * 2 == rows
    core_scalar = core.astype(jnp.int32).reshape(1)

    def mate(value):
        return lax.ppermute(value, "mp", [(0, 1), (1, 0)])

    def tie(*values):
        return lax.optimization_barrier(values)

    def exchange(value):
        return lax.all_to_all(value, "dp", split_axis=0, concat_axis=0, tiled=True)

    ain_mate = mate(attention_in)
    bias_mate = mate(attention_bias)
    aout_mate = mate(attention_out)
    up_bias_own = up_bias.reshape(1, hidden)
    up_bias_mate = mate(up_bias_own)
    up_mate = mate(up_weight)
    down_mate = mate(down_weight)

    number = jnp.arange(rows, dtype=jnp.int32)
    target = region_box // rows
    earlier = (target[:, None] == target[None, :]) & (number[None, :] < number[:, None])
    nth = jnp.sum(earlier.astype(jnp.int32), axis=1)
    even_part = nth < 2 * each
    row_core = jnp.where(even_part, nth // max(each, 1), (target ^ me) & 1)
    depth = jnp.where(even_part, nth % max(each, 1), each)
    spot = jnp.arange(devices * deep, dtype=jnp.int32)
    hit = (spot[:, None] == (target * deep + depth)[None, :]) & (row_core == core)[None, :]
    source = jnp.sum(jnp.where(hit, number[None, :], 0), axis=1)
    slot = jnp.where(even_part, target * each + depth, devices * each + (target >> 1))
    place = jnp.where(row_core == core, slot, slot + slots)[:, None]
    order = jnp.arange(slots, dtype=jnp.int32)
    late = order - devices * each
    where = jnp.where(
        late < 0,
        order // max(each, 1) * deep + order % max(each, 1),
        (2 * late + ((me & 1) ^ core)) * deep + each,
    )
    meta = jnp.concatenate(
        [(region_box % rows)[:, None], lengths[:, None], box_corners], axis=1
    )
    meta_out = jnp.sum(jnp.where(hit[:, :, None], meta[None], 0), axis=1)
    if not full:
        empty = jnp.array([0, 1, 0, 1, 0, 1], jnp.int32)
        meta_out = jnp.where(jnp.any(hit, axis=1)[:, None], meta_out, empty[None])
    arrived = exchange(meta_out)[where]
    ends = jnp.cumsum(box_counts[0])
    image = jnp.sum((ends[None, :] <= arrived[:, 0:1]).astype(jnp.int32), axis=1)
    image = (image + own_images * core) % images
    lens = arrived[:, 1]
    corners = arrived[:, 2:].reshape(-1)

    block_shape = (devices * deep, length, width)
    if full:
        x_out, upstream_out = run(
            partial(fetch_kernel, devices * deep),
            1,
            [source],
            [(text, ANY), (cotangent, ANY)],
            [(block_shape, BF16, whole_spec(block_shape))] * 2,
            [pltpu.SemaphoreType.DMA((2 * devices * deep,))],
            0,
        )
    else:
        valid = jnp.any(hit, axis=1)[:, None, None]
        x_out = jnp.where(valid, text[source], 0)
        upstream_out = jnp.where(valid, cotangent[source], 0)
    x_in = exchange(x_out)

    patches, aout_mate, image, corners, lens = tie(patches, aout_mate, image, corners, lens)
    by_patch = jnp.transpose(patches, (1, 0, 2))
    parts = next(n for n in (5, 4, 3, 2, 1) if patch_count % n == 0)
    weight_scratch = pltpu.VMEM((width, width), BF16)

    def slabs(count):
        return pltpu.VMEM((width // LANES, count, LANES), F32)

    patch_scratch = pltpu.VMEM((parts, patch_count // parts, images, vision), BF16)
    image_shape = (images, patch_pad, width)
    proj, keys, values = run(
        partial(project_kernel, images, own_images, patch_pad, patch_count, local),
        1,
        [core_scalar],
        [
            (by_patch, ANY),
            (proj_weight, whole_spec(proj_weight.shape)),
            (proj_bias.reshape(1, width), whole_spec((1, width))),
            (attention_in, ANY),
            (ain_mate, ANY),
            (attention_bias, whole_spec(attention_bias.shape)),
            (bias_mate, whole_spec(bias_mate.shape)),
        ],
        [((own_images,) + image_shape[1:], BF16, whole_spec((own_images,) + image_shape[1:]))]
        + [(image_shape, BF16, whole_spec(image_shape))] * 2,
        [
            patch_scratch,
            slabs(patch_count * images),
            weight_scratch,
            weight_scratch,
            pltpu.SemaphoreType.DMA((parts,)),
            pltpu.SemaphoreType.DMA((4,)),
        ],
        2 * images * patch_pad * width * (vision + 2 * width),
    )

    upstream_out, proj, keys, values = tie(upstream_out, proj, keys, values)
    upstream_in = exchange(upstream_out)

    def token_in(value):
        return (value, rows_spec((tokens, value.shape[1]), 0))

    def token_out(cols, dtype):
        return ((all_tokens, cols), dtype, rows_spec((tokens, cols), 0))

    block_out = (block_shape, BF16, whole_spec(block_shape))

    def f32_tokens(cols):
        return pltpu.VMEM((tokens, cols), F32)

    def low_tokens(cols):
        return pltpu.VMEM((tokens, cols), BF16)

    def whole(value):
        return (value, whole_spec(value.shape))

    attention_flops = 4 * 4 * all_tokens * width * 64

    x, unit_one, q_self, k_self, v_self, att_own, att_mate, self_low, queries, rstd_one = run(
        partial(self_kernel, steps, step_rows, local, length),
        steps,
        [lens, where],
        [
            whole(x_in),
            (attention_in, ANY),
            (ain_mate, ANY),
            (attention_out, ANY),
            (aout_mate, ANY),
            whole(attention_bias),
            whole(bias_mate),
            whole(output_bias),
            whole(norm_gain),
            whole(norm_bias),
        ],
        [token_out(width, BF16), token_out(width, F32)]
        + [token_out(width, BF16)] * 3
        + [token_out(local, BF16)] * 2
        + [token_out(width, BF16)] * 2
        + [token_out(1, F32)],
        [weight_scratch] * 5
        + [f32_tokens(width)] * 4
        + [low_tokens(width), pltpu.SemaphoreType.DMA((10,))],
        2 * all_tokens * width * width * 5 + attention_flops,
    )

    (attended,) = run(
        partial(cross_kernel, step_rows, length),
        steps,
        [image, corners],
        [token_in(queries), whole(keys), whole(values)],
        [token_out(width, BF16)],
        [f32_tokens(width)] * 2,
        attention_flops * 4,
    )

    result = run(
        partial(feed_kernel, steps, step_rows, local, hidden, length),
        steps,
        [where],
        [
            whole(upstream_in),
            token_in(attended),
            token_in(unit_one),
            (attention_out, ANY),
            (aout_mate, ANY),
            (up_weight, ANY),
            (up_mate, ANY),
            (down_weight, ANY),
            (down_mate, ANY),
            whole(output_bias),
            whole(norm_gain),
            whole(norm_bias),
            whole(up_bias_own),
            whole(up_bias_mate),
        ],
        [block_out]
        + [token_out(width, BF16)] * 3
        + [token_out(width, F32)]
        + [token_out(local, BF16)] * 2
        + [token_out(hidden, BF16)] * 4
        + [
            token_out(width, BF16),
            ((steps, 8, width), F32, rows_spec((1, 8, width), 0)),
            ((steps, 2, hidden), F32, rows_spec((1, 2, hidden), 0)),
        ],
        [weight_scratch]
        + [
            pltpu.VMEM((hidden // TILE, width, 2 * TILE), BF16),
            pltpu.VMEM((hidden // TILE, 2 * TILE, width), BF16),
        ]
        + [f32_tokens(width)] * 3
        + [f32_tokens(1), low_tokens(width), low_tokens(width)]
        + [f32_tokens(2 * TILE)] * 2
        + [pltpu.VMEM((hidden // TILE, tokens, 2 * TILE), F32)]
        + [pltpu.VMEM((8, 8, width), F32), pltpu.VMEM((2, 8, hidden), F32)]
        + [pltpu.SemaphoreType.DMA((2 + 4 * hidden // TILE,))],
        2 * all_tokens * width * (2 * width + 8 * hidden),
    )
    merged_out, cross_low, grad_ffn, grad_cross, dz_two, a_own, a_mate = result[:7]
    g_own, g_mate, du_own, du_mate, grad_att, feed_sums, up_sums = result[7:]

    bits = devices.bit_length() - 1

    def partner_bits(value, mask):
        return lax.ppermute(value, "dp", [(d, d ^ mask) for d in range(devices)])

    def opened(value):
        return value.reshape((2,) * bits + (value.shape[0] // devices, value.shape[1]))

    def swap(value, axis, bit):
        mine = (me >> bit) & 1
        away = lax.dynamic_index_in_dim(value, 1 - mine, axis, keepdims=False)
        stay = lax.dynamic_index_in_dim(value, mine, axis, keepdims=False)
        return stay, partner_bits(away, 1 << bit)

    def first_swaps(by_x, by_y):
        return swap(opened(by_x), bits - 1, 0) + swap(opened(by_y), bits - 2, 1)

    def second_swaps(stay_x, got_x, stay_y, got_y):
        return swap(add(stay_x, got_x), bits - 2, 1) + swap(add(stay_y, got_y), bits - 2, 0)

    def add(stay, got):
        return (stay.astype(F32) + got.astype(F32)).astype(BF16)

    def last_parts(stay_x, got_x, stay_y, got_y):
        parts = [add(stay_x, got_x), add(stay_y, got_y)]
        return jnp.concatenate(
            [part.reshape((devices // 4,) + part.shape[-2:]) for part in parts], axis=2
        )

    def last_sum(both, first_width):
        groups = [[low + 4 * n for n in range(devices // 4)] for low in range(4)]
        both = lax.all_to_all(
            both, "dp", split_axis=0, concat_axis=0, axis_index_groups=groups, tiled=True
        )
        total = jnp.sum(both.astype(F32), axis=0)
        return total[:, :first_width], total[:, first_width:]

    def low_tn(left, right):
        return dot_tn(left, right).astype(BF16)

    merged_in = exchange(merged_out)
    up_away, down_away = low_tn(cross_low, du_mate), low_tn(grad_ffn, g_mate)
    grad_att, queries, up_away, down_away = tie(grad_att, queries, up_away, down_away)
    up_got, down_got = mate(up_away), mate(down_away)

    half_shape = (2, own_images, patch_pad, width)
    image_acc = pltpu.VMEM(image_shape, F32)
    piece, piece_out, grad_queries = run(
        partial(cross_grad_kernel, steps, step_rows, length),
        steps,
        [image, corners],
        [token_in(queries), token_in(grad_att), whole(keys), whole(values)],
        [(half_shape, BF16, whole_spec(half_shape))] * 2 + [token_out(width, BF16)],
        [f32_tokens(width)] * 3 + [image_acc] * 2,
        attention_flops * 12,
    )
    piece_mate = mate(piece_out)

    up_part = (dot_tn(cross_low, du_own) + up_got.astype(F32)).astype(BF16)
    down_part = (dot_tn(grad_ffn, g_own) + down_got.astype(F32)).astype(BF16)
    grad_queries, up_part, down_part = tie(grad_queries, up_part, down_part)
    feed_stage = first_swaps(up_part, down_part)

    token_shape = (length // 2, slots, width)
    final_shape = (length // 2, rows, width)

    def halves(value, after):
        own, away = run(
            partial(halve_kernel, slots, length),
            1,
            [core_scalar, where],
            [whole(value)],
            [(token_shape, BF16, whole_spec(token_shape))] * 2,
            [slabs(all_tokens)],
            0,
            after,
        )
        return own, mate(away)

    def placed(own, got, after):
        (out,) = run(
            place_kernel,
            1,
            [],
            [whole(own), whole(got), whole(place)],
            [(final_shape, BF16, whole_spec(final_shape))],
            [],
            0,
            after,
        )
        return jnp.transpose(out, (1, 0, 2))

    merged_own, merged_got = halves(merged_in, [])

    result = run(
        partial(self_grad_kernel, steps, step_rows, local, length),
        steps,
        [lens, where],
        [
            token_in(grad_queries),
            token_in(unit_one),
            token_in(rstd_one),
            token_in(dz_two),
            token_in(q_self),
            token_in(k_self),
            token_in(v_self),
            (attention_in, ANY),
            (ain_mate, ANY),
            (attention_out, ANY),
            (aout_mate, ANY),
            whole(norm_gain),
        ],
        [block_out]
        + [token_out(width, BF16)]
        + [token_out(local, BF16)] * 2
        + [token_out(3 * local, BF16)] * 2
        + [((steps, 8, width), F32, rows_spec((1, 8, width), 0))],
        [weight_scratch] * 5
        + [f32_tokens(width)] * 2
        + [low_tokens(width)] * 3
        + [f32_tokens(width)] * 3
        + [pltpu.VMEM((8, 8, width), F32), pltpu.SemaphoreType.DMA((10,))],
        2 * all_tokens * width * width * 5 + attention_flops * 2,
        [merged_own],
    )
    text_out, grad_self, dq_own, dq_mate, qkv_own, qkv_mate, self_sums = result
    text_in = exchange(text_out)

    flat_images = own_images * patch_pad
    patch_grad_shape = (patch_count, own_images, vision)
    result = run(
        partial(image_kernel, images, patch_count, local),
        1,
        [core_scalar],
        [
            whole(piece),
            whole(piece_mate),
            (by_patch, ANY),
            whole(proj_weight),
            (attention_in, ANY),
            (ain_mate, ANY),
        ],
        [
            ((flat_images, width), BF16, whole_spec((flat_images, width))),
            ((flat_images, width), BF16, whole_spec((flat_images, width))),
            (patch_grad_shape, BF16, whole_spec(patch_grad_shape)),
            ((vision, width), F32, whole_spec((vision, width))),
            ((8, width), F32, whole_spec((8, width))),
        ],
        [
            slabs(patch_count * own_images),
            slabs(patch_count * images),
            patch_scratch,
            weight_scratch,
            weight_scratch,
            pltpu.VMEM((2, 8, width), F32),
            pltpu.SemaphoreType.DMA((parts,)),
            pltpu.SemaphoreType.DMA((4,)),
        ],
        2 * flat_images * width * (2 * width + 2 * vision),
        (),
        [qkv_mate, qkv_own, grad_self, dq_mate, dq_own],
    )
    kv_own, kv_mate, patch_grad, proj_weight_sum, image_sums = result[:5]
    qkv_mate, qkv_own, grad_self, dq_mate, dq_own = result[5:]

    self_away = jnp.concatenate(
        [
            low_tn(x, qkv_mate),
            low_tn(grad_self, att_mate),
            low_tn(grad_cross, a_mate),
            low_tn(self_low, dq_mate),
        ],
        axis=1,
    )
    self_got = mate(self_away)
    feed_stage = tie(self_away, *feed_stage)[1:]
    feed_stage = second_swaps(*feed_stage)
    self_own = jnp.concatenate(
        [
            dot_tn(x, qkv_own),
            dot_tn(grad_self, att_own),
            dot_tn(grad_cross, a_own),
            dot_tn(self_low, dq_own),
        ],
        axis=1,
    )
    self_part = (self_own + self_got.astype(F32)).astype(BF16)
    half_width = self_part.shape[1] // 2
    self_stage = first_swaps(self_part[:, :half_width], self_part[:, half_width:])
    feed_parts = last_parts(*feed_stage)

    up_grad, down_grad = last_sum(feed_parts, hidden)
    self_got_x, self_got_y = self_stage[1], self_stage[3]
    self_stage = second_swaps(*self_stage)
    kv_low = proj.reshape(flat_images, width)
    kv_away = low_tn(kv_low, kv_mate)
    kv_got = mate(kv_away)
    proj_away = lax.dynamic_slice_in_dim(proj_weight_sum, (1 - core) * local, local, 1)
    proj_got = mate(proj_away.astype(BF16))
    kv_part = (dot_tn(kv_low, kv_own) + kv_got.astype(F32)).astype(BF16)
    proj_own = lax.dynamic_slice_in_dim(proj_weight_sum, core * local, local, 1)
    proj_part = (proj_own + proj_got.astype(F32)).astype(BF16)
    proj_part = proj_part.reshape(width, vision * local // width)
    image_stage = first_swaps(kv_part, proj_part)
    self_one, self_two = last_sum(last_parts(*self_stage), half_width)
    image_stage = second_swaps(*image_stage)
    kv_grad, proj_grad = last_sum(last_parts(*image_stage), width)
    proj_grad = proj_grad.reshape(vision // devices, local)

    lines = 23 + hidden // local
    packed_shape = (-(-lines // 8) * 8, local)
    small, small_out = run(
        partial(pack_kernel, local, hidden),
        1,
        [core_scalar],
        [whole(feed_sums), whole(up_sums), whole(self_sums), whole(image_sums)],
        [(packed_shape, F32, whole_spec(packed_shape))] * 2,
        [],
        0,
        [kv_part, proj_part, self_got_x, self_got_y],
    )
    small = small + mate(small_out)
    for bit in range(bits):
        small = small + partner_bits(small, 1 << bit)
    common = small[:18].reshape(3, 3, width)
    bias_grad = small[18:22].reshape(2, 2, local)
    up_bias_grad = small[22 : 22 + hidden // local].reshape(hidden)
    proj_bias_grad = small[22 + hidden // local]

    ready = [self_one[:, at * local : (at + 1) * local] for at in range(3)]
    out_self, out_cross, query_cross = [
        self_two[:, at * local : (at + 1) * local] for at in range(3)
    ]
    in_grad = jnp.stack(
        ready + [query_cross, kv_grad[:, :local], kv_grad[:, local:]]
    ).reshape(2, 3, width // devices, local)
    out_grad = jnp.stack([out_self.T, out_cross.T])

    return (
        placed(merged_own, merged_got, [kv_part]),
        placed(*halves(text_in, [kv_away, self_part]), [kv_part, proj_part]),
        jnp.transpose(patch_grad, (1, 0, 2)),
        proj_grad,
        proj_bias_grad,
        in_grad,
        bias_grad,
        out_grad,
        common[0],
        common[1],
        common[2],
        up_grad,
        up_bias_grad,
        down_grad.T,
    )


def solution(mesh):
    placed = (
        P("dp", None, None),
        P("dp", None, None),
        P("dp"),
        P("dp", None),
        P("dp", None),
        P("dp"),
        P("dp", None, None),
        P(),
        P(),
        P(None, None, None, "mp"),
        P(None, None, "mp"),
        P(None, "mp", None),
        P(),
        P(),
        P(),
        P(None, "mp"),
        P("mp"),
        P("mp", None),
    )
    return jax.shard_map(
        body,
        mesh=mesh,
        in_specs=placed,
        out_specs=(
            P("dp", "mp", None),
            P("dp", "mp", None),
            P(("dp", "mp"), None, None),
            P("dp", "mp"),
            P("mp"),
            P(None, None, "dp", "mp"),
            P(None, None, "mp"),
            P(None, "mp", "dp"),
            P(),
            P(),
            P(),
            P("dp", "mp"),
            P("mp"),
            P("mp", "dp"),
        ),
        check_vma=False,
    )
```
